32 devices in a mesh: row: 8 (over y, x, core), col: 4 (over z).
Axes of the slice: x: 2, y: 2, z: 4, core: 2. Of those that a mesh axis runs over, the one named last changes fastest.
Arguments:
- a_vals: bfloat16 [8, 4, 2, 6, 5, 128, 128], P('row', 'col'), may hold values from -6 to 6
- a_cols: int32 [8, 4, 2, 6, 5], P('row', 'col'), may hold values from 0 to 5, as said below
- b_vals: bfloat16 [8, 4, 6, 8, 128, 128], P('row', 'col'), may hold values from -0.15625 to 0.15625
- b_cols: int32 [8, 4, 6, 8], P('row', 'col'), may hold values from 0 to 11, as said below
- c_cols: int32 [8, 4, 6, 6], P('row', 'col'), may hold values from 0 to 11, as said below
- panel_owner: int32 [8, 8], replicated, may hold values from 0 to 7, as said below
- atom_size: int32 [48], replicated, may hold values from 64 to 128
Outputs:
- product_blocks: bfloat16 [8, 4, 6, 6, 128, 128], P('row', 'col')
The draws below stay inside these ranges and needn't reach their ends.
Inputs may be any that keep to these rules, and one draw needn't show every extreme that they name: `a_cols`: the 5 indices of one block row are distinct. `b_cols`: the 8 indices of one block row are distinct. `c_cols`: the 6 indices of one block row are distinct. `panel_owner`: each row is a permutation.
All inputs are finite; a program needn't handle non-finite values.
Results may differ from the reference program's by a relative error of at most 0.001.
Values may be sent and summed in bfloat16 or wider, within the bound.
No kernel may reach another device: no remote copies, remote signals or barrier semaphores. Data moves between devices by JAX's collectives and lax.ppermute only.
A program may use at most 128 MiB of HBM per device.

```python
import jax
import jax.numpy as jnp
from jax import lax

BLK = 128
KB = 6
NZA = 5
NZB = 8
NCS = 6
STEPS = 2
CB = 12
NBLK = 48
N_ROW = 8
N_COL = 4


def distinct_picks(key, lead_shape, pool, count):
    raw = jax.random.randint(key, tuple(lead_shape) + (pool,), 0, 1 << 20)
    scores = raw * pool + jnp.arange(pool, dtype=jnp.int32)
    order = jnp.argsort(scores, axis=-1)
    return order[..., :count].astype(jnp.int32)


def draw_a_cols(key, part):
    return distinct_picks(jax.random.fold_in(key, 11), (N_ROW, N_COL, 2, KB), KB, NZA)


def draw_b_cols(key, part):
    return distinct_picks(jax.random.fold_in(key, 23), (N_ROW, N_COL, KB), 2 * KB, NZB)


def draw_c_cols(key, part):
    return distinct_picks(jax.random.fold_in(key, 37), (N_ROW, N_COL, KB), 2 * KB, NCS)


def draw_panel_owner(key, part):
    return distinct_picks(jax.random.fold_in(key, 41), (N_ROW,), N_ROW, N_ROW)


def set_ends(drawn, stream_key, least, largest):
    extent = drawn.shape
    place = [jax.random.randint(jax.random.fold_in(stream_key, axis), (), 0, extent[axis]) for axis in range(len(extent))]
    drawn = drawn.at[tuple(place)].set(least)
    longest = extent.index(max(extent))
    place[longest] = (place[longest] + 1) % extent[longest]
    return drawn.at[tuple(place)].set(largest)


def level_of(stream_key, dims, split, least, largest):
    def one(dim, blocks):
        draws = jax.random.uniform(jax.random.fold_in(jax.random.fold_in(stream_key, 6), dim), (blocks,), jnp.float32, least / len(split), largest / len(split))
        return jnp.repeat(jnp.exp(draws), dims[dim] // blocks).reshape((-1,) + (1,) * (len(dims) - dim - 1))

    gain = one(*split[0])
    for cut in split[1:]:
        gain = gain * one(*cut)
    return gain


def noise(rng, shape, width, bound, shards=(), kind=jnp.bfloat16):
    loudness = level_of(rng, shape, shards, -0.22, 0.18) if shards else 1.0
    values = jax.random.normal(rng, shape, jnp.float32) * width * loudness
    return jnp.minimum(jnp.maximum(values, -bound), bound).astype(kind)


def setup_inputs(seed: int = 0) -> dict:
    arg_keys = jax.random.split(jax.random.key(seed), 8)
    return {
        "a_vals": noise(arg_keys[0], (N_ROW, N_COL, 2, KB, NZA, BLK, BLK), 1.0, 6.0, ((0, 8), (1, 4))),
        "a_cols": draw_a_cols(jax.random.fold_in(arg_keys[7], 71), 0),
        "b_vals": noise(arg_keys[2], (N_ROW, N_COL, KB, NZB, BLK, BLK), (STEPS * NZA * BLK) ** -0.5, 0.15625, ((0, 8), (1, 4))),
        "b_cols": draw_b_cols(jax.random.fold_in(arg_keys[7], 71), 0),
        "c_cols": draw_c_cols(jax.random.fold_in(arg_keys[7], 71), 0),
        "panel_owner": draw_panel_owner(jax.random.fold_in(arg_keys[7], 71), 0),
        "atom_size": set_ends(jax.random.randint(arg_keys[6], (NBLK,), BLK // 2, BLK + 1), jax.random.fold_in(arg_keys[6], 1), BLK // 2, BLK).astype(jnp.int32),
    }


def sizes_at(atom_size, start, count):
    return lax.dynamic_slice_in_dim(atom_size, start, count)


def pick_sizes(indices, table):
    lane_ids = jnp.arange(table.shape[0], dtype=jnp.int32)
    return jnp.sum(jnp.where(indices[..., None] == lane_ids, table, 0), axis=-1)


def panel_term(avals, acols, bvals, bcols, ccols, k_sizes):
    block_size = avals.shape[-1]
    inner_sizes = pick_sizes(acols, k_sizes)
    inside = jnp.arange(block_size, dtype=jnp.int32) < inner_sizes[..., None]
    masked = jnp.where(inside[..., None, :], avals, jnp.zeros((), avals.dtype))
    picked_v = bvals[acols]
    picked_c = bcols[acols]
    products = jnp.einsum('imab,imnbc->imnac', masked.astype(jnp.float32), picked_v.astype(jnp.float32), precision=lax.Precision.HIGHEST)
    select = (picked_c[..., None] == ccols[:, None, None, :]).astype(jnp.float32)
    return jnp.einsum('imns,imnac->isac', select, products, precision=lax.Precision.HIGHEST)


def finish(summed, ccols, row_sizes, col_table):
    block_size = summed.shape[-1]
    col_sizes = pick_sizes(ccols, col_table)
    lane_ids = jnp.arange(block_size, dtype=jnp.int32)
    inside = (lane_ids[:, None] < row_sizes[:, None, None, None]) & (lane_ids[None, :] < col_sizes[:, :, None, None])
    return jnp.where(inside, summed, jnp.zeros((), summed.dtype)).astype(jnp.bfloat16)


def reference(a_vals, a_cols, b_vals, b_cols, c_cols, panel_owner, atom_size):
    def one_panel(flat_index):
        row_id = flat_index // N_COL
        col_id = flat_index % N_COL
        summed = jnp.zeros((KB, NCS, BLK, BLK), jnp.float32)
        for fox_step in range(STEPS):
            k_panel = (row_id + fox_step) % N_ROW
            position = panel_owner[row_id, k_panel]
            holder = position // 2
            slot_index = position % 2
            summed = summed + panel_term(a_vals[row_id, holder, slot_index], a_cols[row_id, holder, slot_index], b_vals[k_panel, col_id], b_cols[k_panel, col_id], c_cols[row_id, col_id], sizes_at(atom_size, k_panel * KB, KB))
        return finish(summed, c_cols[row_id, col_id], sizes_at(atom_size, row_id * KB, KB), sizes_at(atom_size, col_id * CB, CB))

    result = lax.map(one_panel, jnp.arange(N_ROW * N_COL, dtype=jnp.int32))
    return result.reshape(N_ROW, N_COL, KB, NCS, BLK, BLK)
```

```python
import functools

import jax
import jax.numpy as jnp
from jax import lax
from jax.experimental import pallas as pl
from jax.experimental.pallas import tpu as pltpu
from jax.sharding import PartitionSpec as P

STEPS = 2
GROUPS = ((0, 1, 2), (3, 4), (5,))


def row_groups(rows):
    if rows == sum(len(g) for g in GROUPS):
        return GROUPS
    return (tuple(range(rows)),)


def pick(indices, table):
    ids = jnp.arange(table.shape[0], dtype=jnp.int32)
    return jnp.sum(jnp.where(indices[..., None] == ids, table, 0), axis=-1)


def rows_kernel(rows, hops, nz, nzb, kept, scal, *refs):
    refs = list(refs)
    arrived = {}
    for t in range(STEPS):
        for i in rows:
            for way in range(2):
                for k in range(hops):
                    arrived[t, i, way, k] = refs.pop(0)
    own, b_first, b_second = refs.pop(0), refs.pop(0), refs.pop(0)
    out, a_vm, b_vm, o_vm, a_sem, b_sem, o_sem = refs[-7:]
    stored = b_first.shape[0]
    blk = a_vm.shape[-1]
    width = STEPS * nz

    b_copies = [
        pltpu.make_async_copy(ref, b_vm.at[pl.ds(t * stored, stored)], b_sem.at[t])
        for t, ref in enumerate((b_first, b_second))
    ]
    for place, i in enumerate(rows):
        for t in range(STEPS):
            dst = a_vm.at[place, pl.ds(t * nz, nz)]
            source, slot = scal[0, t], scal[0, STEPS + t]

            @pl.when(source == 0)
            def _():
                pltpu.make_async_copy(own.at[slot, i], dst, a_sem.at[place, t]).start()

            for way in range(2):
                for k in range(hops):

                    @pl.when(source == 1 + way * hops + k)
                    def _():
                        pltpu.make_async_copy(arrived[t, i, way, k], dst, a_sem.at[place, t]).start()

    for copy in b_copies:
        copy.start()
    b_vm[STEPS * stored] = jnp.zeros((blk, blk), b_vm.dtype)
    for copy in b_copies:
        copy.wait()

    lane = lax.broadcasted_iota(jnp.int32, (blk, blk), 1)
    sub = lax.broadcasted_iota(jnp.int32, (blk, blk), 0)
    out_copies = []
    for place, i in enumerate(rows):
        line = 1 + i
        for t in range(STEPS):
            pltpu.make_async_copy(own.at[0, i], a_vm.at[place, pl.ds(t * nz, nz)], a_sem.at[place, t]).wait()
        left = jnp.concatenate(
            [
                jnp.where(lane < scal[line, kept * width + q], a_vm[place, q], jnp.zeros((), a_vm.dtype))
                for q in range(width)
            ],
            axis=1,
        )
        row_size = scal[line, kept * width + width]
        for s in range(0, kept, 2):
            pair = [s, s + 1] if s + 1 < kept else [s]
            right = jnp.concatenate(
                [
                    jnp.concatenate([b_vm[scal[line, e * width + q]] for q in range(width)], axis=0)
                    for e in pair
                ],
                axis=1,
            )
            total = jnp.dot(left, right, preferred_element_type=jnp.float32)
            for at, e in enumerate(pair):
                col_size = scal[line, kept * width + width + 1 + e]
                inside = (sub < row_size) & (lane < col_size)
                part = total[:, at * blk : (at + 1) * blk]
                o_vm[place, e] = jnp.where(inside, part, 0.0).astype(o_vm.dtype)
        copy = pltpu.make_async_copy(o_vm.at[place], out.at[i], o_sem.at[place])
        copy.start()
        out_copies.append(copy)
    for copy in out_copies:
        copy.wait()


def multiply_rows(rows, hops, scal, arrived, own, b_first, b_second, so_far, kept):
    nz, blk = own.shape[2], own.shape[-1]
    total_rows = own.shape[1]
    stored = b_first.shape[0]
    operands = [scal]
    for t in range(STEPS):
        for i in rows:
            for way in range(2):
                for k in range(hops):
                    operands.append(arrived[t][way][i + k])
    operands += [own, b_first, b_second]
    aliases = {}
    if so_far is not None:
        aliases = {len(operands): 0}
        operands.append(so_far)
    count = len(rows)
    flops = 2 * count * blk * blk * blk * STEPS * nz * kept
    return pl.pallas_call(
        functools.partial(rows_kernel, rows, hops, nz, stored, kept),
        out_shape=jax.ShapeDtypeStruct((total_rows, kept, blk, blk), jnp.bfloat16),
        in_specs=[pl.BlockSpec(memory_space=pltpu.SMEM)]
        + [pl.BlockSpec(memory_space=pl.ANY)] * (len(operands) - 1),
        out_specs=pl.BlockSpec(memory_space=pl.ANY),
        scratch_shapes=[
            pltpu.VMEM((count, STEPS * nz, blk, blk), jnp.bfloat16),
            pltpu.VMEM((STEPS * stored + 1, blk, blk), jnp.bfloat16),
            pltpu.VMEM((count, kept, blk, blk), jnp.bfloat16),
            pltpu.SemaphoreType.DMA((count, STEPS)),
            pltpu.SemaphoreType.DMA((STEPS,)),
            pltpu.SemaphoreType.DMA((count,)),
        ],
        input_output_aliases=aliases,
        compiler_params=pltpu.CompilerParams(vmem_limit_bytes=16 * 1024 * 1024),
        cost_estimate=pl.CostEstimate(flops=flops, bytes_accessed=4 * 1024 * 1024, transcendentals=0),
    )(*operands)


def local(a_vals, a_cols, b_vals, b_cols, c_cols, panel_owner, atom_size):
    row_id = lax.axis_index("row")
    col_id = lax.axis_index("col")
    row_count = lax.axis_size("row")
    col_count = lax.axis_size("col")
    own_a, own_ac = a_vals[0, 0], a_cols[0, 0]
    stored_b, stored_bc = b_vals[0, 0], b_cols[0, 0]
    targets = c_cols[0, 0]
    rows, nz, blk = own_a.shape[1], own_a.shape[2], own_a.shape[-1]
    nzb = stored_b.shape[1]
    kept = targets.shape[1]
    hops = col_count - 1

    panels = [(row_id + t) % row_count for t in range(STEPS)]
    owners = lax.dynamic_index_in_dim(panel_owner, row_id, 0, keepdims=False)
    places = [lax.dynamic_index_in_dim(owners, k, 0, keepdims=False) for k in panels]
    holders = [p // 2 for p in places]
    slots = [p % 2 for p in places]

    from_next = [((i + 1) % row_count, i) for i in range(row_count)]
    moved_b = lax.ppermute(stored_b, "row", from_next)
    moved_bc = lax.ppermute(stored_bc, "row", from_next)

    up = [(i, i + 1) for i in range(hops)]
    down = [(i + 1, i) for i in range(hops)]
    rounds = rows + hops - 1
    arrived = [[[], []] for _ in range(STEPS)]
    for step in range(rounds):
        for t in range(STEPS):
            for way, (route, lag) in enumerate(((up, col_id), (down, hops - col_id))):
                chunk = jnp.clip(step - lag, 0, rows - 1)
                block = lax.dynamic_slice(
                    own_a, (slots[t], chunk, 0, 0, 0), (1, 1) + own_a.shape[2:]
                )[0, 0]
                if step:
                    block = jnp.where(holders[t] == col_id, block, arrived[t][way][-1])
                arrived[t][way].append(lax.ppermute(block, "col", route))

    turned = [own_ac] + [
        lax.ppermute(own_ac, "col", [(i, (i + d) % col_count) for i in range(col_count)])
        for d in range(1, col_count)
    ]
    turned = jnp.stack(turned)

    tables, sizes = [], []
    for t, bc in enumerate((stored_bc, moved_bc)):
        distance = (col_id - holders[t]) % col_count
        ac = lax.dynamic_slice(turned, (distance, slots[t], 0, 0), (1, 1, rows, nz))[0, 0]
        ids = jnp.arange(rows, dtype=jnp.int32)
        picked = jnp.sum(jnp.where(ac[:, :, None, None] == ids[:, None], bc, 0), axis=2)
        match = picked[:, None, :, :] == targets[:, :, None, None]
        nth = jnp.sum(jnp.where(match, jnp.arange(1, nzb + 1, dtype=jnp.int32), 0), axis=-1)
        base = t * rows * nzb + ac * nzb - 1
        tables.append(jnp.where(nth > 0, base[:, None, :] + nth, STEPS * rows * nzb))
        sizes.append(pick(ac, lax.dynamic_slice_in_dim(atom_size, panels[t] * rows, rows)))
    table = jnp.concatenate(tables, axis=2).reshape(rows, kept * STEPS * nz)
    row_sizes = lax.dynamic_slice_in_dim(atom_size, row_id * rows, rows)
    col_table = lax.dynamic_slice_in_dim(atom_size, col_id * 2 * rows, 2 * rows)
    col_sizes = pick(targets, col_table)
    lines = jnp.concatenate([table] + sizes + [row_sizes[:, None], col_sizes], axis=1)
    source = [
        jnp.where(
            h == col_id, 0, jnp.where(h < col_id, col_id, 1 + hops + (hops - 1 - col_id))
        )
        for h in holders
    ]
    head = jnp.stack(source + slots)
    head = jnp.pad(head, (0, lines.shape[1] - head.shape[0]))[None]
    scal = jnp.concatenate([head, lines], axis=0).astype(jnp.int32)

    flat_b = stored_b.reshape(rows * nzb, blk, blk)
    flat_moved = moved_b.reshape(rows * nzb, blk, blk)
    result = None
    for group in row_groups(rows):
        result = multiply_rows(group, hops, scal, arrived, own_a, flat_b, flat_moved, result, kept)
    return result[None, None]


def solution(mesh):
    placed = (
        P("row", "col", None, None, None, None, None),
        P("row", "col", None, None, None),
        P("row", "col", None, None, None, None),
        P("row", "col", None, None),
        P("row", "col", None, None),
        P(),
        P(),
    )
    return jax.shard_map(
        local,
        mesh=mesh,
        in_specs=placed,
        out_specs=P("row", "col", None, None, None, None),
        check_vma=False,
    )
```

```python
import functools

import jax
import jax.numpy as jnp
from jax import lax
from jax.experimental import pallas as pl
from jax.experimental.pallas import tpu as pltpu
from jax.sharding import PartitionSpec as P

STEPS = 2
AHEAD = 2


def places_of(owner_ref):
    row_id, row_count = lax.axis_index("row"), lax.axis_size("row")
    panels = [lax.rem(row_id + t, row_count) for t in range(STEPS)]
    places = [owner_ref[row_id, k] for k in panels]
    return panels, [lax.div(p, 2) for p in places], [lax.rem(p, 2) for p in places]


def relay_kernel(row, following, hop, arrives, waits, owner, own, *refs):
    refs = list(refs)
    arrived = refs.pop(0) if arrives else None
    del refs[:waits]
    sem = refs.pop()
    _, holders, slots = places_of(owner)
    col_id, last = lax.axis_index("col"), lax.axis_size("col") - 1

    if row is not None:
        onward = refs.pop(0)

        @pl.when((col_id == hop) | (col_id == last - hop))
        def _():
            for t in range(STEPS):
                if arrived is None:
                    pltpu.make_async_copy(own.at[slots[t], row], onward.at[t], sem.at[0, t]).start()
                else:

                    @pl.when(holders[t] == col_id)
                    def _():
                        pltpu.make_async_copy(own.at[slots[t], row], onward.at[t], sem.at[0, t]).start()

                    @pl.when(holders[t] != col_id)
                    def _():
                        pltpu.make_async_copy(arrived.at[t], onward.at[t], sem.at[0, t]).start()

            for t in range(STEPS):
                pltpu.make_async_copy(own.at[0, row], onward.at[t], sem.at[0, t]).wait()

    if following is not None:
        fresh = refs.pop(0)

        @pl.when((col_id == 0) | (col_id == last))
        def _():
            copies = [
                pltpu.make_async_copy(own.at[slots[t], following], fresh.at[t], sem.at[1, t])
                for t in range(STEPS)
            ]
            for copy in copies:
                copy.start()
            for copy in copies:
                copy.wait()


def relay(owner, own, row, following, hop, arrived, after):
    operands = [owner, own]
    if arrived is not None:
        operands.append(arrived)
    operands += after
    piece = jax.ShapeDtypeStruct((STEPS,) + own.shape[2:], own.dtype)
    count = 1 + (following is not None)
    anywhere = pl.BlockSpec(memory_space=pl.ANY)
    return pl.pallas_call(
        functools.partial(relay_kernel, row, following, hop, arrived is not None, len(after)),
        out_shape=[piece] * count,
        in_specs=[pl.BlockSpec(memory_space=pltpu.SMEM)] + [anywhere] * (len(operands) - 1),
        out_specs=[anywhere] * count,
        scratch_shapes=[pltpu.SemaphoreType.DMA((2, STEPS))],
        cost_estimate=pl.CostEstimate(flops=0, bytes_accessed=1024 * 1024, transcendentals=0),
        name="relay",
    )(*operands)


def rows_kernel(first, count, hops, chained, owner, atoms, acols, bcols0, bcols1, ccols, *refs):
    refs = list(refs)
    b_refs = [refs.pop(0), refs.pop(0)]
    own = refs.pop(0)
    pieces = []
    for _ in range(count):
        pieces.append([refs.pop(0) for _ in range(hops)])
    if chained:
        refs.pop(0)
    out, a_vm, left_vm, o_vm, found, a_sem, o_sem = refs
    blk = a_vm.shape[-1]
    nz = acols.shape[-1]
    panel_rows, nzb = bcols0.shape
    kept = ccols.shape[1]
    columns = found.shape[1]
    row_id, col_id = lax.axis_index("row"), lax.axis_index("col")
    col_count = hops + 1
    panels, holders, slots = places_of(owner)
    turn = [lax.rem(col_id - h + col_count, col_count) for h in holders]

    for t in range(STEPS):
        h = holders[t]
        hop = jnp.where(h == col_id, 0, jnp.where(h < col_id, col_id, col_count - 1 - col_id))
        for at in range(count):

            @pl.when(hop == 0)
            def _():
                pltpu.make_async_copy(own.at[slots[t], first + at], a_vm.at[at, t], a_sem.at[at, t]).start()

            for k in range(hops):

                @pl.when(hop == 1 + k)
                def _():
                    pltpu.make_async_copy(pieces[at][k].at[t], a_vm.at[at, t], a_sem.at[at, t]).start()

    def clear(j, carry):
        for c in range(columns):
            found[j, c] = -1
        return carry

    lax.fori_loop(0, STEPS * panel_rows, clear, 0)

    def fill(j, carry):
        for t, bcols in enumerate((bcols0, bcols1)):
            for n in range(nzb):
                found[t * panel_rows + j, bcols[j, n]] = n
        return carry

    lax.fori_loop(0, panel_rows, fill, 0)

    lane = lax.broadcasted_iota(jnp.int32, (blk, blk), 1)
    sub = lax.broadcasted_iota(jnp.int32, (blk, blk), 0)

    def one_row(at, carry):
        i = first + at
        inner = []
        for t in range(STEPS):
            pltpu.make_async_copy(a_vm.at[at, t], a_vm.at[at, t], a_sem.at[at, t]).wait()
            for m in range(nz):
                j = acols[turn[t], slots[t], i, m]
                inner.append(j)
                size = atoms[panels[t] * panel_rows + j]
                q = t * nz + m
                left_vm[:, q * blk : (q + 1) * blk] = jnp.where(
                    lane < size, a_vm[at, t, m], jnp.zeros((), a_vm.dtype)
                )
        row_size = atoms[row_id * panel_rows + i]

        def one_pair(p, carry):
            cols = [ccols[i, 2 * p + e] for e in range(2)]
            sides = []
            for c in cols:
                parts = []
                for q, j in enumerate(inner):
                    t = q // nz
                    n = found[t * panel_rows + j, c]
                    block = b_refs[t][j, jnp.maximum(n, 0)]
                    parts.append(jnp.where(n >= 0, block, jnp.zeros((), block.dtype)))
                sides.append(jnp.concatenate(parts, axis=0))
            total = jnp.dot(
                left_vm[...], jnp.concatenate(sides, axis=1), preferred_element_type=jnp.float32
            )
            for e, c in enumerate(cols):
                col_size = atoms[col_id * columns + c]
                inside = (sub < row_size) & (lane < col_size)
                part = total[:, e * blk : (e + 1) * blk]
                o_vm[at, 2 * p + e] = jnp.where(inside, part, 0.0).astype(o_vm.dtype)
            return carry

        lax.fori_loop(0, kept // 2, one_pair, 0)
        pltpu.make_async_copy(o_vm.at[at], out.at[i], o_sem.at[at]).start()
        return carry

    lax.fori_loop(0, count, one_row, 0)
    for at in range(count):
        pltpu.make_async_copy(o_vm.at[at], out.at[first + at], o_sem.at[at]).wait()


def multiply_rows(first, count, tables, b_panels, own, pieces, so_far):
    owner, atoms, acols, bcols0, bcols1, ccols = tables
    hops = acols.shape[0] - 1
    rows, kept = ccols.shape
    nz, blk = acols.shape[-1], b_panels[0].shape[-1]
    operands = list(tables) + list(b_panels) + [own]
    for at in range(count):
        operands += pieces[first + at]
    aliases = {}
    if so_far is not None:
        aliases = {len(operands): 0}
        operands.append(so_far)
    smem, vmem = pl.BlockSpec(memory_space=pltpu.SMEM), pl.BlockSpec(memory_space=pltpu.VMEM)
    flops = 2 * count * blk * blk * blk * STEPS * nz * kept
    return pl.pallas_call(
        functools.partial(rows_kernel, first, count, hops, so_far is not None),
        out_shape=jax.ShapeDtypeStruct((rows, kept, blk, blk), jnp.bfloat16),
        in_specs=[smem] * len(tables)
        + [vmem] * 2
        + [pl.BlockSpec(memory_space=pl.ANY)] * (len(operands) - len(tables) - 2),
        out_specs=pl.BlockSpec(memory_space=pl.ANY),
        scratch_shapes=[
            pltpu.VMEM((count, STEPS, nz, blk, blk), jnp.bfloat16),
            pltpu.VMEM((blk, STEPS * nz * blk), jnp.bfloat16),
            pltpu.VMEM((count, kept, blk, blk), jnp.bfloat16),
            pltpu.SMEM((STEPS * rows, 2 * rows), jnp.int32),
            pltpu.SemaphoreType.DMA((count, STEPS)),
            pltpu.SemaphoreType.DMA((count,)),
        ],
        input_output_aliases=aliases,
        compiler_params=pltpu.CompilerParams(vmem_limit_bytes=16 * 1024 * 1024),
        cost_estimate=pl.CostEstimate(flops=flops, bytes_accessed=4 * 1024 * 1024, transcendentals=0),
        name="multiply_rows",
    )(*operands)


def local(a_vals, a_cols, b_vals, b_cols, c_cols, panel_owner, atom_size):
    row_count = lax.axis_size("row")
    col_count = lax.axis_size("col")
    own_a, own_ac = a_vals[0, 0], a_cols[0, 0]
    stored_b, stored_bc = b_vals[0, 0], b_cols[0, 0]
    targets = c_cols[0, 0]
    rows = own_a.shape[1]
    hops = col_count - 1

    arrived = [[] for _ in range(rows)]

    def send(row, hop, piece):
        route = [(hop, hop + 1), (col_count - 1 - hop, col_count - 2 - hop)]
        arrived[row].append(lax.ppermute(piece, "col", route))

    for row in range(min(AHEAD, rows)):
        (newest,) = relay(panel_owner, own_a, row, None, 0, None, [newest] if row else [])
        send(row, 0, newest)
    from_next = [((i + 1) % row_count, i) for i in range(row_count)]
    moved_b = lax.ppermute(stored_b, "row", from_next)
    moved_bc = lax.ppermute(stored_bc, "row", from_next)
    turned = [own_ac] + [
        lax.ppermute(own_ac, "col", [(i, (i + d) % col_count) for i in range(col_count)])
        for d in range(1, col_count)
    ]
    for step in range(1, rows + hops - 1):
        for hop in range(1, hops):
            row = step - hop
            if not 0 <= row < rows:
                continue
            following = row + AHEAD if hop == 1 and row + AHEAD < rows else None
            after = [newest]
            if step == 2 and hop == 1:
                after += [moved_bc] + turned
            if hop == hops - 1 and row >= 2:
                after.append(arrived[row - 2][hop])
            made = relay(panel_owner, own_a, row, following, hop, arrived[row][hop - 1], after)
            newest = made[0]
            send(row, hop, made[0])
            if following is not None:
                send(following, 0, made[1])
    turned = jnp.stack(turned)

    tables = (panel_owner, atom_size, turned, stored_bc, moved_bc, targets)
    result = None
    for first, count in ((0, rows - 1), (rows - 1, 1)):
        result = multiply_rows(first, count, tables, (stored_b, moved_b), own_a, arrived, result)
    return result[None, None]


def solution(mesh):
    placed = (
        P("row", "col", None, None, None, None, None),
        P("row", "col", None, None, None),
        P("row", "col", None, None, None, None),
        P("row", "col", None, None),
        P("row", "col", None, None),
        P(),
        P(),
    )
    return jax.shard_map(
        local,
        mesh=mesh,
        in_specs=placed,
        out_specs=P("row", "col", None, None, None, None),
        check_vma=False,
    )
```

```python
import functools

import jax
import jax.numpy as jnp
from jax import lax
from jax.experimental import pallas as pl
from jax.experimental.pallas import tpu as pltpu
from jax.sharding import PartitionSpec as P

STEPS = 2
AHEAD = 2
MIB = 1024 * 1024

SMEM = pl.BlockSpec(memory_space=pltpu.SMEM)
VMEM = pl.BlockSpec(memory_space=pltpu.VMEM)
ANYWHERE = pl.BlockSpec(memory_space=pl.ANY)


def places_of(owner_ref):
    row_id, row_count = lax.axis_index("row"), lax.axis_size("row")
    panels = [lax.rem(row_id + t, row_count) for t in range(STEPS)]
    places = [owner_ref[row_id, k] for k in panels]
    return panels, [lax.div(p, 2) for p in places], [lax.rem(p, 2) for p in places]


def relay_kernel(row, following, hop, waits, owner, own, *refs):
    refs = list(refs)
    arrived = refs.pop(0) if hop else None
    del refs[:waits]
    onward = refs.pop(0)
    fresh = refs.pop(0) if following is not None else None
    kept, sem = refs
    _, holders, slots = places_of(owner)
    col_id, last = lax.axis_index("col"), lax.axis_size("col") - 1
    sends = (col_id == hop) | (col_id == last - hop)
    starts = (col_id == 0) | (col_id == last)
    jobs = []
    for t in range(STEPS):
        mine = holders[t] == col_id
        jobs.append((sends & mine, pltpu.make_async_copy(own.at[slots[t], row], onward.at[t], sem.at[0, t])))
        if following is not None:
            copy = pltpu.make_async_copy(own.at[slots[t], following], fresh.at[t], sem.at[1, t])
            jobs.append((starts, copy))
        if hop:
            wanted = ((col_id == hop) & (holders[t] < col_id)) | (
                (col_id == last - hop) & (holders[t] > col_id)
            )
            jobs.append((wanted, pltpu.make_async_copy(arrived.at[t], kept.at[row, t], sem.at[2, t])))
    for when, copy in jobs:
        pl.when(when)(copy.start)
    if hop:
        for t in range(STEPS):

            @pl.when(sends & (holders[t] != col_id))
            def _():
                onward[t] = arrived[t]

    for when, copy in jobs:
        pl.when(when)(copy.wait)


def relay(owner, own, row, following, hop, arrived, kept, after):
    operands = [owner, own]
    specs = [SMEM, ANYWHERE]
    if hop:
        operands.append(arrived)
        specs.append(VMEM)
    if kept is not None:
        after = [kept] + after
    operands += after
    specs += [ANYWHERE] * len(after)
    aliases = {}
    outs = 1 + (following is not None)
    if kept is not None:
        aliases = {2 + (hop > 0): outs}
    piece = jax.ShapeDtypeStruct((STEPS,) + own.shape[2:], own.dtype)
    whole = jax.ShapeDtypeStruct((own.shape[1],) + piece.shape, own.dtype)
    return pl.pallas_call(
        functools.partial(relay_kernel, row, following, hop, len(after)),
        out_shape=[piece] * outs + [whole],
        in_specs=specs,
        out_specs=[VMEM] * outs + [ANYWHERE],
        scratch_shapes=[pltpu.SemaphoreType.DMA((3, STEPS))],
        input_output_aliases=aliases,
        compiler_params=pltpu.CompilerParams(vmem_limit_bytes=4 * MIB),
        cost_estimate=pl.CostEstimate(flops=0, bytes_accessed=MIB, transcendentals=0),
        name="relay",
    )(*operands)


def plan_kernel(owner, atoms, bcols0, bcols1, ccols, *refs):
    acols, plan, found = refs[:-2], refs[-2], refs[-1]
    panels, holders, slots = places_of(owner)
    row_id, col_id, col_count = lax.axis_index("row"), lax.axis_index("col"), lax.axis_size("col")
    panel_rows, nzb = bcols0.shape
    rows, kept = ccols.shape
    nz = acols[0].shape[-1]
    width = STEPS * nz
    columns = found.shape[1]

    def clear(j, carry):
        for c in range(columns):
            found[j, c] = -1
        return carry

    lax.fori_loop(0, STEPS * panel_rows, clear, 0)

    def fill(j, carry):
        for t, bcols in enumerate((bcols0, bcols1)):
            for n in range(nzb):
                found[t * panel_rows + j, bcols[j, n]] = j * nzb + n
        return carry

    lax.fori_loop(0, panel_rows, fill, 0)

    def one_row(i, carry):
        for e in range(kept):
            plan[i, kept * width + width + 1 + e] = atoms[col_id * columns + ccols[i, e]]
        plan[i, kept * width + width] = atoms[row_id * panel_rows + i]
        for t in range(STEPS):
            turn = lax.rem(col_id - holders[t] + col_count, col_count)
            for m in range(nz):
                j = acols[0][slots[t], i, m]
                for d in range(1, len(acols)):
                    j = jnp.where(turn == d, acols[d][slots[t], i, m], j)
                q = t * nz + m
                plan[i, kept * width + q] = atoms[panels[t] * panel_rows + j]
                for e in range(kept):
                    plan[i, e * width + q] = found[t * panel_rows + j, ccols[i, e]]
        return carry

    lax.fori_loop(0, rows, one_row, 0)


def make_plan(owner, atoms, bcols0, bcols1, ccols, acols):
    rows, kept = ccols.shape
    width = STEPS * acols[0].shape[-1]
    operands = [owner, atoms, bcols0, bcols1, ccols, *acols]
    return pl.pallas_call(
        plan_kernel,
        out_shape=jax.ShapeDtypeStruct((rows, kept * width + width + 1 + kept), jnp.int32),
        in_specs=[SMEM] * len(operands),
        out_specs=SMEM,
        scratch_shapes=[pltpu.SMEM((STEPS * rows, 2 * rows), jnp.int32)],
        compiler_params=pltpu.CompilerParams(vmem_limit_bytes=4 * MIB),
        cost_estimate=pl.CostEstimate(flops=0, bytes_accessed=MIB, transcendentals=0),
        name="make_plan",
    )(*operands)


def rows_kernel(first, count, owner, plan, b0, b1, own, passed, *refs):
    arrived = refs[:count]
    out, a_vm, left_vm, o_vm, a_sem, o_sem = refs[-6:]
    kept, blk = o_vm.shape[1], o_vm.shape[-1]
    nz = a_vm.shape[2]
    width = STEPS * nz
    col_id, last = lax.axis_index("col"), lax.axis_size("col") - 1
    _, holders, slots = places_of(owner)
    edge = (col_id == 0) | (col_id == last)
    waits = []
    for at in range(count):
        for t in range(STEPS):
            mine = holders[t] == col_id
            dst, sem = a_vm.at[at, t], a_sem.at[at, t]
            pl.when(mine)(pltpu.make_async_copy(own.at[slots[t], first + at], dst, sem).start)
            copy = pltpu.make_async_copy(passed.at[first + at, t], dst, sem)
            pl.when(jnp.logical_not(mine | edge))(copy.start)
            waits.append((mine | jnp.logical_not(edge), copy))

            @pl.when(edge & jnp.logical_not(mine))
            def _():
                a_vm[at, t] = arrived[at][t]

    for when, copy in waits:
        pl.when(when)(copy.wait)

    lane = lax.broadcasted_iota(jnp.int32, (blk, blk), 1)
    sub = lax.broadcasted_iota(jnp.int32, (blk, blk), 0)
    flat = [b.reshape(b.shape[0] * b.shape[1], blk, blk) for b in (b0, b1)]

    def one_row(at, carry):
        i = first + at
        for t in range(STEPS):
            for m in range(nz):
                q = t * nz + m
                left_vm[:, q * blk : (q + 1) * blk] = jnp.where(
                    lane < plan[i, kept * width + q], a_vm[at, t, m], jnp.zeros((), a_vm.dtype)
                )
        row_size = plan[i, kept * width + width]

        def one_pair(p, carry):
            sides = []
            for e in range(2):
                parts = []
                for q in range(width):
                    n = plan[i, (2 * p + e) * width + q]
                    block = flat[q // nz][jnp.maximum(n, 0)]
                    parts.append(jnp.where(n >= 0, block, jnp.zeros((), block.dtype)))
                sides.append(jnp.concatenate(parts, axis=0))
            total = jnp.dot(
                left_vm[...], jnp.concatenate(sides, axis=1), preferred_element_type=jnp.float32
            )
            for e in range(2):
                col_size = plan[i, kept * width + width + 1 + 2 * p + e]
                inside = (sub < row_size) & (lane < col_size)
                part = total[:, e * blk : (e + 1) * blk]
                o_vm[at, 2 * p + e] = jnp.where(inside, part, 0.0).astype(o_vm.dtype)
            return carry

        lax.fori_loop(0, kept // 2, one_pair, 0)
        pltpu.make_async_copy(o_vm.at[at], out.at[i], o_sem.at[at]).start()
        return carry

    lax.fori_loop(0, count, one_row, 0)
    for at in range(count):
        pltpu.make_async_copy(o_vm.at[at], out.at[first + at], o_sem.at[at]).wait()


def multiply_rows(first, count, owner, plan, b_panels, own, passed, arrived, kept, so_far):
    rows, nz, blk = own.shape[1], own.shape[2], own.shape[-1]
    operands = [owner, plan, *b_panels, own, passed, *arrived]
    specs = [SMEM] * 2 + [VMEM] * 2 + [ANYWHERE] * 2 + [VMEM] * count
    aliases = {}
    if so_far is not None:
        aliases = {len(operands): 0}
        operands.append(so_far)
        specs.append(ANYWHERE)
    flops = 2 * count * blk * blk * blk * STEPS * nz * kept
    return pl.pallas_call(
        functools.partial(rows_kernel, first, count),
        out_shape=jax.ShapeDtypeStruct((rows, kept, blk, blk), jnp.bfloat16),
        in_specs=specs,
        out_specs=ANYWHERE,
        scratch_shapes=[
            pltpu.VMEM((count, STEPS, nz, blk, blk), jnp.bfloat16),
            pltpu.VMEM((blk, STEPS * nz * blk), jnp.bfloat16),
            pltpu.VMEM((count, kept, blk, blk), jnp.bfloat16),
            pltpu.SemaphoreType.DMA((count, STEPS)),
            pltpu.SemaphoreType.DMA((count,)),
        ],
        input_output_aliases=aliases,
        compiler_params=pltpu.CompilerParams(vmem_limit_bytes=16 * MIB),
        cost_estimate=pl.CostEstimate(flops=flops, bytes_accessed=4 * MIB, transcendentals=0),
        name="multiply_rows",
    )(*operands)


def local(a_vals, a_cols, b_vals, b_cols, c_cols, panel_owner, atom_size):
    row_count = lax.axis_size("row")
    col_count = lax.axis_size("col")
    own_a, own_ac = a_vals[0, 0], a_cols[0, 0]
    stored_b, stored_bc = b_vals[0, 0], b_cols[0, 0]
    targets = c_cols[0, 0]
    rows = own_a.shape[1]
    hops = col_count - 1

    arrived = [[] for _ in range(rows)]
    passed = None

    def send(row, hop, piece):
        route = [(hop, hop + 1), (col_count - 1 - hop, col_count - 2 - hop)]
        arrived[row].append(lax.ppermute(piece, "col", route))

    for row in range(min(AHEAD, rows)):
        piece, passed = relay(panel_owner, own_a, row, None, 0, None, passed, [])
        send(row, 0, piece)
    from_next = [((i + 1) % row_count, i) for i in range(row_count)]
    moved_b = lax.ppermute(stored_b, "row", from_next)
    moved_bc = lax.ppermute(stored_bc, "row", from_next)
    turned = [own_ac] + [
        lax.ppermute(own_ac, "col", [(i, (i + d) % col_count) for i in range(col_count)])
        for d in range(1, col_count)
    ]
    plan = None
    for step in range(1, rows + hops - 1):
        for hop in range(1, hops):
            row = step - hop
            if not 0 <= row < rows:
                continue
            following = row + AHEAD if hop == 1 and row + AHEAD < rows else None
            after = []
            if step == 3 and hop == 1:
                plan = make_plan(panel_owner, atom_size, stored_bc, moved_bc, targets, turned)
                after.append(plan)
            if hop == hops - 1 and row >= 2:
                after.append(arrived[row - 2][hop])
            *made, passed = relay(panel_owner, own_a, row, following, hop, arrived[row][hop - 1], passed, after)
            send(row, hop, made[0])
            if following is not None:
                send(following, 0, made[1])

    result = None
    for first, count in ((0, rows - 1), (rows - 1, 1)):
        ends = [arrived[i][-1] for i in range(first, first + count)]
        result = multiply_rows(
            first, count, panel_owner, plan, (stored_b, moved_b), own_a, passed, ends, targets.shape[1], result
        )
    return result[None, None]


def solution(mesh):
    placed = (
        P("row", "col", None, None, None, None, None),
        P("row", "col", None, None, None),
        P("row", "col", None, None, None, None),
        P("row", "col", None, None),
        P("row", "col", None, None),
        P(),
        P(),
    )
    return jax.shard_map(
        local,
        mesh=mesh,
        in_specs=placed,
        out_specs=P("row", "col", None, None, None, None),
        check_vma=False,
    )
```

```python
import functools

import jax
import jax.numpy as jnp
from jax import lax
from jax.experimental import pallas as pl
from jax.experimental.pallas import tpu as pltpu
from jax.sharding import PartitionSpec as P

STEPS = 2
NOTED = 1
NOTE = 16
MIB = 1024 * 1024

SMEM = pl.BlockSpec(memory_space=pltpu.SMEM)
VMEM = pl.BlockSpec(memory_space=pltpu.VMEM)
ANYWHERE = pl.BlockSpec(memory_space=pl.ANY)


def places_of(owner_ref):
    row_id, row_count = lax.axis_index("row"), lax.axis_size("row")
    panels = [lax.rem(row_id + t, row_count) for t in range(STEPS)]
    places = [owner_ref[row_id, k] for k in panels]
    return panels, [lax.div(p, 2) for p in places], [lax.rem(p, 2) for p in places]


def lag_of(hop, hops):
    return hop + (2 * hop >= hops)


def relay_kernel(roles, waits, owner, own, *refs):
    refs = list(refs)
    notes = refs.pop(0) if any(row == NOTED for row, _, _ in roles) else None
    arrivals = [refs.pop(0) if arrives else None for _, _, arrives in roles]
    del refs[:waits]
    onward, sem = refs
    _, holders, slots = places_of(owner)
    col_id, last = lax.axis_index("col"), lax.axis_size("col") - 1
    size = own.shape[2]
    jobs = []
    for place, ((row, hop, _), arrived) in enumerate(zip(roles, arrivals)):
        sends = (col_id == hop) | (col_id == last - hop)
        for t in range(STEPS):
            mine = sends if hop == 0 else sends & (holders[t] == col_id)
            dst = onward.at[t, pl.ds(0, size)]
            jobs.append((mine, pltpu.make_async_copy(own.at[slots[t], row], dst, sem.at[place, t])))
            if row == NOTED:
                dst = onward.at[t, pl.ds(size, NOTE)]
                jobs.append((mine, pltpu.make_async_copy(notes.at[slots[t]], dst, sem.at[place, STEPS + t])))
    for when, copy in jobs:
        pl.when(when)(copy.start)
    for (row, hop, _), arrived in zip(roles, arrivals):
        if arrived is None:
            continue
        sends = (col_id == hop) | (col_id == last - hop)
        extent = size + (NOTE if row == NOTED else 0)
        for t in range(STEPS):

            @pl.when(sends & (holders[t] != col_id))
            def _():
                onward[t, :extent] = arrived[t, :extent]

    for when, copy in jobs:
        pl.when(when)(copy.wait)


def relay(owner, own, notes, roles, arrivals, after, limit):
    noted = any(row == NOTED for row, _ in roles)
    size = own.shape[2] + (NOTE if noted else 0)
    given = [a for a in arrivals if a is not None]
    operands = [owner, own] + [notes] * noted + given + after
    specs = [SMEM, ANYWHERE] + [ANYWHERE] * noted + [VMEM] * len(given) + [ANYWHERE] * len(after)
    roles = tuple((row, hop, a is not None) for (row, hop), a in zip(roles, arrivals))
    return pl.pallas_call(
        functools.partial(relay_kernel, roles, len(after)),
        out_shape=jax.ShapeDtypeStruct((STEPS, size, own.shape[3]), own.dtype),
        in_specs=specs,
        out_specs=VMEM,
        scratch_shapes=[pltpu.SemaphoreType.DMA((2, 2 * STEPS))],
        compiler_params=pltpu.CompilerParams(vmem_limit_bytes=limit),
        cost_estimate=pl.CostEstimate(flops=0, bytes_accessed=MIB, transcendentals=0),
        name="relay",
    )(*operands)


def plan_kernel(owner, atoms, bcols0, bcols1, ccols, *refs):
    notes, arrivals = refs[0], refs[1:-6]
    plan, found, note_vm, note_sm, sem = refs[-5:]
    panels, holders, slots = places_of(owner)
    row_id, col_id, col_count = lax.axis_index("row"), lax.axis_index("col"), lax.axis_size("col")
    panel_rows, nzb = bcols0.shape
    rows, kept = ccols.shape
    nz = (plan.shape[1] - 1 - kept) // (STEPS * (kept + 1))
    width = STEPS * nz
    columns = found.shape[1]
    for t in range(STEPS):
        hop = jnp.where(holders[t] < col_id, col_id - 1, col_count - 2 - col_id)
        mine = holders[t] == col_id

        @pl.when(mine)
        def _():
            note_vm[t] = notes[slots[t]].astype(jnp.float32).astype(jnp.int32)

        for h, arrived in enumerate(arrivals):

            @pl.when(jnp.logical_not(mine) & (hop == h))
            def _():
                note_vm[t] = arrived[t, arrived.shape[1] - NOTE :].astype(jnp.float32).astype(jnp.int32)

    copy = pltpu.make_async_copy(note_vm, note_sm, sem)
    copy.start()

    def clear(j, carry):
        for c in range(columns):
            found[j, c] = -1
        return carry

    lax.fori_loop(0, STEPS * panel_rows, clear, 0)

    def fill(j, carry):
        for t, bcols in enumerate((bcols0, bcols1)):
            for n in range(nzb):
                found[t * panel_rows + j, bcols[j, n]] = j * nzb + n
        return carry

    lax.fori_loop(0, panel_rows, fill, 0)
    copy.wait()

    def one_row(i, carry):
        for e in range(kept):
            plan[i, kept * width + width + 1 + e] = atoms[col_id * columns + ccols[i, e]]
        plan[i, kept * width + width] = atoms[row_id * panel_rows + i]
        for t in range(STEPS):
            for m in range(nz):
                j = note_sm[t, i, m]
                q = t * nz + m
                plan[i, kept * width + q] = atoms[panels[t] * panel_rows + j]
                for e in range(kept):
                    plan[i, e * width + q] = found[t * panel_rows + j, ccols[i, e]]
        return carry

    lax.fori_loop(0, rows, one_row, 0)


def make_plan(owner, atoms, bcols0, bcols1, ccols, notes, arrivals, nz, after):
    rows, kept = ccols.shape
    width = STEPS * nz
    operands = [owner, atoms, bcols0, bcols1, ccols, notes, *arrivals, after]
    return pl.pallas_call(
        plan_kernel,
        out_shape=jax.ShapeDtypeStruct((rows, kept * width + width + 1 + kept), jnp.int32),
        in_specs=[SMEM] * 5 + [VMEM] * (1 + len(arrivals)) + [ANYWHERE],
        out_specs=SMEM,
        scratch_shapes=[
            pltpu.SMEM((STEPS * rows, 2 * rows), jnp.int32),
            pltpu.VMEM((STEPS, NOTE, notes.shape[-1]), jnp.int32),
            pltpu.SMEM((STEPS, NOTE, notes.shape[-1]), jnp.int32),
            pltpu.SemaphoreType.DMA,
        ],
        compiler_params=pltpu.CompilerParams(vmem_limit_bytes=8 * MIB),
        cost_estimate=pl.CostEstimate(flops=0, bytes_accessed=MIB, transcendentals=0),
        name="make_plan",
    )(*operands)


def rows_kernel(first, count, hops, owner, plan, b0, b1, own, *refs):
    arrived = [refs[at * hops : (at + 1) * hops] for at in range(count)]
    out, a_vm, left_vm, o_vm, a_sem, o_sem = refs[-6:]
    kept, blk = o_vm.shape[1], o_vm.shape[-1]
    size = a_vm.shape[2]
    nz = size // blk
    width = STEPS * nz
    col_id, last = lax.axis_index("col"), lax.axis_size("col") - 1
    _, holders, slots = places_of(owner)
    copies = []
    for at in range(count):
        for t in range(STEPS):
            copy = pltpu.make_async_copy(own.at[slots[t], first + at], a_vm.at[at, t], a_sem.at[at, t])
            copies.append((holders[t] == col_id, copy))
    for when, copy in copies:
        pl.when(when)(copy.start)
    for t in range(STEPS):
        hop = jnp.where(holders[t] < col_id, col_id - 1, last - 1 - col_id)
        for h in range(hops):

            @pl.when((holders[t] != col_id) & (hop == h))
            def _():
                for at in range(count):

                    def one_block(m, carry):
                        part = pl.ds(pl.multiple_of(m * blk, blk), blk)
                        a_vm[at, t, part] = arrived[at][h][t, part]
                        return carry

                    lax.fori_loop(0, nz, one_block, 0)

    for when, copy in copies:
        pl.when(when)(copy.wait)

    lane = lax.broadcasted_iota(jnp.int32, (blk, blk), 1)
    sub = lax.broadcasted_iota(jnp.int32, (blk, blk), 0)
    flat = [b.reshape(b.shape[0] * b.shape[1], blk, blk) for b in (b0, b1)]

    def one_row(at, carry):
        i = first + at
        for t in range(STEPS):
            for m in range(nz):
                q = t * nz + m
                left_vm[:, q * blk : (q + 1) * blk] = jnp.where(
                    lane < plan[i, kept * width + q],
                    a_vm[at, t, m * blk : (m + 1) * blk],
                    jnp.zeros((), a_vm.dtype),
                )
        row_size = plan[i, kept * width + width]

        for p in range(kept // 2):
            sides = []
            for e in range(2):
                parts = []
                for q in range(width):
                    n = plan[i, (2 * p + e) * width + q]
                    block = flat[q // nz][jnp.maximum(n, 0)]
                    parts.append(jnp.where(n >= 0, block, jnp.zeros((), block.dtype)))
                sides.append(jnp.concatenate(parts, axis=0))
            total = jnp.dot(
                left_vm[...], jnp.concatenate(sides, axis=1), preferred_element_type=jnp.float32
            )
            for e in range(2):
                col_size = plan[i, kept * width + width + 1 + 2 * p + e]
                inside = (sub < row_size) & (lane < col_size)
                part = total[:, e * blk : (e + 1) * blk]
                o_vm[at, 2 * p + e] = jnp.where(inside, part, 0.0).astype(o_vm.dtype)
        pltpu.make_async_copy(o_vm.at[at], out.at[i], o_sem.at[at]).start()
        return carry

    lax.fori_loop(0, count, one_row, 0)
    for at in range(count):
        pltpu.make_async_copy(o_vm.at[at], out.at[first + at], o_sem.at[at]).wait()


def multiply_rows(first, count, owner, plan, b_panels, own, arrived, kept, so_far):
    rows, size, blk = own.shape[1:]
    nz, hops = size // blk, len(arrived[0])
    operands = [owner, plan, *b_panels, own]
    for at in range(count):
        operands += arrived[at]
    specs = [SMEM] * 2 + [VMEM] * 2 + [ANYWHERE] + [VMEM] * (count * hops)
    aliases = {}
    if so_far is not None:
        aliases = {len(operands): 0}
        operands.append(so_far)
        specs.append(ANYWHERE)
    flops = 2 * count * blk * blk * blk * STEPS * nz * kept
    limit = (12 + count * hops // 2) * MIB
    return pl.pallas_call(
        functools.partial(rows_kernel, first, count, hops),
        out_shape=jax.ShapeDtypeStruct((rows, kept, blk, blk), jnp.bfloat16),
        in_specs=specs,
        out_specs=ANYWHERE,
        scratch_shapes=[
            pltpu.VMEM((count, STEPS, size, blk), jnp.bfloat16),
            pltpu.VMEM((blk, STEPS * size), jnp.bfloat16),
            pltpu.VMEM((count, kept, blk, blk), jnp.bfloat16),
            pltpu.SemaphoreType.DMA((count, STEPS)),
            pltpu.SemaphoreType.DMA((count,)),
        ],
        input_output_aliases=aliases,
        compiler_params=pltpu.CompilerParams(vmem_limit_bytes=limit),
        cost_estimate=pl.CostEstimate(flops=flops, bytes_accessed=4 * MIB, transcendentals=0),
        name="multiply_rows",
    )(*operands)


def local(a_vals, a_cols, b_vals, b_cols, c_cols, panel_owner, atom_size):
    row_count = lax.axis_size("row")
    col_count = lax.axis_size("col")
    stored_b, stored_bc = b_vals[0, 0], b_cols[0, 0]
    targets = c_cols[0, 0]
    slot_count, rows, nz, blk = a_vals.shape[2:6]
    own_a = a_vals.reshape(slot_count, rows, nz * blk, blk)
    notes = jnp.pad(
        a_cols[0, 0].astype(own_a.dtype), ((0, 0), (0, NOTE - rows), (0, blk - nz))
    )
    hops = col_count - 1
    from_next = [((i + 1) % row_count, i) for i in range(row_count)]

    arrived = [[None] * hops for _ in range(rows)]
    newest = plan = moved_b = moved_bc = None
    edges = []
    last_slot = rows + lag_of(hops - 1, hops) - 1
    for slot in range(last_slot + 1):
        for lane in range((hops + 1) // 2):
            roles = []
            for hop in sorted({lane, hops - 1 - lane}):
                row = slot - lag_of(hop, hops)
                if 0 <= row < rows:
                    roles.append((row, hop))
            if not roles:
                continue
            after = [] if newest is None else [newest]
            if slot == 2 and lane == 0:
                after.append(moved_bc)
            if lane == 0:
                after += [got for got in edges[slot - 2 : slot - 1] if slot >= 2]
            if slot == last_slot:
                plan = make_plan(
                    panel_owner, atom_size, stored_bc, moved_bc, targets, notes, arrived[NOTED], nz, newest
                )
                after.append(plan)
            arrivals = [arrived[row][hop - 1] if hop else None for row, hop in roles]
            limit = 62 * MIB if newest is None else 4 * MIB
            newest = relay(panel_owner, own_a, notes, roles, arrivals, after, limit)
            route = []
            for _, hop in roles:
                route += [(hop, hop + 1), (hops - hop, hops - hop - 1)]
            got = lax.ppermute(newest, "col", route)
            for row, hop in roles:
                arrived[row][hop] = got
            if lane == 0:
                edges.append(got)
            if slot == 1 and lane == 0:
                moved_b = lax.ppermute(stored_b, "row", from_next)
                moved_bc = lax.ppermute(stored_bc, "row", from_next)

    result = None
    for first, count in ((0, rows - 1), (rows - 1, 1)):
        result = multiply_rows(
            first,
            count,
            panel_owner,
            plan,
            (stored_b, moved_b),
            own_a,
            arrived[first : first + count],
            targets.shape[1],
            result,
        )
    return result[None, None]


def solution(mesh):
    placed = (
        P("row", "col", None, None, None, None, None),
        P("row", "col", None, None, None),
        P("row", "col", None, None, None, None),
        P("row", "col", None, None),
        P("row", "col", None, None),
        P(),
        P(),
    )
    return jax.shard_map(
        local,
        mesh=mesh,
        in_specs=placed,
        out_specs=P("row", "col", None, None, None, None),
        check_vma=False,
    )
```

```python
import functools

import jax
import jax.numpy as jnp
from jax import lax
from jax.experimental import pallas as pl
from jax.experimental.pallas import tpu as pltpu
from jax.sharding import PartitionSpec as P

STEPS = 2
NOTED = 1
NOTE = 16
MIB = 1024 * 1024

SMEM = pl.BlockSpec(memory_space=pltpu.SMEM)
VMEM = pl.BlockSpec(memory_space=pltpu.VMEM)
ANYWHERE = pl.BlockSpec(memory_space=pl.ANY)


def places_of(owner_ref):
    row_id, row_count = lax.axis_index("row"), lax.axis_size("row")
    panels = [lax.rem(row_id + t, row_count) for t in range(STEPS)]
    places = [owner_ref[row_id, k] for k in panels]
    return panels, [lax.div(p, 2) for p in places], [lax.rem(p, 2) for p in places]


def lag_of(hop, hops):
    return hop + (2 * hop >= hops)


def relay_kernel(roles, waits, owner, own, *refs):
    refs = list(refs)
    notes = refs.pop(0) if any(row == NOTED for row, _, _ in roles) else None
    arrivals = [refs.pop(0) if arrives else None for _, _, arrives in roles]
    del refs[:waits]
    onward, sem = refs
    _, holders, slots = places_of(owner)
    col_id, last = lax.axis_index("col"), lax.axis_size("col") - 1
    size = own.shape[2]
    jobs = []
    for place, ((row, hop, _), arrived) in enumerate(zip(roles, arrivals)):
        sends = (col_id == hop) | (col_id == last - hop)
        for t in range(STEPS):
            mine = sends if hop == 0 else sends & (holders[t] == col_id)
            dst = onward.at[t, pl.ds(0, size)]
            jobs.append((mine, pltpu.make_async_copy(own.at[slots[t], row], dst, sem.at[place, t])))
            if row == NOTED:
                dst = onward.at[t, pl.ds(size, NOTE)]
                jobs.append((mine, pltpu.make_async_copy(notes.at[slots[t]], dst, sem.at[place, STEPS + t])))
    for when, copy in jobs:
        pl.when(when)(copy.start)
    for (row, hop, _), arrived in zip(roles, arrivals):
        if arrived is None:
            continue
        sends = (col_id == hop) | (col_id == last - hop)
        extent = size + (NOTE if row == NOTED else 0)
        for t in range(STEPS):

            @pl.when(sends & (holders[t] != col_id))
            def _():
                onward[t, :extent] = arrived[t, :extent]

    for when, copy in jobs:
        pl.when(when)(copy.wait)


def relay(owner, own, notes, roles, arrivals, after, limit, name):
    noted = any(row == NOTED for row, _ in roles)
    size = own.shape[2] + (NOTE if noted else 0)
    given = [a for a in arrivals if a is not None]
    operands = [owner, own] + [notes] * noted + given + after
    specs = [SMEM, ANYWHERE] + [ANYWHERE] * noted + [VMEM] * len(given) + [ANYWHERE] * len(after)
    roles = tuple((row, hop, a is not None) for (row, hop), a in zip(roles, arrivals))
    return pl.pallas_call(
        functools.partial(relay_kernel, roles, len(after)),
        out_shape=jax.ShapeDtypeStruct((STEPS, size, own.shape[3]), own.dtype),
        in_specs=specs,
        out_specs=VMEM,
        scratch_shapes=[pltpu.SemaphoreType.DMA((2, 2 * STEPS))],
        compiler_params=pltpu.CompilerParams(vmem_limit_bytes=limit),
        cost_estimate=pl.CostEstimate(flops=10**9, bytes_accessed=1024, transcendentals=0),
        name=name,
    )(*operands)


def plan_kernel(owner, atoms, bcols0, bcols1, ccols, *refs):
    notes, arrivals = refs[0], refs[1:-6]
    plan, found, note_vm, note_sm, sem = refs[-5:]
    panels, holders, slots = places_of(owner)
    row_id, col_id, col_count = lax.axis_index("row"), lax.axis_index("col"), lax.axis_size("col")
    panel_rows, nzb = bcols0.shape
    rows, kept = ccols.shape
    nz = (plan.shape[1] - 1 - kept) // (STEPS * (kept + 1))
    width = STEPS * nz
    columns = found.shape[1]
    for t in range(STEPS):
        hop = jnp.where(holders[t] < col_id, col_id - 1, col_count - 2 - col_id)
        mine = holders[t] == col_id

        @pl.when(mine)
        def _():
            note_vm[t] = notes[slots[t]].astype(jnp.float32).astype(jnp.int32)

        for h, arrived in enumerate(arrivals):

            @pl.when(jnp.logical_not(mine) & (hop == h))
            def _():
                note_vm[t] = arrived[t, arrived.shape[1] - NOTE :].astype(jnp.float32).astype(jnp.int32)

    copy = pltpu.make_async_copy(note_vm, note_sm, sem)
    copy.start()

    def clear(j, carry):
        for c in range(columns):
            found[j, c] = -1
        return carry

    lax.fori_loop(0, STEPS * panel_rows, clear, 0)

    def fill(j, carry):
        for t, bcols in enumerate((bcols0, bcols1)):
            for n in range(nzb):
                found[t * panel_rows + j, bcols[j, n]] = j * nzb + n
        return carry

    lax.fori_loop(0, panel_rows, fill, 0)
    copy.wait()

    def one_row(i, carry):
        for e in range(kept):
            plan[i, kept * width + width + 1 + e] = atoms[col_id * columns + ccols[i, e]]
        plan[i, kept * width + width] = atoms[row_id * panel_rows + i]
        for t in range(STEPS):
            for m in range(nz):
                j = note_sm[t, i, m]
                q = t * nz + m
                plan[i, kept * width + q] = atoms[panels[t] * panel_rows + j]
                for e in range(kept):
                    plan[i, e * width + q] = found[t * panel_rows + j, ccols[i, e]]
        return carry

    lax.fori_loop(0, rows, one_row, 0)


def make_plan(owner, atoms, bcols0, bcols1, ccols, notes, arrivals, nz, after):
    rows, kept = ccols.shape
    width = STEPS * nz
    operands = [owner, atoms, bcols0, bcols1, ccols, notes, *arrivals, after]
    return pl.pallas_call(
        plan_kernel,
        out_shape=jax.ShapeDtypeStruct((rows, kept * width + width + 1 + kept), jnp.int32),
        in_specs=[SMEM] * 5 + [VMEM] * (1 + len(arrivals)) + [ANYWHERE],
        out_specs=SMEM,
        scratch_shapes=[
            pltpu.SMEM((STEPS * rows, 2 * rows), jnp.int32),
            pltpu.VMEM((STEPS, NOTE, notes.shape[-1]), jnp.int32),
            pltpu.SMEM((STEPS, NOTE, notes.shape[-1]), jnp.int32),
            pltpu.SemaphoreType.DMA,
        ],
        compiler_params=pltpu.CompilerParams(vmem_limit_bytes=8 * MIB),
        cost_estimate=pl.CostEstimate(flops=10**9, bytes_accessed=1024, transcendentals=0),
        name="make_plan",
    )(*operands)


def rows_kernel(first, count, hops, owner, plan, b0, b1, own, *refs):
    arrived = [refs[at * hops : (at + 1) * hops] for at in range(count)]
    out, a_vm, left_vm, o_vm, a_sem, o_sem = refs[-6:]
    kept, blk = o_vm.shape[1], o_vm.shape[-1]
    size = a_vm.shape[2]
    nz = size // blk
    width = STEPS * nz
    col_id, last = lax.axis_index("col"), lax.axis_size("col") - 1
    _, holders, slots = places_of(owner)
    copies = []
    for at in range(count):
        for t in range(STEPS):
            copy = pltpu.make_async_copy(own.at[slots[t], first + at], a_vm.at[at, t], a_sem.at[at, t])
            copies.append((holders[t] == col_id, copy))
    for when, copy in copies:
        pl.when(when)(copy.start)
    for t in range(STEPS):
        hop = jnp.where(holders[t] < col_id, col_id - 1, last - 1 - col_id)
        for h in range(hops):

            @pl.when((holders[t] != col_id) & (hop == h))
            def _():
                for at in range(count):

                    def one_block(m, carry):
                        part = pl.ds(pl.multiple_of(m * blk, blk), blk)
                        a_vm[at, t, part] = arrived[at][h][t, part]
                        return carry

                    lax.fori_loop(0, nz, one_block, 0)

    for when, copy in copies:
        pl.when(when)(copy.wait)

    lane = lax.broadcasted_iota(jnp.int32, (blk, blk), 1)
    sub = lax.broadcasted_iota(jnp.int32, (blk, blk), 0)
    flat = [b.reshape(b.shape[0] * b.shape[1], blk, blk) for b in (b0, b1)]

    def one_row(at, carry):
        i = first + at
        for t in range(STEPS):
            for m in range(nz):
                q = t * nz + m
                left_vm[:, q * blk : (q + 1) * blk] = jnp.where(
                    lane < plan[i, kept * width + q],
                    a_vm[at, t, m * blk : (m + 1) * blk],
                    jnp.zeros((), a_vm.dtype),
                )
        row_size = plan[i, kept * width + width]

        for p in range(kept // 2):
            sides = []
            for e in range(2):
                parts = []
                for q in range(width):
                    n = plan[i, (2 * p + e) * width + q]
                    block = flat[q // nz][jnp.maximum(n, 0)]
                    parts.append(jnp.where(n >= 0, block, jnp.zeros((), block.dtype)))
                sides.append(jnp.concatenate(parts, axis=0))
            total = jnp.dot(
                left_vm[...], jnp.concatenate(sides, axis=1), preferred_element_type=jnp.float32
            )
            for e in range(2):
                col_size = plan[i, kept * width + width + 1 + 2 * p + e]
                inside = (sub < row_size) & (lane < col_size)
                part = total[:, e * blk : (e + 1) * blk]
                o_vm[at, 2 * p + e] = jnp.where(inside, part, 0.0).astype(o_vm.dtype)
        pltpu.make_async_copy(o_vm.at[at], out.at[i], o_sem.at[at]).start()
        return carry

    lax.fori_loop(0, count, one_row, 0)
    for at in range(count):
        pltpu.make_async_copy(o_vm.at[at], out.at[first + at], o_sem.at[at]).wait()


def multiply_rows(first, count, owner, plan, b_panels, own, arrived, kept, so_far):
    rows, size, blk = own.shape[1:]
    nz, hops = size // blk, len(arrived[0])
    operands = [owner, plan, *b_panels, own]
    for at in range(count):
        operands += arrived[at]
    specs = [SMEM] * 2 + [VMEM] * 2 + [ANYWHERE] + [VMEM] * (count * hops)
    aliases = {}
    if so_far is not None:
        aliases = {len(operands): 0}
        operands.append(so_far)
        specs.append(ANYWHERE)
    flops = 2 * count * blk * blk * blk * STEPS * nz * kept
    limit = (12 + count * hops // 2) * MIB
    return pl.pallas_call(
        functools.partial(rows_kernel, first, count, hops),
        out_shape=jax.ShapeDtypeStruct((rows, kept, blk, blk), jnp.bfloat16),
        in_specs=specs,
        out_specs=ANYWHERE,
        scratch_shapes=[
            pltpu.VMEM((count, STEPS, size, blk), jnp.bfloat16),
            pltpu.VMEM((blk, STEPS * size), jnp.bfloat16),
            pltpu.VMEM((count, kept, blk, blk), jnp.bfloat16),
            pltpu.SemaphoreType.DMA((count, STEPS)),
            pltpu.SemaphoreType.DMA((count,)),
        ],
        input_output_aliases=aliases,
        compiler_params=pltpu.CompilerParams(vmem_limit_bytes=limit),
        cost_estimate=pl.CostEstimate(flops=flops, bytes_accessed=4 * MIB, transcendentals=0),
        name="multiply_rows",
    )(*operands)


def local(a_vals, a_cols, b_vals, b_cols, c_cols, panel_owner, atom_size):
    row_count = lax.axis_size("row")
    col_count = lax.axis_size("col")
    stored_b, stored_bc = b_vals[0, 0], b_cols[0, 0]
    targets = c_cols[0, 0]
    slot_count, rows, nz, blk = a_vals.shape[2:6]
    own_a = a_vals.reshape(slot_count, rows, nz * blk, blk)
    notes = jnp.pad(
        a_cols[0, 0].astype(own_a.dtype), ((0, 0), (0, NOTE - rows), (0, blk - nz))
    )
    hops = col_count - 1
    from_next = [((i + 1) % row_count, i) for i in range(row_count)]

    arrived = [[None] * hops for _ in range(rows)]
    newest = plan = moved_b = moved_bc = None
    edges = []
    last_slot = rows + lag_of(hops - 1, hops) - 1
    for slot in range(last_slot + 1):
        for lane in range((hops + 1) // 2):
            roles = []
            for hop in sorted({lane, hops - 1 - lane}):
                row = slot - lag_of(hop, hops)
                if 0 <= row < rows:
                    roles.append((row, hop))
            if not roles:
                continue
            after = [newest] if slot > 1 else []
            if lane == 0:
                before = 1 if slot > rows else 2
                after += edges[slot - before : slot - before + 1] if slot >= before + 1 else []
            if slot == last_slot:
                plan = make_plan(
                    panel_owner, atom_size, stored_bc, moved_bc, targets, notes, arrived[NOTED], nz, newest
                )
                after.append(plan)
            arrivals = [arrived[row][hop - 1] if hop else None for row, hop in roles]
            limit = 62 * MIB if newest is None else 4 * MIB
            newest = relay(panel_owner, own_a, notes, roles, arrivals, after, limit, f"lane{lane}_{slot}")
            if slot == lane == 1:
                behind_bc, behind_b, newest = lax.optimization_barrier((stored_bc, stored_b, newest))
                moved_bc = lax.ppermute(behind_bc, "row", from_next)
                moved_b = lax.ppermute(behind_b, "row", from_next)
            route = []
            for _, hop in roles:
                route += [(hop, hop + 1), (hops - hop, hops - hop - 1)]
            got = lax.ppermute(newest, "col", route)
            for row, hop in roles:
                arrived[row][hop] = got
            if lane == 0:
                edges.append(got)

    result = None
    for first, count in ((0, rows - 1), (rows - 1, 1)):
        result = multiply_rows(
            first,
            count,
            panel_owner,
            plan,
            (stored_b, moved_b),
            own_a,
            arrived[first : first + count],
            targets.shape[1],
            result,
        )
    return result[None, None]


def solution(mesh):
    placed = (
        P("row", "col", None, None, None, None, None),
        P("row", "col", None, None, None),
        P("row", "col", None, None, None, None),
        P("row", "col", None, None),
        P("row", "col", None, None),
        P(),
        P(),
    )
    return jax.shard_map(
        local,
        mesh=mesh,
        in_specs=placed,
        out_specs=P("row", "col", None, None, None, None),
        check_vma=False,
    )
```

```python
import functools

import jax
import jax.numpy as jnp
from jax import lax
from jax.experimental import pallas as pl
from jax.experimental.pallas import tpu as pltpu
from jax.sharding import PartitionSpec as P

STEPS = 2
NOTED = 1
NOTE = 16
MIB = 1024 * 1024

SMEM = pl.BlockSpec(memory_space=pltpu.SMEM)
VMEM = pl.BlockSpec(memory_space=pltpu.VMEM)
ANYWHERE = pl.BlockSpec(memory_space=pl.ANY)


def places_of(owner_ref):
    row_id, row_count = lax.axis_index("row"), lax.axis_size("row")
    panels = [lax.rem(row_id + t, row_count) for t in range(STEPS)]
    places = [owner_ref[row_id, k] for k in panels]
    return panels, [lax.div(p, 2) for p in places], [lax.rem(p, 2) for p in places]


def lag_of(hop, hops):
    return hop + (2 * hop >= hops)


def relay_kernel(roles, waits, owner, own, *refs):
    refs = list(refs)
    notes = refs.pop(0) if any(row == NOTED for row, _, _ in roles) else None
    arrivals = [refs.pop(0) if arrives else None for _, _, arrives in roles]
    del refs[:waits]
    onward, sem = refs
    _, holders, slots = places_of(owner)
    col_id, last = lax.axis_index("col"), lax.axis_size("col") - 1
    size = own.shape[2]
    jobs = []
    for place, ((row, hop, _), arrived) in enumerate(zip(roles, arrivals)):
        sends = (col_id == hop) | (col_id == last - hop)
        for t in range(STEPS):
            mine = sends if hop == 0 else sends & (holders[t] == col_id)
            dst = onward.at[t, pl.ds(0, size)]
            jobs.append((mine, pltpu.make_async_copy(own.at[slots[t], row], dst, sem.at[place, t])))
            if row == NOTED:
                dst = onward.at[t, pl.ds(size, NOTE)]
                jobs.append((mine, pltpu.make_async_copy(notes.at[slots[t]], dst, sem.at[place, STEPS + t])))
    for when, copy in jobs:
        pl.when(when)(copy.start)
    for (row, hop, _), arrived in zip(roles, arrivals):
        if arrived is None:
            continue
        sends = (col_id == hop) | (col_id == last - hop)
        extent = size + (NOTE if row == NOTED else 0)
        for t in range(STEPS):

            @pl.when(sends & (holders[t] != col_id))
            def _():
                onward[t, :extent] = arrived[t, :extent]

    for when, copy in jobs:
        pl.when(when)(copy.wait)


def relay(owner, own, notes, roles, arrivals, after, limit, name):
    noted = any(row == NOTED for row, _ in roles)
    size = own.shape[2] + (NOTE if noted else 0)
    given = [a for a in arrivals if a is not None]
    operands = [owner, own] + [notes] * noted + given + after
    specs = [SMEM, ANYWHERE] + [ANYWHERE] * noted + [VMEM] * len(given) + [ANYWHERE] * len(after)
    roles = tuple((row, hop, a is not None) for (row, hop), a in zip(roles, arrivals))
    return pl.pallas_call(
        functools.partial(relay_kernel, roles, len(after)),
        out_shape=jax.ShapeDtypeStruct((STEPS, size, own.shape[3]), own.dtype),
        in_specs=specs,
        out_specs=VMEM,
        scratch_shapes=[pltpu.SemaphoreType.DMA((2, 2 * STEPS))],
        compiler_params=pltpu.CompilerParams(vmem_limit_bytes=limit),
        cost_estimate=pl.CostEstimate(flops=10**9, bytes_accessed=1024, transcendentals=0),
        name=name,
    )(*operands)


def plan_kernel(owner, atoms, bcols0, bcols1, ccols, *refs):
    notes, arrivals = refs[0], refs[1:-6]
    plan, found, note_vm, note_sm, sem = refs[-5:]
    panels, holders, slots = places_of(owner)
    row_id, col_id, col_count = lax.axis_index("row"), lax.axis_index("col"), lax.axis_size("col")
    panel_rows, nzb = bcols0.shape
    rows, kept = ccols.shape
    nz = (plan.shape[1] - 1 - kept) // (STEPS * (kept + 1))
    width = STEPS * nz
    columns = found.shape[1]
    for t in range(STEPS):
        hop = jnp.where(holders[t] < col_id, col_id - 1, col_count - 2 - col_id)
        mine = holders[t] == col_id

        @pl.when(mine)
        def _():
            note_vm[t] = notes[slots[t]].astype(jnp.float32).astype(jnp.int32)

        for h, arrived in enumerate(arrivals):

            @pl.when(jnp.logical_not(mine) & (hop == h))
            def _():
                note_vm[t] = arrived[t, arrived.shape[1] - NOTE :].astype(jnp.float32).astype(jnp.int32)

    copy = pltpu.make_async_copy(note_vm, note_sm, sem)
    copy.start()

    def clear(j, carry):
        for c in range(columns):
            found[j, c] = -1
        return carry

    lax.fori_loop(0, STEPS * panel_rows, clear, 0)

    def fill(j, carry):
        for t, bcols in enumerate((bcols0, bcols1)):
            for n in range(nzb):
                found[t * panel_rows + j, bcols[j, n]] = j * nzb + n
        return carry

    lax.fori_loop(0, panel_rows, fill, 0)
    copy.wait()

    def one_row(i, carry):
        for e in range(kept):
            plan[i, kept * width + width + 1 + e] = atoms[col_id * columns + ccols[i, e]]
        plan[i, kept * width + width] = atoms[row_id * panel_rows + i]
        for t in range(STEPS):
            for m in range(nz):
                j = note_sm[t, i, m]
                q = t * nz + m
                plan[i, kept * width + q] = atoms[panels[t] * panel_rows + j]
                for e in range(kept):
                    plan[i, e * width + q] = found[t * panel_rows + j, ccols[i, e]]
        return carry

    lax.fori_loop(0, rows, one_row, 0)


def make_plan(owner, atoms, bcols0, bcols1, ccols, notes, arrivals, nz, after):
    rows, kept = ccols.shape
    width = STEPS * nz
    operands = [owner, atoms, bcols0, bcols1, ccols, notes, *arrivals, after]
    return pl.pallas_call(
        plan_kernel,
        out_shape=jax.ShapeDtypeStruct((rows, kept * width + width + 1 + kept), jnp.int32),
        in_specs=[SMEM] * 5 + [VMEM] * (1 + len(arrivals)) + [ANYWHERE],
        out_specs=SMEM,
        scratch_shapes=[
            pltpu.SMEM((STEPS * rows, 2 * rows), jnp.int32),
            pltpu.VMEM((STEPS, NOTE, notes.shape[-1]), jnp.int32),
            pltpu.SMEM((STEPS, NOTE, notes.shape[-1]), jnp.int32),
            pltpu.SemaphoreType.DMA,
        ],
        compiler_params=pltpu.CompilerParams(vmem_limit_bytes=8 * MIB),
        cost_estimate=pl.CostEstimate(flops=10**9, bytes_accessed=1024, transcendentals=0),
        name="make_plan",
    )(*operands)


def rows_kernel(first, count, hops, owner, plan, b0, b1, own, *refs):
    arrived = [refs[at * hops : (at + 1) * hops] for at in range(count)]
    out, a_vm, left_vm, o_vm, a_sem, o_sem = refs[-6:]
    kept, blk = o_vm.shape[1], o_vm.shape[-1]
    size = a_vm.shape[2]
    nz = size // blk
    width = STEPS * nz
    col_id, last = lax.axis_index("col"), lax.axis_size("col") - 1
    _, holders, slots = places_of(owner)
    copies = []
    for at in range(count):
        for t in range(STEPS):
            copy = pltpu.make_async_copy(own.at[slots[t], first + at], a_vm.at[at, t], a_sem.at[at, t])
            copies.append((holders[t] == col_id, copy))
    for when, copy in copies:
        pl.when(when)(copy.start)
    for t in range(STEPS):
        hop = jnp.where(holders[t] < col_id, col_id - 1, last - 1 - col_id)
        for h in range(hops):

            @pl.when((holders[t] != col_id) & (hop == h))
            def _():
                for at in range(count):

                    def one_block(m, carry):
                        part = pl.ds(pl.multiple_of(m * blk, blk), blk)
                        a_vm[at, t, part] = arrived[at][h][t, part]
                        return carry

                    lax.fori_loop(0, nz, one_block, 0)

    for when, copy in copies:
        pl.when(when)(copy.wait)

    lane = lax.broadcasted_iota(jnp.int32, (blk, blk), 1)
    sub = lax.broadcasted_iota(jnp.int32, (blk, blk), 0)
    flat = [b.reshape(b.shape[0] * b.shape[1], blk, blk) for b in (b0, b1)]

    def one_row(at, carry):
        i = first + at
        for t in range(STEPS):
            for m in range(nz):
                q = t * nz + m
                left_vm[:, q * blk : (q + 1) * blk] = jnp.where(
                    lane < plan[i, kept * width + q],
                    a_vm[at, t, m * blk : (m + 1) * blk],
                    jnp.zeros((), a_vm.dtype),
                )
        row_size = plan[i, kept * width + width]

        for p in range(kept // 2):
            sides = []
            for e in range(2):
                parts = []
                for q in range(width):
                    n = plan[i, (2 * p + e) * width + q]
                    block = flat[q // nz][jnp.maximum(n, 0)]
                    parts.append(jnp.where(n >= 0, block, jnp.zeros((), block.dtype)))
                sides.append(jnp.concatenate(parts, axis=0))
            total = jnp.dot(
                left_vm[...], jnp.concatenate(sides, axis=1), preferred_element_type=jnp.float32
            )
            for e in range(2):
                col_size = plan[i, kept * width + width + 1 + 2 * p + e]
                inside = (sub < row_size) & (lane < col_size)
                part = total[:, e * blk : (e + 1) * blk]
                o_vm[at, 2 * p + e] = jnp.where(inside, part, 0.0).astype(o_vm.dtype)
        pltpu.make_async_copy(o_vm.at[at], out.at[i], o_sem.at[at]).start()
        return carry

    lax.fori_loop(0, count, one_row, 0)
    for at in range(count):
        pltpu.make_async_copy(o_vm.at[at], out.at[first + at], o_sem.at[at]).wait()


def multiply_rows(first, count, owner, plan, b_panels, own, arrived, kept, so_far):
    rows, size, blk = own.shape[1:]
    nz, hops = size // blk, len(arrived[0])
    operands = [owner, plan, *b_panels, own]
    for at in range(count):
        operands += arrived[at]
    specs = [SMEM] * 2 + [VMEM] * 2 + [ANYWHERE] + [VMEM] * (count * hops)
    aliases = {}
    if so_far is not None:
        aliases = {len(operands): 0}
        operands.append(so_far)
        specs.append(ANYWHERE)
    flops = 2 * count * blk * blk * blk * STEPS * nz * kept
    limit = (12 + count * hops // 2) * MIB
    return pl.pallas_call(
        functools.partial(rows_kernel, first, count, hops),
        out_shape=jax.ShapeDtypeStruct((rows, kept, blk, blk), jnp.bfloat16),
        in_specs=specs,
        out_specs=ANYWHERE,
        scratch_shapes=[
            pltpu.VMEM((count, STEPS, size, blk), jnp.bfloat16),
            pltpu.VMEM((blk, STEPS * size), jnp.bfloat16),
            pltpu.VMEM((count, kept, blk, blk), jnp.bfloat16),
            pltpu.SemaphoreType.DMA((count, STEPS)),
            pltpu.SemaphoreType.DMA((count,)),
        ],
        input_output_aliases=aliases,
        compiler_params=pltpu.CompilerParams(vmem_limit_bytes=limit),
        cost_estimate=pl.CostEstimate(flops=flops, bytes_accessed=4 * MIB, transcendentals=0),
        name="multiply_rows",
    )(*operands)


def local(a_vals, a_cols, b_vals, b_cols, c_cols, panel_owner, atom_size):
    row_count = lax.axis_size("row")
    col_count = lax.axis_size("col")
    stored_b, stored_bc = b_vals[0, 0], b_cols[0, 0]
    targets = c_cols[0, 0]
    slot_count, rows, nz, blk = a_vals.shape[2:6]
    own_a = a_vals.reshape(slot_count, rows, nz * blk, blk)
    notes = jnp.pad(
        a_cols[0, 0].astype(own_a.dtype), ((0, 0), (0, NOTE - rows), (0, blk - nz))
    )
    hops = col_count - 1
    from_next = [((i + 1) % row_count, i) for i in range(row_count)]

    arrived = [[None] * hops for _ in range(rows)]
    newest = plan = moved_b = moved_bc = None
    edges = {}
    last_slot = rows + lag_of(hops - 1, hops) - 1
    plan_slot = max(rows, NOTED + lag_of(hops - 1, hops) + 1)
    for slot in range(last_slot + 1):
        for lane in range((hops + 1) // 2):
            roles = []
            for hop in sorted({lane, hops - 1 - lane}):
                row = slot - lag_of(hop, hops)
                if 0 <= row < rows:
                    roles.append((row, hop))
            if not roles:
                continue
            after = [newest] if slot > 1 else []
            if slot == 1 and lane == 1:
                after.append(moved_bc)
            before = slot - 1 if slot == rows + 1 else slot - 2
            if lane == 0 and before > 0 and before in edges:
                after.append(edges[before])
            if slot == plan_slot and lane == 0:
                plan = make_plan(
                    panel_owner, atom_size, stored_bc, moved_bc, targets, notes, arrived[NOTED], nz, newest
                )
                after.append(plan)
            arrivals = [arrived[row][hop - 1] if hop else None for row, hop in roles]
            limit = 62 * MIB if newest is None else 4 * MIB
            newest = relay(panel_owner, own_a, notes, roles, arrivals, after, limit, f"lane{lane}_{slot}")
            if slot == 0 and lane == 0:
                behind_bc, newest = lax.optimization_barrier((stored_bc, newest))
                moved_bc = lax.ppermute(behind_bc, "row", from_next)
            if slot == lane == 1:
                behind_b, newest = lax.optimization_barrier((stored_b, newest))
                moved_b = lax.ppermute(behind_b, "row", from_next)
            route = []
            for _, hop in roles:
                route += [(hop, hop + 1), (hops - hop, hops - hop - 1)]
            got = lax.ppermute(newest, "col", route)
            for row, hop in roles:
                arrived[row][hop] = got
            if lane == 0:
                edges[slot] = got

    result = None
    for first, count in ((0, rows - 1), (rows - 1, 1)):
        result = multiply_rows(
            first,
            count,
            panel_owner,
            plan,
            (stored_b, moved_b),
            own_a,
            arrived[first : first + count],
            targets.shape[1],
            result,
        )
    return result[None, None]


def solution(mesh):
    placed = (
        P("row", "col", None, None, None, None, None),
        P("row", "col", None, None, None),
        P("row", "col", None, None, None, None),
        P("row", "col", None, None),
        P("row", "col", None, None),
        P(),
        P(),
    )
    return jax.shard_map(
        local,
        mesh=mesh,
        in_specs=placed,
        out_specs=P("row", "col", None, None, None, None),
        check_vma=False,
    )
```

```python
import functools

import jax
import jax.numpy as jnp
from jax import lax
from jax.experimental import pallas as pl
from jax.experimental.pallas import tpu as pltpu
from jax.sharding import PartitionSpec as P

STEPS = 2
NOTED = 1
NOTE = 16
MIB = 1024 * 1024

SMEM = pl.BlockSpec(memory_space=pltpu.SMEM)
VMEM = pl.BlockSpec(memory_space=pltpu.VMEM)
ANYWHERE = pl.BlockSpec(memory_space=pl.ANY)


def places_of(owner_ref):
    row_id, row_count = lax.axis_index("row"), lax.axis_size("row")
    panels = [lax.rem(row_id + t, row_count) for t in range(STEPS)]
    places = [owner_ref[row_id, k] for k in panels]
    return panels, [lax.div(p, 2) for p in places], [lax.rem(p, 2) for p in places]


def lag_of(hop, hops):
    return hop + (2 * hop >= hops)


def relay_kernel(roles, waits, owner, own, *refs):
    refs = list(refs)
    notes = refs.pop(0) if any(row == NOTED for row, _, _ in roles) else None
    arrivals = [refs.pop(0) if arrives else None for _, _, arrives in roles]
    del refs[:waits]
    onward, sem = refs
    _, holders, slots = places_of(owner)
    col_id, last = lax.axis_index("col"), lax.axis_size("col") - 1
    size = own.shape[2]
    jobs = []
    for place, ((row, hop, _), arrived) in enumerate(zip(roles, arrivals)):
        sends = (col_id == hop) | (col_id == last - hop)
        for t in range(STEPS):
            mine = sends if hop == 0 else sends & (holders[t] == col_id)
            dst = onward.at[t, pl.ds(0, size)]
            jobs.append((mine, pltpu.make_async_copy(own.at[slots[t], row], dst, sem.at[place, t])))
            if row == NOTED:
                dst = onward.at[t, pl.ds(size, NOTE)]
                jobs.append((mine, pltpu.make_async_copy(notes.at[slots[t]], dst, sem.at[place, STEPS + t])))
    for when, copy in jobs:
        pl.when(when)(copy.start)
    for (row, hop, _), arrived in zip(roles, arrivals):
        if arrived is None:
            continue
        sends = (col_id == hop) | (col_id == last - hop)
        extent = size + (NOTE if row == NOTED else 0)
        for t in range(STEPS):

            @pl.when(sends & (holders[t] != col_id))
            def _():
                onward[t, :extent] = arrived[t, :extent]

    for when, copy in jobs:
        pl.when(when)(copy.wait)


def relay(owner, own, notes, roles, arrivals, after, limit, flops, name):
    noted = any(row == NOTED for row, _ in roles)
    size = own.shape[2] + (NOTE if noted else 0)
    given = [a for a in arrivals if a is not None]
    operands = [owner, own] + [notes] * noted + given + after
    specs = [SMEM, ANYWHERE] + [ANYWHERE] * noted + [VMEM] * len(given) + [ANYWHERE] * len(after)
    roles = tuple((row, hop, a is not None) for (row, hop), a in zip(roles, arrivals))
    return pl.pallas_call(
        functools.partial(relay_kernel, roles, len(after)),
        out_shape=jax.ShapeDtypeStruct((STEPS, size, own.shape[3]), own.dtype),
        in_specs=specs,
        out_specs=VMEM,
        scratch_shapes=[pltpu.SemaphoreType.DMA((2, 2 * STEPS))],
        compiler_params=pltpu.CompilerParams(vmem_limit_bytes=limit),
        cost_estimate=pl.CostEstimate(flops=flops, bytes_accessed=1024, transcendentals=0),
        name=name,
    )(*operands)


def plan_kernel(nz, owner, atoms, bcols0, bcols1, ccols, notes, *refs):
    arrivals, (plan, note_vm, ccols_vm) = refs[:-4], refs[-3:]
    panels, holders, slots = places_of(owner)
    row_id, col_id, col_count = lax.axis_index("row"), lax.axis_index("col"), lax.axis_size("col")
    panel_rows, nzb = bcols0.shape
    rows, kept = ccols.shape
    lanes = plan.shape[1]
    width = STEPS * nz
    sizes_at, row_at = kept * width, (kept + 1) * width
    for t in range(STEPS):
        hop = jnp.where(holders[t] < col_id, col_id - 1, col_count - 2 - col_id)
        mine = holders[t] == col_id

        @pl.when(mine)
        def _():
            note_vm[t] = notes[slots[t]]

        for h, arrived in enumerate(arrivals):

            @pl.when(jnp.logical_not(mine) & (hop == h))
            def _():
                note_vm[t] = arrived[t, arrived.shape[1] - NOTE :]

    ccols_vm[...] = jnp.zeros_like(ccols_vm)
    ccols_vm[:rows, :kept] = ccols[...].astype(jnp.float32)

    source = lax.broadcasted_iota(jnp.int32, (lanes, lanes), 0)
    target = lax.broadcasted_iota(jnp.int32, (lanes, lanes), 1)

    def spread(values, hits):
        return jnp.dot(values, hits.astype(jnp.float32).astype(jnp.bfloat16), preferred_element_type=jnp.float32)

    lane = lax.broadcasted_iota(jnp.int32, plan.shape, 1)
    line = lax.broadcasted_iota(jnp.int32, plan.shape, 0)
    inner = jnp.zeros(plan.shape, jnp.float32)
    second = jnp.zeros(plan.shape, jnp.bool_)
    for t in range(STEPS):
        hits = source < 0
        for e in range(kept + 1):
            at = e * width + t * nz
            hits = hits | (target == source + at)
            if t:
                second = second | ((lane >= at) & (lane < at + nz))
        inner = inner + spread(note_vm[t], hits & (source < nz))
    inner = inner.astype(jnp.int32) + jnp.where(second, panel_rows, 0)
    hits = target == source + row_at + 1
    for e in range(kept):
        hits = hits | ((source == e) & (target >= e * width) & (target < (e + 1) * width))
    column = spread(ccols_vm[...].astype(jnp.bfloat16), hits & (source < kept)).astype(jnp.int32)

    block = jnp.full(plan.shape, -1, jnp.int32)
    size = jnp.zeros(plan.shape, jnp.int32)
    for t, bcols in enumerate((bcols0, bcols1)):
        for j in range(panel_rows):
            here = inner == t * panel_rows + j
            size = jnp.where(here, atoms[panels[t] * panel_rows + j], size)
            for n in range(nzb):
                block = jnp.where(here & (column == bcols[j, n]), j * nzb + n, block)
    col_size = jnp.zeros(plan.shape, jnp.int32)
    for c in range(2 * rows):
        col_size = jnp.where(column == c, atoms[col_id * 2 * rows + c], col_size)
    row_size = jnp.zeros(plan.shape, jnp.int32)
    for i in range(rows):
        row_size = jnp.where(line == i, atoms[row_id * panel_rows + i], row_size)
    tail = jnp.where(lane == row_at, row_size, col_size)
    plan[...] = jnp.where(lane < sizes_at, block, jnp.where(lane < row_at, size, tail))


def make_plan(owner, atoms, bcols0, bcols1, ccols, notes, arrivals, nz, after):
    operands = [owner, atoms, bcols0, bcols1, ccols, notes, *arrivals, after]
    return pl.pallas_call(
        functools.partial(plan_kernel, nz),
        out_shape=jax.ShapeDtypeStruct(notes.shape[1:], jnp.int32),
        in_specs=[SMEM] * 4 + [VMEM] * (2 + len(arrivals)) + [ANYWHERE],
        out_specs=VMEM,
        scratch_shapes=[pltpu.VMEM(notes.shape, notes.dtype), pltpu.VMEM(notes.shape[1:], jnp.float32)],
        compiler_params=pltpu.CompilerParams(vmem_limit_bytes=8 * MIB),
        cost_estimate=pl.CostEstimate(flops=10**9, bytes_accessed=1024, transcendentals=0),
        name="make_plan",
    )(*operands)


def rows_kernel(first, count, hops, owner, plan, b0, b1, own, *refs):
    arrived = [refs[at * hops : (at + 1) * hops] for at in range(count)]
    out, a_vm, left_vm, o_vm, a_sem, o_sem = refs[-6:]
    kept, blk = o_vm.shape[1], o_vm.shape[-1]
    size = a_vm.shape[2]
    nz = size // blk
    width = STEPS * nz
    col_id, last = lax.axis_index("col"), lax.axis_size("col") - 1
    _, holders, slots = places_of(owner)
    copies = []
    for at in range(count):
        for t in range(STEPS):
            copy = pltpu.make_async_copy(own.at[slots[t], first + at], a_vm.at[at, t], a_sem.at[at, t])
            copies.append((holders[t] == col_id, copy))
    for when, copy in copies:
        pl.when(when)(copy.start)
    for t in range(STEPS):
        hop = jnp.where(holders[t] < col_id, col_id - 1, last - 1 - col_id)
        for h in range(hops):

            @pl.when((holders[t] != col_id) & (hop == h))
            def _():
                for at in range(count):

                    def one_block(m, carry):
                        part = pl.ds(pl.multiple_of(m * blk, blk), blk)
                        a_vm[at, t, part] = arrived[at][h][t, part]
                        return carry

                    lax.fori_loop(0, nz, one_block, 0)

    for when, copy in copies:
        pl.when(when)(copy.wait)

    lane = lax.broadcasted_iota(jnp.int32, (blk, blk), 1)
    sub = lax.broadcasted_iota(jnp.int32, (blk, blk), 0)
    flat = [b.reshape(b.shape[0] * b.shape[1], blk, blk) for b in (b0, b1)]

    def one_row(at, carry):
        i = first + at
        for t in range(STEPS):
            for m in range(nz):
                q = t * nz + m
                left_vm[:, q * blk : (q + 1) * blk] = jnp.where(
                    lane < plan[i, kept * width + q],
                    a_vm[at, t, m * blk : (m + 1) * blk],
                    jnp.zeros((), a_vm.dtype),
                )
        row_size = plan[i, kept * width + width]

        for p in range(kept // 2):
            sides = []
            for e in range(2):
                parts = []
                for q in range(width):
                    n = plan[i, (2 * p + e) * width + q]
                    block = flat[q // nz][jnp.maximum(n, 0)]
                    parts.append(jnp.where(n >= 0, block, jnp.zeros((), block.dtype)))
                sides.append(jnp.concatenate(parts, axis=0))
            total = jnp.dot(
                left_vm[...], jnp.concatenate(sides, axis=1), preferred_element_type=jnp.float32
            )
            for e in range(2):
                col_size = plan[i, kept * width + width + 1 + 2 * p + e]
                inside = (sub < row_size) & (lane < col_size)
                part = total[:, e * blk : (e + 1) * blk]
                o_vm[at, 2 * p + e] = jnp.where(inside, part, 0.0).astype(o_vm.dtype)
        pltpu.make_async_copy(o_vm.at[at], out.at[i], o_sem.at[at]).start()
        return carry

    lax.fori_loop(0, count, one_row, 0)
    for at in range(count):
        pltpu.make_async_copy(o_vm.at[at], out.at[first + at], o_sem.at[at]).wait()


def multiply_rows(first, count, owner, plan, b_panels, own, arrived, kept, so_far):
    rows, size, blk = own.shape[1:]
    nz, hops = size // blk, len(arrived[0])
    operands = [owner, plan, *b_panels, own]
    for at in range(count):
        operands += arrived[at]
    specs = [SMEM] * 2 + [VMEM] * 2 + [ANYWHERE] + [VMEM] * (count * hops)
    aliases = {}
    if so_far is not None:
        aliases = {len(operands): 0}
        operands.append(so_far)
        specs.append(ANYWHERE)
    flops = 2 * count * blk * blk * blk * STEPS * nz * kept
    limit = (12 + count * hops // 2) * MIB
    return pl.pallas_call(
        functools.partial(rows_kernel, first, count, hops),
        out_shape=jax.ShapeDtypeStruct((rows, kept, blk, blk), jnp.bfloat16),
        in_specs=specs,
        out_specs=ANYWHERE,
        scratch_shapes=[
            pltpu.VMEM((count, STEPS, size, blk), jnp.bfloat16),
            pltpu.VMEM((blk, STEPS * size), jnp.bfloat16),
            pltpu.VMEM((count, kept, blk, blk), jnp.bfloat16),
            pltpu.SemaphoreType.DMA((count, STEPS)),
            pltpu.SemaphoreType.DMA((count,)),
        ],
        input_output_aliases=aliases,
        compiler_params=pltpu.CompilerParams(vmem_limit_bytes=limit),
        cost_estimate=pl.CostEstimate(flops=flops, bytes_accessed=4 * MIB, transcendentals=0),
        name="multiply_rows",
    )(*operands)


def local(a_vals, a_cols, b_vals, b_cols, c_cols, panel_owner, atom_size):
    row_count = lax.axis_size("row")
    col_count = lax.axis_size("col")
    stored_b, stored_bc = b_vals[0, 0], b_cols[0, 0]
    targets = c_cols[0, 0]
    slot_count, rows, nz, blk = a_vals.shape[2:6]
    own_a = a_vals.reshape(slot_count, rows, nz * blk, blk)
    notes = jnp.pad(
        a_cols[0, 0].astype(own_a.dtype), ((0, 0), (0, NOTE - rows), (0, blk - nz))
    )
    hops = col_count - 1
    from_next = [((i + 1) % row_count, i) for i in range(row_count)]

    arrived = [[None] * hops for _ in range(rows)]
    newest = plan = moved_b = moved_bc = None
    edges = {}
    last_slot = rows + lag_of(hops - 1, hops) - 1
    plan_slot = max(rows, NOTED + lag_of(hops - 1, hops) + 1)
    for slot in range(last_slot + 1):
        for lane in range((hops + 1) // 2):
            roles = []
            for hop in sorted({lane, hops - 1 - lane}):
                row = slot - lag_of(hop, hops)
                if 0 <= row < rows:
                    roles.append((row, hop))
            if not roles:
                continue
            after = [newest] if slot > 1 else []
            if slot == 1 and lane == 0:
                after.append(moved_bc)
            before = slot - 2
            if lane == 0 and before > 0 and before in edges:
                after.append(edges[before])
            if slot == plan_slot and lane == 0:
                plan = make_plan(
                    panel_owner, atom_size, stored_bc, moved_bc[0, 0], targets, notes, arrived[NOTED], nz, newest
                )
                after.append(plan)
            arrivals = [arrived[row][hop - 1] if hop else None for row, hop in roles]
            flops = (2 if lane == 0 and slot == rows + 1 else 1) * 10**9
            limit = 62 * MIB if newest is None else 4 * MIB
            newest = relay(panel_owner, own_a, notes, roles, arrivals, after, limit, flops, f"lane{lane}_{slot}")
            if slot == 0 and lane == 0:
                behind_bc, newest = lax.optimization_barrier((b_cols, newest))
                moved_bc = lax.ppermute(behind_bc, "row", from_next)
            if slot == lane == 1:
                behind_b, newest = lax.optimization_barrier((stored_b, newest))
                moved_b = lax.ppermute(behind_b, "row", from_next)
            route = []
            for _, hop in roles:
                route += [(hop, hop + 1), (hops - hop, hops - hop - 1)]
            got = lax.ppermute(newest, "col", route)
            for row, hop in roles:
                arrived[row][hop] = got
            if lane == 0:
                edges[slot] = got

    result = None
    for first, count in ((0, rows - 2), (rows - 2, 2)):
        result = multiply_rows(
            first,
            count,
            panel_owner,
            plan,
            (stored_b, moved_b),
            own_a,
            arrived[first : first + count],
            targets.shape[1],
            result,
        )
    return result[None, None]


def solution(mesh):
    placed = (
        P("row", "col", None, None, None, None, None),
        P("row", "col", None, None, None),
        P("row", "col", None, None, None, None),
        P("row", "col", None, None),
        P("row", "col", None, None),
        P(),
        P(),
    )
    return jax.shard_map(
        local,
        mesh=mesh,
        in_specs=placed,
        out_specs=P("row", "col", None, None, None, None),
        check_vma=False,
    )
```

```python
import functools

import jax
import jax.numpy as jnp
from jax import lax
from jax.experimental import pallas as pl
from jax.experimental.pallas import tpu as pltpu
from jax.sharding import PartitionSpec as P

STEPS = 2
PIECES = 8
NOTED = 1
NOTE = 16
STRIDE = 64
MIB = 1024 * 1024

SMEM = pl.BlockSpec(memory_space=pltpu.SMEM)
VMEM = pl.BlockSpec(memory_space=pltpu.VMEM)
ANYWHERE = pl.BlockSpec(memory_space=pl.ANY)


def places_of(owner_ref):
    row_id, row_count = lax.axis_index("row"), lax.axis_size("row")
    panels = [lax.rem(row_id + t, row_count) for t in range(STEPS)]
    places = [owner_ref[row_id, k] for k in panels]
    return panels, [lax.div(p, 2) for p in places], [lax.rem(p, 2) for p in places]


def lag_of(hop, hops):
    return hop + (2 * hop >= hops)


def cut(rows, size):
    lines = STEPS * rows * size // PIECES
    pieces = []
    for piece in range(PIECES):
        segments, at = [], piece * lines
        while at < (piece + 1) * lines:
            unit, first = divmod(at, size)
            count = min(size - first, (piece + 1) * lines - at)
            segments.append((unit % STEPS, unit // STEPS, first, count, at - piece * lines))
            at += count
        if piece == NOTED:
            segments += [(t, -1, 0, NOTE, lines + t * NOTE) for t in range(STEPS)]
        pieces.append(tuple(segments))
    return pieces


def extent_of(segments):
    return max(offset + count for _, _, _, count, offset in segments)


def relay_kernel(roles, waits, owner, own, *refs):
    refs = list(refs)
    notes = refs.pop(0) if any(i < 0 for segments, _, _ in roles for _, i, _, _, _ in segments) else None
    arrivals = [refs.pop(0) if arrives else None for _, _, arrives in roles]
    del refs[:waits]
    onward, sem = refs
    _, holders, slots = places_of(owner)
    col_id, last = lax.axis_index("col"), lax.axis_size("col") - 1
    jobs = []
    for place, (segments, hop, _) in enumerate(roles):
        sends = (col_id == hop) | (col_id == last - hop)
        for n, (t, i, first, count, offset) in enumerate(segments):
            mine = sends if hop == 0 else sends & (holders[t] == col_id)
            src = notes.at[slots[t]] if i < 0 else own.at[slots[t], i, pl.ds(first, count)]
            jobs.append((mine, pltpu.make_async_copy(src, onward.at[pl.ds(offset, count)], sem.at[place, n])))
    for when, copy in jobs:
        pl.when(when)(copy.start)
    for (segments, hop, _), arrived in zip(roles, arrivals):
        if arrived is None:
            continue
        sends = (col_id == hop) | (col_id == last - hop)
        for t, _, _, count, offset in segments:

            @pl.when(sends & (holders[t] != col_id))
            def _():
                onward[offset : offset + count] = arrived[offset : offset + count]

    for when, copy in jobs:
        pl.when(when)(copy.wait)


def relay(owner, own, notes, roles, arrivals, after, limit, flops, name):
    noted = any(i < 0 for segments, _ in roles for _, i, _, _, _ in segments)
    size = max(extent_of(segments) for segments, _ in roles)
    given = [a for a in arrivals if a is not None]
    operands = [owner, own] + [notes] * noted + given + after
    specs = [SMEM, ANYWHERE] + [ANYWHERE] * noted + [VMEM] * len(given) + [ANYWHERE] * len(after)
    roles = tuple((segments, hop, a is not None) for (segments, hop), a in zip(roles, arrivals))
    return pl.pallas_call(
        functools.partial(relay_kernel, roles, len(after)),
        out_shape=jax.ShapeDtypeStruct((size, own.shape[3]), own.dtype),
        in_specs=specs,
        out_specs=VMEM,
        scratch_shapes=[pltpu.SemaphoreType.DMA((2, max(len(segments) for segments, _, _ in roles)))],
        compiler_params=pltpu.CompilerParams(vmem_limit_bytes=limit),
        cost_estimate=pl.CostEstimate(flops=flops, bytes_accessed=1024, transcendentals=0),
        name=name,
    )(*operands)


def plan_kernel(nz, spots, owner, atoms, bcols0, bcols1, ccols, notes, *refs):
    arrivals, (plan, note_vm, ccols_vm) = refs[:-4], refs[-3:]
    panels, holders, slots = places_of(owner)
    row_id, col_id, col_count = lax.axis_index("row"), lax.axis_index("col"), lax.axis_size("col")
    panel_rows, nzb = bcols0.shape
    rows, kept = ccols.shape
    lanes = plan.shape[1]
    width = STEPS * nz
    sizes_at, row_at = kept * width, (kept + 1) * width
    for t in range(STEPS):
        hop = jnp.where(holders[t] < col_id, col_id - 1, col_count - 2 - col_id)
        mine = holders[t] == col_id

        @pl.when(mine)
        def _():
            note_vm[t] = notes[slots[t]]

        for h, arrived in enumerate(arrivals):

            @pl.when(jnp.logical_not(mine) & (hop == h))
            def _():
                note_vm[t] = arrived[spots[t] : spots[t] + NOTE]

    ccols_vm[...] = jnp.zeros_like(ccols_vm)
    ccols_vm[:rows, :kept] = ccols[...].astype(jnp.float32)

    source = lax.broadcasted_iota(jnp.int32, (lanes, lanes), 0)
    target = lax.broadcasted_iota(jnp.int32, (lanes, lanes), 1)

    def spread(values, hits):
        return jnp.dot(values, hits.astype(jnp.float32).astype(jnp.bfloat16), preferred_element_type=jnp.float32)

    lane = lax.broadcasted_iota(jnp.int32, plan.shape, 1)
    line = lax.broadcasted_iota(jnp.int32, plan.shape, 0)
    inner = jnp.zeros(plan.shape, jnp.float32)
    second = jnp.zeros(plan.shape, jnp.bool_)
    for t in range(STEPS):
        hits = source < 0
        for e in range(kept + 1):
            at = e * width + t * nz
            hits = hits | (target == source + at)
            if t:
                second = second | ((lane >= at) & (lane < at + nz))
        inner = inner + spread(note_vm[t], hits & (source < nz))
    inner = inner.astype(jnp.int32) + jnp.where(second, panel_rows, 0)
    hits = target == source + row_at + 1
    for e in range(kept):
        hits = hits | ((source == e) & (target >= e * width) & (target < (e + 1) * width))
    column = spread(ccols_vm[...].astype(jnp.bfloat16), hits & (source < kept)).astype(jnp.int32)

    block = jnp.full(plan.shape, -1, jnp.int32)
    size = jnp.zeros(plan.shape, jnp.int32)
    for t, bcols in enumerate((bcols0, bcols1)):
        for j in range(panel_rows):
            here = inner == t * panel_rows + j
            size = jnp.where(here, atoms[panels[t] * panel_rows + j], size)
            for n in range(nzb):
                block = jnp.where(here & (column == bcols[j, n]), j * nzb + n, block)
    col_size = jnp.zeros(plan.shape, jnp.int32)
    for c in range(2 * rows):
        col_size = jnp.where(column == c, atoms[col_id * 2 * rows + c], col_size)
    row_size = jnp.zeros(plan.shape, jnp.int32)
    for i in range(rows):
        row_size = jnp.where(line == i, atoms[row_id * panel_rows + i], row_size)
    tail = jnp.where(lane == row_at, row_size, col_size)
    plan[...] = jnp.where(lane < sizes_at, block, jnp.where(lane < row_at, size, tail))


def make_plan(owner, atoms, bcols0, bcols1, ccols, notes, arrivals, nz, spots, after):
    operands = [owner, atoms, bcols0, bcols1, ccols, notes, *arrivals, after]
    return pl.pallas_call(
        functools.partial(plan_kernel, nz, spots),
        out_shape=jax.ShapeDtypeStruct(notes.shape[1:], jnp.int32),
        in_specs=[SMEM] * 4 + [VMEM] * (2 + len(arrivals)) + [ANYWHERE],
        out_specs=VMEM,
        scratch_shapes=[pltpu.VMEM(notes.shape, notes.dtype), pltpu.VMEM(notes.shape[1:], jnp.float32)],
        compiler_params=pltpu.CompilerParams(vmem_limit_bytes=8 * MIB),
        cost_estimate=pl.CostEstimate(flops=10**9, bytes_accessed=1024, transcendentals=0),
        name="make_plan",
    )(*operands)


def rows_kernel(first, count, hops, sources, owner, plan, b0, b1, own, *refs):
    places = 1 + max(source[0] for source in sources)
    arrived = [refs[at * hops : (at + 1) * hops] for at in range(places)]
    out, a_vm, left_vm, o_vm, a_sem, o_sem = refs[-6:]
    kept, blk = o_vm.shape[1], o_vm.shape[-1]
    size = a_vm.shape[2]
    nz = size // blk
    width = STEPS * nz
    col_id, last = lax.axis_index("col"), lax.axis_size("col") - 1
    _, holders, slots = places_of(owner)
    copies = []
    for at in range(count):
        for t in range(STEPS):
            copy = pltpu.make_async_copy(own.at[slots[t], first + at], a_vm.at[at, t], a_sem.at[at, t])
            copies.append((holders[t] == col_id, copy))
    for when, copy in copies:
        pl.when(when)(copy.start)
    for t in range(STEPS):
        hop = jnp.where(holders[t] < col_id, col_id - 1, last - 1 - col_id)
        for h in range(hops):

            @pl.when((holders[t] != col_id) & (hop == h))
            def _():
                for place, step, i, start, lines, offset in sources:
                    if step != t:
                        continue

                    def one_stride(n, carry):
                        src = pl.ds(pl.multiple_of(offset + n * STRIDE, STRIDE), STRIDE)
                        dst = pl.ds(pl.multiple_of(start + n * STRIDE, STRIDE), STRIDE)
                        a_vm[i - first, t, dst] = arrived[place][h][src]
                        return carry

                    lax.fori_loop(0, lines // STRIDE, one_stride, 0)

    for when, copy in copies:
        pl.when(when)(copy.wait)

    lane = lax.broadcasted_iota(jnp.int32, (blk, blk), 1)
    sub = lax.broadcasted_iota(jnp.int32, (blk, blk), 0)
    flat = [b.reshape(b.shape[0] * b.shape[1], blk, blk) for b in (b0, b1)]

    def one_row(at, carry):
        i = first + at
        for t in range(STEPS):
            for m in range(nz):
                q = t * nz + m
                left_vm[:, q * blk : (q + 1) * blk] = jnp.where(
                    lane < plan[i, kept * width + q],
                    a_vm[at, t, m * blk : (m + 1) * blk],
                    jnp.zeros((), a_vm.dtype),
                )
        row_size = plan[i, kept * width + width]

        for p in range(kept // 2):
            sides = []
            for e in range(2):
                parts = []
                for q in range(width):
                    n = plan[i, (2 * p + e) * width + q]
                    block = flat[q // nz][jnp.maximum(n, 0)]
                    parts.append(jnp.where(n >= 0, block, jnp.zeros((), block.dtype)))
                sides.append(jnp.concatenate(parts, axis=0))
            total = jnp.dot(
                left_vm[...], jnp.concatenate(sides, axis=1), preferred_element_type=jnp.float32
            )
            for e in range(2):
                col_size = plan[i, kept * width + width + 1 + 2 * p + e]
                inside = (sub < row_size) & (lane < col_size)
                part = total[:, e * blk : (e + 1) * blk]
                o_vm[at, 2 * p + e] = jnp.where(inside, part, 0.0).astype(o_vm.dtype)
        pltpu.make_async_copy(o_vm.at[at], out.at[i], o_sem.at[at]).start()
        return carry

    lax.fori_loop(0, count, one_row, 0)
    for at in range(count):
        pltpu.make_async_copy(o_vm.at[at], out.at[first + at], o_sem.at[at]).wait()


def multiply_rows(first, count, owner, plan, b_panels, own, pieces, arrived, kept, so_far):
    rows, size, blk = own.shape[1:]
    nz, hops = size // blk, len(arrived[0])
    operands = [owner, plan, *b_panels, own]
    sources, places = [], 0
    for piece, segments in enumerate(pieces):
        found = [segment for segment in segments if first <= segment[1] < first + count]
        if found:
            sources += [(places, *segment) for segment in found]
            operands += arrived[piece]
            places += 1
    specs = [SMEM] * 2 + [VMEM] * 2 + [ANYWHERE] + [VMEM] * (places * hops)
    aliases = {}
    if so_far is not None:
        aliases = {len(operands): 0}
        operands.append(so_far)
        specs.append(ANYWHERE)
    flops = 2 * count * blk * blk * blk * STEPS * nz * kept
    limit = (12 + places * hops // 2) * MIB
    return pl.pallas_call(
        functools.partial(rows_kernel, first, count, hops, tuple(sources)),
        out_shape=jax.ShapeDtypeStruct((rows, kept, blk, blk), jnp.bfloat16),
        in_specs=specs,
        out_specs=ANYWHERE,
        scratch_shapes=[
            pltpu.VMEM((count, STEPS, size, blk), jnp.bfloat16),
            pltpu.VMEM((blk, STEPS * size), jnp.bfloat16),
            pltpu.VMEM((count, kept, blk, blk), jnp.bfloat16),
            pltpu.SemaphoreType.DMA((count, STEPS)),
            pltpu.SemaphoreType.DMA((count,)),
        ],
        input_output_aliases=aliases,
        compiler_params=pltpu.CompilerParams(vmem_limit_bytes=limit),
        cost_estimate=pl.CostEstimate(flops=flops, bytes_accessed=4 * MIB, transcendentals=0),
        name="multiply_rows",
    )(*operands)


def local(a_vals, a_cols, b_vals, b_cols, c_cols, panel_owner, atom_size):
    row_count = lax.axis_size("row")
    col_count = lax.axis_size("col")
    stored_b, stored_bc = b_vals[0, 0], b_cols[0, 0]
    targets = c_cols[0, 0]
    slot_count, rows, nz, blk = a_vals.shape[2:6]
    own_a = a_vals.reshape(slot_count, rows, nz * blk, blk)
    notes = jnp.pad(
        a_cols[0, 0].astype(own_a.dtype), ((0, 0), (0, NOTE - rows), (0, blk - nz))
    )
    hops = col_count - 1
    from_next = [((i + 1) % row_count, i) for i in range(row_count)]

    pieces = cut(rows, nz * blk)
    spots = tuple(offset for _, i, _, _, offset in pieces[NOTED] if i < 0)
    arrived = [[None] * hops for _ in pieces]
    newest = plan = moved_b = moved_bc = None
    edges = {}
    last_slot = PIECES + lag_of(hops - 1, hops) - 1
    plan_slot = max(PIECES, NOTED + lag_of(hops - 1, hops) + 1)
    for slot in range(last_slot + 1):
        for lane in range((hops + 1) // 2):
            roles = []
            for hop in sorted({lane, hops - 1 - lane}):
                piece = slot - lag_of(hop, hops)
                if 0 <= piece < PIECES:
                    roles.append((piece, hop))
            if not roles:
                continue
            after = [newest] if slot > 1 else []
            if slot == 1 and lane == 0:
                after.append(moved_bc)
            before = slot - 2
            if lane == 0 and before > 0 and before in edges:
                after.append(edges[before])
            if slot == plan_slot and lane == 0:
                plan = make_plan(
                    panel_owner, atom_size, stored_bc, moved_bc[0, 0], targets, notes, arrived[NOTED], nz, spots, newest
                )
                after.append(plan)
            arrivals = [arrived[piece][hop - 1] if hop else None for piece, hop in roles]
            sent = [(pieces[piece], hop) for piece, hop in roles]
            flops = (2 if lane == 0 and slot == PIECES + 1 else 1) * 10**9
            limit = 62 * MIB if newest is None else 4 * MIB
            newest = relay(panel_owner, own_a, notes, sent, arrivals, after, limit, flops, f"lane{lane}_{slot}")
            if slot == 0 and lane == 0:
                behind_bc, newest = lax.optimization_barrier((b_cols, newest))
                moved_bc = lax.ppermute(behind_bc, "row", from_next)
            if slot == lane == 1:
                behind_b, newest = lax.optimization_barrier((stored_b, newest))
                moved_b = lax.ppermute(behind_b, "row", from_next)
            route = []
            for _, hop in roles:
                route += [(hop, hop + 1), (hops - hop, hops - hop - 1)]
            got = lax.ppermute(newest, "col", route)
            for piece, hop in roles:
                arrived[piece][hop] = got
            if lane == 0:
                edges[slot] = got

    result = None
    for first, count in ((0, rows - 1), (rows - 1, 1)):
        result = multiply_rows(
            first,
            count,
            panel_owner,
            plan,
            (stored_b, moved_b),
            own_a,
            pieces,
            arrived,
            targets.shape[1],
            result,
        )
    return result[None, None]


def solution(mesh):
    placed = (
        P("row", "col", None, None, None, None, None),
        P("row", "col", None, None, None),
        P("row", "col", None, None, None, None),
        P("row", "col", None, None),
        P("row", "col", None, None),
        P(),
        P(),
    )
    return jax.shard_map(
        local,
        mesh=mesh,
        in_specs=placed,
        out_specs=P("row", "col", None, None, None, None),
        check_vma=False,
    )
```

```python
import functools

import jax
import jax.numpy as jnp
from jax import lax
from jax.experimental import pallas as pl
from jax.experimental.pallas import tpu as pltpu
from jax.sharding import PartitionSpec as P

STEPS = 2
SHARES = (15, 21, 21, 21, 22, 20)
PIECES = len(SHARES)
NOTED = 1
NOTE = 16
STRIDE = 64
MIB = 1024 * 1024

SMEM = pl.BlockSpec(memory_space=pltpu.SMEM)
VMEM = pl.BlockSpec(memory_space=pltpu.VMEM)
ANYWHERE = pl.BlockSpec(memory_space=pl.ANY)


def places_of(owner_ref):
    row_id, row_count = lax.axis_index("row"), lax.axis_size("row")
    panels = [lax.rem(row_id + t, row_count) for t in range(STEPS)]
    places = [owner_ref[row_id, k] for k in panels]
    return panels, [lax.div(p, 2) for p in places], [lax.rem(p, 2) for p in places]


def lag_of(hop, hops):
    return hop + (2 * hop >= hops)


def cut(rows, size):
    total = STEPS * rows * size
    pieces, at = [], 0
    for piece in range(PIECES):
        begin, end = at, total * sum(SHARES[: piece + 1]) // sum(SHARES)
        segments = []
        while at < end:
            unit, first = divmod(at, size)
            count = min(size - first, end - at)
            segments.append((unit % STEPS, unit // STEPS, first, count, at - begin))
            at += count
        if piece == NOTED:
            segments += [(t, -1, 0, NOTE, end - begin + t * NOTE) for t in range(STEPS)]
        pieces.append(tuple(segments))
    return pieces


def extent_of(segments):
    return max(offset + count for _, _, _, count, offset in segments)


def relay_kernel(roles, waits, owner, own, *refs):
    refs = list(refs)
    notes = refs.pop(0) if any(i < 0 for segments, _, _ in roles for _, i, _, _, _ in segments) else None
    arrivals = [refs.pop(0) if arrives else None for _, _, arrives in roles]
    del refs[:waits]
    onward, sem = refs
    _, holders, slots = places_of(owner)
    col_id, last = lax.axis_index("col"), lax.axis_size("col") - 1
    jobs = []
    for place, (segments, hop, _) in enumerate(roles):
        sends = (col_id == hop) | (col_id == last - hop)
        for n, (t, i, first, count, offset) in enumerate(segments):
            mine = sends if hop == 0 else sends & (holders[t] == col_id)
            src = notes.at[slots[t]] if i < 0 else own.at[slots[t], i, pl.ds(first, count)]
            jobs.append((mine, pltpu.make_async_copy(src, onward.at[pl.ds(offset, count)], sem.at[place, n])))
    for when, copy in jobs:
        pl.when(when)(copy.start)
    for (segments, hop, _), arrived in zip(roles, arrivals):
        if arrived is None:
            continue
        sends = (col_id == hop) | (col_id == last - hop)
        for t, _, _, count, offset in segments:

            @pl.when(sends & (holders[t] != col_id))
            def _():
                onward[offset : offset + count] = arrived[offset : offset + count]

    for when, copy in jobs:
        pl.when(when)(copy.wait)


def relay(owner, own, notes, roles, arrivals, after, limit, flops, name):
    noted = any(i < 0 for segments, _ in roles for _, i, _, _, _ in segments)
    size = max(extent_of(segments) for segments, _ in roles)
    given = [a for a in arrivals if a is not None]
    operands = [owner, own] + [notes] * noted + given + after
    specs = [SMEM, ANYWHERE] + [ANYWHERE] * noted + [VMEM] * len(given)
    specs += [pl.BlockSpec(memory_space=pltpu.HBM) if name == "lane0_1" else ANYWHERE] * len(after)
    roles = tuple((segments, hop, a is not None) for (segments, hop), a in zip(roles, arrivals))
    return pl.pallas_call(
        functools.partial(relay_kernel, roles, len(after)),
        out_shape=jax.ShapeDtypeStruct((size, own.shape[3]), own.dtype),
        in_specs=specs,
        out_specs=VMEM,
        scratch_shapes=[pltpu.SemaphoreType.DMA((2, max(len(segments) for segments, _, _ in roles)))],
        compiler_params=pltpu.CompilerParams(vmem_limit_bytes=limit),
        cost_estimate=pl.CostEstimate(flops=flops, bytes_accessed=1024, transcendentals=0),
        name=name,
    )(*operands)


def plan_kernel(nz, spots, owner, atoms, bcols0, bcols1, ccols, notes, *refs):
    arrivals, (plan, note_vm, ccols_vm) = refs[:-4], refs[-3:]
    panels, holders, slots = places_of(owner)
    row_id, col_id, col_count = lax.axis_index("row"), lax.axis_index("col"), lax.axis_size("col")
    panel_rows, nzb = bcols0.shape
    rows, kept = ccols.shape
    lanes = plan.shape[1]
    width = STEPS * nz
    sizes_at, row_at = kept * width, (kept + 1) * width
    for t in range(STEPS):
        hop = jnp.where(holders[t] < col_id, col_id - 1, col_count - 2 - col_id)
        mine = holders[t] == col_id

        @pl.when(mine)
        def _():
            note_vm[t] = notes[slots[t]]

        for h, arrived in enumerate(arrivals):

            @pl.when(jnp.logical_not(mine) & (hop == h))
            def _():
                note_vm[t] = arrived[spots[t] : spots[t] + NOTE]

    ccols_vm[...] = jnp.zeros_like(ccols_vm)
    ccols_vm[:rows, :kept] = ccols[...].astype(jnp.float32)

    source = lax.broadcasted_iota(jnp.int32, (lanes, lanes), 0)
    target = lax.broadcasted_iota(jnp.int32, (lanes, lanes), 1)

    def spread(values, hits):
        return jnp.dot(values, hits.astype(jnp.float32).astype(jnp.bfloat16), preferred_element_type=jnp.float32)

    lane = lax.broadcasted_iota(jnp.int32, plan.shape, 1)
    line = lax.broadcasted_iota(jnp.int32, plan.shape, 0)
    inner = jnp.zeros(plan.shape, jnp.float32)
    second = jnp.zeros(plan.shape, jnp.bool_)
    for t in range(STEPS):
        hits = source < 0
        for e in range(kept + 1):
            at = e * width + t * nz
            hits = hits | (target == source + at)
            if t:
                second = second | ((lane >= at) & (lane < at + nz))
        inner = inner + spread(note_vm[t], hits & (source < nz))
    inner = inner.astype(jnp.int32) + jnp.where(second, panel_rows, 0)
    hits = target == source + row_at + 1
    for e in range(kept):
        hits = hits | ((source == e) & (target >= e * width) & (target < (e + 1) * width))
    column = spread(ccols_vm[...].astype(jnp.bfloat16), hits & (source < kept)).astype(jnp.int32)

    block = jnp.full(plan.shape, -1, jnp.int32)
    size = jnp.zeros(plan.shape, jnp.int32)
    for t, bcols in enumerate((bcols0, bcols1)):
        for j in range(panel_rows):
            here = inner == t * panel_rows + j
            size = jnp.where(here, atoms[panels[t] * panel_rows + j], size)
            for n in range(nzb):
                block = jnp.where(here & (column == bcols[j, n]), j * nzb + n, block)
    col_size = jnp.zeros(plan.shape, jnp.int32)
    for c in range(2 * rows):
        col_size = jnp.where(column == c, atoms[col_id * 2 * rows + c], col_size)
    row_size = jnp.zeros(plan.shape, jnp.int32)
    for i in range(rows):
        row_size = jnp.where(line == i, atoms[row_id * panel_rows + i], row_size)
    tail = jnp.where(lane == row_at, row_size, col_size)
    plan[...] = jnp.where(lane < sizes_at, block, jnp.where(lane < row_at, size, tail))


def make_plan(owner, atoms, bcols0, bcols1, ccols, notes, arrivals, nz, spots, after):
    operands = [owner, atoms, bcols0, bcols1, ccols, notes, *arrivals, after]
    return pl.pallas_call(
        functools.partial(plan_kernel, nz, spots),
        out_shape=jax.ShapeDtypeStruct(notes.shape[1:], jnp.int32),
        in_specs=[SMEM] * 4 + [VMEM] * (2 + len(arrivals)) + [ANYWHERE],
        out_specs=VMEM,
        scratch_shapes=[pltpu.VMEM(notes.shape, notes.dtype), pltpu.VMEM(notes.shape[1:], jnp.float32)],
        compiler_params=pltpu.CompilerParams(vmem_limit_bytes=8 * MIB),
        cost_estimate=pl.CostEstimate(flops=10**9, bytes_accessed=1024, transcendentals=0),
        name="make_plan",
    )(*operands)


def rows_kernel(first, count, hops, sources, owner, plan, b0, b1, own, *refs):
    places = 1 + max(source[0] for source in sources)
    arrived = [refs[at * hops : (at + 1) * hops] for at in range(places)]
    out, a_vm, left_vm, o_vm, a_sem, o_sem = refs[-6:]
    kept, blk = o_vm.shape[1], o_vm.shape[-1]
    size = a_vm.shape[2]
    nz = size // blk
    width = STEPS * nz
    col_id, last = lax.axis_index("col"), lax.axis_size("col") - 1
    _, holders, slots = places_of(owner)
    copies = []
    for at in range(count):
        for t in range(STEPS):
            copy = pltpu.make_async_copy(own.at[slots[t], first + at], a_vm.at[at, t], a_sem.at[at, t])
            copies.append((holders[t] == col_id, copy))
    for when, copy in copies:
        pl.when(when)(copy.start)
    for t in range(STEPS):
        hop = jnp.where(holders[t] < col_id, col_id - 1, last - 1 - col_id)
        for h in range(hops):

            @pl.when((holders[t] != col_id) & (hop == h))
            def _():
                for place, step, i, start, lines, offset in sources:
                    if step != t:
                        continue

                    def one_stride(n, carry):
                        src = pl.ds(pl.multiple_of(offset + n * STRIDE, STRIDE), STRIDE)
                        dst = pl.ds(pl.multiple_of(start + n * STRIDE, STRIDE), STRIDE)
                        a_vm[i - first, t, dst] = arrived[place][h][src]
                        return carry

                    lax.fori_loop(0, lines // STRIDE, one_stride, 0)

    for when, copy in copies:
        pl.when(when)(copy.wait)

    lane = lax.broadcasted_iota(jnp.int32, (blk, blk), 1)
    sub = lax.broadcasted_iota(jnp.int32, (blk, blk), 0)
    flat = [b.reshape(b.shape[0] * b.shape[1], blk, blk) for b in (b0, b1)]

    def one_row(at, carry):
        i = first + at
        for t in range(STEPS):
            for m in range(nz):
                q = t * nz + m
                left_vm[:, q * blk : (q + 1) * blk] = jnp.where(
                    lane < plan[i, kept * width + q],
                    a_vm[at, t, m * blk : (m + 1) * blk],
                    jnp.zeros((), a_vm.dtype),
                )
        row_size = plan[i, kept * width + width]

        for p in range(kept // 2):
            sides = []
            for e in range(2):
                parts = []
                for q in range(width):
                    n = plan[i, (2 * p + e) * width + q]
                    block = flat[q // nz][jnp.maximum(n, 0)]
                    parts.append(jnp.where(n >= 0, block, jnp.zeros((), block.dtype)))
                sides.append(jnp.concatenate(parts, axis=0))
            total = jnp.dot(
                left_vm[...], jnp.concatenate(sides, axis=1), preferred_element_type=jnp.float32
            )
            for e in range(2):
                col_size = plan[i, kept * width + width + 1 + 2 * p + e]
                inside = (sub < row_size) & (lane < col_size)
                part = total[:, e * blk : (e + 1) * blk]
                o_vm[at, 2 * p + e] = jnp.where(inside, part, 0.0).astype(o_vm.dtype)
        pltpu.make_async_copy(o_vm.at[at], out.at[i], o_sem.at[at]).start()
        return carry

    lax.fori_loop(0, count, one_row, 0)
    for at in range(count):
        pltpu.make_async_copy(o_vm.at[at], out.at[first + at], o_sem.at[at]).wait()


def multiply_rows(first, count, owner, plan, b_panels, own, pieces, arrived, kept, so_far):
    rows, size, blk = own.shape[1:]
    nz, hops = size // blk, len(arrived[0])
    operands = [owner, plan, *b_panels, own]
    sources, places = [], 0
    for piece, segments in enumerate(pieces):
        found = [segment for segment in segments if first <= segment[1] < first + count]
        if found:
            sources += [(places, *segment) for segment in found]
            operands += arrived[piece]
            places += 1
    specs = [SMEM] * 2 + [VMEM] * 2 + [ANYWHERE] + [VMEM] * (places * hops)
    aliases = {}
    if so_far is not None:
        aliases = {len(operands): 0}
        operands.append(so_far)
        specs.append(ANYWHERE)
    flops = 4 * count * blk * blk * blk * STEPS * nz * kept
    limit = (12 + places * hops // 2) * MIB
    return pl.pallas_call(
        functools.partial(rows_kernel, first, count, hops, tuple(sources)),
        out_shape=jax.ShapeDtypeStruct((rows, kept, blk, blk), jnp.bfloat16),
        in_specs=specs,
        out_specs=ANYWHERE,
        scratch_shapes=[
            pltpu.VMEM((count, STEPS, size, blk), jnp.bfloat16),
            pltpu.VMEM((blk, STEPS * size), jnp.bfloat16),
            pltpu.VMEM((count, kept, blk, blk), jnp.bfloat16),
            pltpu.SemaphoreType.DMA((count, STEPS)),
            pltpu.SemaphoreType.DMA((count,)),
        ],
        input_output_aliases=aliases,
        compiler_params=pltpu.CompilerParams(vmem_limit_bytes=limit),
        cost_estimate=pl.CostEstimate(flops=flops, bytes_accessed=4 * MIB, transcendentals=0),
        name="multiply_rows",
    )(*operands)


def local(a_vals, a_cols, b_vals, b_cols, c_cols, panel_owner, atom_size):
    row_count = lax.axis_size("row")
    col_count = lax.axis_size("col")
    stored_b, stored_bc = b_vals[0, 0], b_cols[0, 0]
    targets = c_cols[0, 0]
    slot_count, rows, nz, blk = a_vals.shape[2:6]
    own_a = a_vals.reshape(slot_count, rows, nz * blk, blk)
    notes = jnp.pad(
        a_cols[0, 0].astype(own_a.dtype), ((0, 0), (0, NOTE - rows), (0, blk - nz))
    )
    hops = col_count - 1
    from_next = [((i + 1) % row_count, i) for i in range(row_count)]

    pieces = cut(rows, nz * blk)
    spots = tuple(offset for _, i, _, _, offset in pieces[NOTED] if i < 0)
    arrived = [[None] * hops for _ in pieces]
    newest = plan = moved_b = moved_bc = None
    edges = {}
    last_slot = PIECES + lag_of(hops - 1, hops) - 1
    plan_slot = max(PIECES, NOTED + lag_of(hops - 1, hops) + 1)
    for slot in range(last_slot + 1):
        for lane in range((hops + 1) // 2):
            roles = []
            for hop in sorted({lane, hops - 1 - lane}):
                piece = slot - lag_of(hop, hops)
                if 0 <= piece < PIECES:
                    roles.append((piece, hop))
            if not roles:
                continue
            after = [newest] if newest is not None else []
            if slot == PIECES and lane == 1:
                after.append(moved_b)
            before = slot - 2
            if lane == 0 and before > 0 and before in edges:
                after.append(edges[before])
            if slot == plan_slot and lane == 0:
                plan = make_plan(
                    panel_owner, atom_size, stored_bc, moved_bc[0, 0], targets, notes, arrived[NOTED], nz, spots, newest
                )
                after.append(plan)
            arrivals = [arrived[piece][hop - 1] if hop else None for piece, hop in roles]
            sent = [(pieces[piece], hop) for piece, hop in roles]
            flops = (2 if lane == 0 and slot == PIECES + 1 else 1) * 10**9
            limit = 62 * MIB if newest is None else 4 * MIB
            newest = relay(panel_owner, own_a, notes, sent, arrivals, after, limit, flops, f"lane{lane}_{slot}")
            if slot == 1 and lane == 0:
                behind_bc, newest = lax.optimization_barrier((b_cols, newest))
                moved_bc = lax.ppermute(behind_bc, "row", from_next)
                moved_bc, newest, behind_b = lax.optimization_barrier((moved_bc, newest, stored_b))
                moved_b = lax.ppermute(behind_b, "row", from_next)
            route = []
            for _, hop in roles:
                route += [(hop, hop + 1), (hops - hop, hops - hop - 1)]
            got = lax.ppermute(newest, "col", route)
            for piece, hop in roles:
                arrived[piece][hop] = got
            if lane == 0:
                edges[slot] = got

    result = None
    for first, count in ((0, rows - 1), (rows - 1, 1)):
        result = multiply_rows(
            first,
            count,
            panel_owner,
            plan,
            (stored_b, moved_b),
            own_a,
            pieces,
            arrived,
            targets.shape[1],
            result,
        )
    return result[None, None]


def solution(mesh):
    placed = (
        P("row", "col", None, None, None, None, None),
        P("row", "col", None, None, None),
        P("row", "col", None, None, None, None),
        P("row", "col", None, None),
        P("row", "col", None, None),
        P(),
        P(),
    )
    return jax.shard_map(
        local,
        mesh=mesh,
        in_specs=placed,
        out_specs=P("row", "col", None, None, None, None),
        check_vma=False,
    )
```

```python
import functools

import jax
import jax.numpy as jnp
from jax import lax
from jax.experimental import pallas as pl
from jax.experimental.pallas import tpu as pltpu
from jax.sharding import PartitionSpec as P

STEPS = 2
SHARES = (1, 1, 1, 1, 1, 1)
PIECES = len(SHARES)
NOTED = 1
NOTE = 16
MIB = 1024 * 1024

SMEM = pl.BlockSpec(memory_space=pltpu.SMEM)
VMEM = pl.BlockSpec(memory_space=pltpu.VMEM)
ANYWHERE = pl.BlockSpec(memory_space=pl.ANY)


def places_of(owner_ref):
    row_id, row_count = lax.axis_index("row"), lax.axis_size("row")
    panels = [lax.rem(row_id + t, row_count) for t in range(STEPS)]
    places = [owner_ref[row_id, k] for k in panels]
    return panels, [lax.div(p, 2) for p in places], [lax.rem(p, 2) for p in places]


def lag_of(hop, hops):
    return hop + (2 * hop >= hops)


def cut(rows, size):
    total = STEPS * rows * size
    pieces, at = [], 0
    for piece in range(PIECES):
        begin, end = at, total * sum(SHARES[: piece + 1]) // sum(SHARES)
        segments = []
        while at < end:
            unit, first = divmod(at, size)
            count = min(size - first, end - at)
            segments.append((unit % STEPS, unit // STEPS, first, count, at - begin))
            at += count
        if piece == NOTED:
            segments += [(t, -1, 0, NOTE, end - begin + t * NOTE) for t in range(STEPS)]
        pieces.append(tuple(segments))
    return pieces


def extent_of(segments):
    return max(offset + count for _, _, _, count, offset in segments)


def relay_kernel(roles, waits, owner, own, *refs):
    refs = list(refs)
    notes = refs.pop(0) if any(i < 0 for segments, _, _ in roles for _, i, _, _, _ in segments) else None
    arrivals = [refs.pop(0) if arrives else None for _, _, arrives in roles]
    del refs[:waits]
    onward, sem = refs
    _, holders, slots = places_of(owner)
    col_id, last = lax.axis_index("col"), lax.axis_size("col") - 1
    jobs = []
    for place, (segments, hop, _) in enumerate(roles):
        sends = (col_id == hop) | (col_id == last - hop)
        for n, (t, i, first, count, offset) in enumerate(segments):
            mine = sends if hop == 0 else sends & (holders[t] == col_id)
            src = notes.at[slots[t]] if i < 0 else own.at[slots[t], i, pl.ds(first, count)]
            jobs.append((mine, pltpu.make_async_copy(src, onward.at[pl.ds(offset, count)], sem.at[place, n])))
    for when, copy in jobs:
        pl.when(when)(copy.start)
    for (segments, hop, _), arrived in zip(roles, arrivals):
        if arrived is None:
            continue
        sends = (col_id == hop) | (col_id == last - hop)
        for t, _, _, count, offset in segments:

            @pl.when(sends & (holders[t] != col_id))
            def _():
                onward[offset : offset + count] = arrived[offset : offset + count]

    for when, copy in jobs:
        pl.when(when)(copy.wait)


def relay(owner, own, notes, roles, arrivals, after, limit, flops, name):
    noted = any(i < 0 for segments, _ in roles for _, i, _, _, _ in segments)
    size = max(extent_of(segments) for segments, _ in roles)
    given = [a for a in arrivals if a is not None]
    operands = [owner, own] + [notes] * noted + given + after
    specs = [SMEM, ANYWHERE] + [ANYWHERE] * noted + [VMEM] * len(given)
    specs += [pl.BlockSpec(memory_space=pltpu.HBM) if name == "lane0_1" else ANYWHERE] * len(after)
    roles = tuple((segments, hop, a is not None) for (segments, hop), a in zip(roles, arrivals))
    return pl.pallas_call(
        functools.partial(relay_kernel, roles, len(after)),
        out_shape=jax.ShapeDtypeStruct((size, own.shape[3]), own.dtype),
        in_specs=specs,
        out_specs=VMEM,
        scratch_shapes=[pltpu.SemaphoreType.DMA((2, max(len(segments) for segments, _, _ in roles)))],
        compiler_params=pltpu.CompilerParams(vmem_limit_bytes=limit),
        cost_estimate=pl.CostEstimate(flops=flops, bytes_accessed=1024, transcendentals=0),
        name=name,
    )(*operands)


def plan_kernel(nz, spots, owner, atoms, bcols0, bcols1, ccols, notes, *refs):
    arrivals, (plan, note_vm, ccols_vm) = refs[:-4], refs[-3:]
    panels, holders, slots = places_of(owner)
    row_id, col_id, col_count = lax.axis_index("row"), lax.axis_index("col"), lax.axis_size("col")
    panel_rows, nzb = bcols0.shape
    rows, kept = ccols.shape
    lanes = plan.shape[1]
    width = STEPS * nz
    sizes_at, row_at = kept * width, (kept + 1) * width
    for t in range(STEPS):
        hop = jnp.where(holders[t] < col_id, col_id - 1, col_count - 2 - col_id)
        mine = holders[t] == col_id

        @pl.when(mine)
        def _():
            note_vm[t] = notes[slots[t]]

        for h, arrived in enumerate(arrivals):

            @pl.when(jnp.logical_not(mine) & (hop == h))
            def _():
                note_vm[t] = arrived[spots[t] : spots[t] + NOTE]

    ccols_vm[...] = jnp.zeros_like(ccols_vm)
    ccols_vm[:rows, :kept] = ccols[...].astype(jnp.float32)

    source = lax.broadcasted_iota(jnp.int32, (lanes, lanes), 0)
    target = lax.broadcasted_iota(jnp.int32, (lanes, lanes), 1)

    def spread(values, hits):
        return jnp.dot(values, hits.astype(jnp.float32).astype(jnp.bfloat16), preferred_element_type=jnp.float32)

    lane = lax.broadcasted_iota(jnp.int32, plan.shape, 1)
    line = lax.broadcasted_iota(jnp.int32, plan.shape, 0)
    inner = jnp.zeros(plan.shape, jnp.float32)
    second = jnp.zeros(plan.shape, jnp.bool_)
    for t in range(STEPS):
        hits = source < 0
        for e in range(kept + 1):
            at = e * width + t * nz
            hits = hits | (target == source + at)
            if t:
                second = second | ((lane >= at) & (lane < at + nz))
        inner = inner + spread(note_vm[t], hits & (source < nz))
    inner = inner.astype(jnp.int32) + jnp.where(second, panel_rows, 0)
    hits = target == source + row_at + 1
    for e in range(kept):
        hits = hits | ((source == e) & (target >= e * width) & (target < (e + 1) * width))
    column = spread(ccols_vm[...].astype(jnp.bfloat16), hits & (source < kept)).astype(jnp.int32)

    block = jnp.full(plan.shape, -1, jnp.int32)
    size = jnp.zeros(plan.shape, jnp.int32)
    for t, bcols in enumerate((bcols0, bcols1)):
        for j in range(panel_rows):
            here = inner == t * panel_rows + j
            size = jnp.where(here, atoms[panels[t] * panel_rows + j], size)
            for n in range(nzb):
                block = jnp.where(here & (column == bcols[j, n]), j * nzb + n, block)
    col_size = jnp.zeros(plan.shape, jnp.int32)
    for c in range(2 * rows):
        col_size = jnp.where(column == c, atoms[col_id * 2 * rows + c], col_size)
    row_size = jnp.zeros(plan.shape, jnp.int32)
    for i in range(rows):
        row_size = jnp.where(line == i, atoms[row_id * panel_rows + i], row_size)
    tail = jnp.where(lane == row_at, row_size, col_size)
    plan[...] = jnp.where(lane < sizes_at, block, jnp.where(lane < row_at, size, tail))


def make_plan(owner, atoms, bcols0, bcols1, ccols, notes, arrivals, nz, spots, after):
    operands = [owner, atoms, bcols0, bcols1, ccols, notes, *arrivals, after]
    return pl.pallas_call(
        functools.partial(plan_kernel, nz, spots),
        out_shape=jax.ShapeDtypeStruct(notes.shape[1:], jnp.int32),
        in_specs=[SMEM] * 4 + [VMEM] * (2 + len(arrivals)) + [ANYWHERE],
        out_specs=VMEM,
        scratch_shapes=[pltpu.VMEM(notes.shape, notes.dtype), pltpu.VMEM(notes.shape[1:], jnp.float32)],
        compiler_params=pltpu.CompilerParams(vmem_limit_bytes=8 * MIB),
        cost_estimate=pl.CostEstimate(flops=10**9, bytes_accessed=1024, transcendentals=0),
        name="make_plan",
    )(*operands)


def rows_kernel(first, count, hops, sources, owner, plan, b0, b1, own, *refs):
    places = 1 + max(source[0] for source in sources)
    arrived = [refs[at * hops : (at + 1) * hops] for at in range(places)]
    out, a_vm, left_vm, o_vm, a_sem, o_sem = refs[-6:]
    kept, blk = o_vm.shape[1], o_vm.shape[-1]
    size = a_vm.shape[2]
    nz = size // blk
    width = STEPS * nz
    col_id, last = lax.axis_index("col"), lax.axis_size("col") - 1
    _, holders, slots = places_of(owner)
    copies = []
    for at in range(count):
        for t in range(STEPS):
            copy = pltpu.make_async_copy(own.at[slots[t], first + at], a_vm.at[at, t], a_sem.at[at, t])
            copies.append((holders[t] == col_id, copy))
    for when, copy in copies:
        pl.when(when)(copy.start)
    for t in range(STEPS):
        hop = jnp.where(holders[t] < col_id, col_id - 1, last - 1 - col_id)
        for h in range(hops):

            @pl.when((holders[t] != col_id) & (hop == h))
            def _():
                for place, step, i, start, lines, offset in sources:
                    if step == t:
                        a_vm[i - first, t, start : start + lines] = arrived[place][h][offset : offset + lines]

    for when, copy in copies:
        pl.when(when)(copy.wait)

    lane = lax.broadcasted_iota(jnp.int32, (blk, blk), 1)
    sub = lax.broadcasted_iota(jnp.int32, (blk, blk), 0)
    flat = [b.reshape(b.shape[0] * b.shape[1], blk, blk) for b in (b0, b1)]

    def one_row(at, carry):
        i = first + at
        for t in range(STEPS):
            for m in range(nz):
                q = t * nz + m
                left_vm[:, q * blk : (q + 1) * blk] = jnp.where(
                    lane < plan[i, kept * width + q],
                    a_vm[at, t, m * blk : (m + 1) * blk],
                    jnp.zeros((), a_vm.dtype),
                )
        row_size = plan[i, kept * width + width]

        for p in range(kept // 2):
            sides = []
            for e in range(2):
                parts = []
                for q in range(width):
                    n = plan[i, (2 * p + e) * width + q]
                    block = flat[q // nz][jnp.maximum(n, 0)]
                    parts.append(jnp.where(n >= 0, block, jnp.zeros((), block.dtype)))
                sides.append(jnp.concatenate(parts, axis=0))
            total = jnp.dot(
                left_vm[...], jnp.concatenate(sides, axis=1), preferred_element_type=jnp.float32
            )
            for e in range(2):
                col_size = plan[i, kept * width + width + 1 + 2 * p + e]
                inside = (sub < row_size) & (lane < col_size)
                part = total[:, e * blk : (e + 1) * blk]
                o_vm[at, 2 * p + e] = jnp.where(inside, part, 0.0).astype(o_vm.dtype)
        pltpu.make_async_copy(o_vm.at[at], out.at[i], o_sem.at[at]).start()
        return carry

    lax.fori_loop(0, count, one_row, 0)
    for at in range(count):
        pltpu.make_async_copy(o_vm.at[at], out.at[first + at], o_sem.at[at]).wait()


def multiply_rows(first, count, owner, plan, b_panels, own, pieces, arrived, kept, so_far):
    rows, size, blk = own.shape[1:]
    nz, hops = size // blk, len(arrived[0])
    operands = [owner, plan, *b_panels, own]
    sources, places = [], 0
    for piece, segments in enumerate(pieces):
        found = [segment for segment in segments if first <= segment[1] < first + count]
        if found:
            sources += [(places, *segment) for segment in found]
            operands += arrived[piece]
            places += 1
    specs = [SMEM] * 2 + [VMEM] * 2 + [ANYWHERE] + [VMEM] * (places * hops)
    aliases = {}
    if so_far is not None:
        aliases = {len(operands): 0}
        operands.append(so_far)
        specs.append(ANYWHERE)
    flops = 4 * count * blk * blk * blk * STEPS * nz * kept
    limit = (12 + places * hops // 2) * MIB
    return pl.pallas_call(
        functools.partial(rows_kernel, first, count, hops, tuple(sources)),
        out_shape=jax.ShapeDtypeStruct((rows, kept, blk, blk), jnp.bfloat16),
        in_specs=specs,
        out_specs=ANYWHERE,
        scratch_shapes=[
            pltpu.VMEM((count, STEPS, size, blk), jnp.bfloat16),
            pltpu.VMEM((blk, STEPS * size), jnp.bfloat16),
            pltpu.VMEM((count, kept, blk, blk), jnp.bfloat16),
            pltpu.SemaphoreType.DMA((count, STEPS)),
            pltpu.SemaphoreType.DMA((count,)),
        ],
        input_output_aliases=aliases,
        compiler_params=pltpu.CompilerParams(vmem_limit_bytes=limit),
        cost_estimate=pl.CostEstimate(flops=flops, bytes_accessed=4 * MIB, transcendentals=0),
        name="multiply_rows",
    )(*operands)


def local(a_vals, a_cols, b_vals, b_cols, c_cols, panel_owner, atom_size):
    row_count = lax.axis_size("row")
    col_count = lax.axis_size("col")
    stored_b, stored_bc = b_vals[0, 0], b_cols[0, 0]
    targets = c_cols[0, 0]
    slot_count, rows, nz, blk = a_vals.shape[2:6]
    own_a = a_vals.reshape(slot_count, rows, nz * blk, blk)
    notes = jnp.pad(
        a_cols[0, 0].astype(own_a.dtype), ((0, 0), (0, NOTE - rows), (0, blk - nz))
    )
    hops = col_count - 1
    from_next = [((i + 1) % row_count, i) for i in range(row_count)]

    pieces = cut(rows, nz * blk)
    spots = tuple(offset for _, i, _, _, offset in pieces[NOTED] if i < 0)
    arrived = [[None] * hops for _ in pieces]
    newest = plan = moved_b = moved_bc = None
    edges = {}
    last_slot = PIECES + lag_of(hops - 1, hops) - 1
    plan_slot = max(PIECES, NOTED + lag_of(hops - 1, hops) + 1)
    for slot in range(last_slot + 1):
        for lane in range((hops + 1) // 2):
            roles = []
            for hop in sorted({lane, hops - 1 - lane}):
                piece = slot - lag_of(hop, hops)
                if 0 <= piece < PIECES:
                    roles.append((piece, hop))
            if not roles:
                continue
            after = [newest] if newest is not None else []
            if slot == PIECES and lane == 1:
                after.append(moved_b)
            before = slot - 2
            if lane == 0 and before > 0 and before in edges:
                after.append(edges[before])
            if slot == plan_slot and lane == 0:
                plan = make_plan(
                    panel_owner, atom_size, stored_bc, moved_bc[0, 0], targets, notes, arrived[NOTED], nz, spots, newest
                )
                after.append(plan)
            arrivals = [arrived[piece][hop - 1] if hop else None for piece, hop in roles]
            sent = [(pieces[piece], hop) for piece, hop in roles]
            flops = (2 if lane == 0 and slot == PIECES + 1 else 1) * 10**9
            limit = 62 * MIB if newest is None else 4 * MIB
            newest = relay(panel_owner, own_a, notes, sent, arrivals, after, limit, flops, f"lane{lane}_{slot}")
            if slot == 1 and lane == 0:
                behind_bc, newest = lax.optimization_barrier((b_cols, newest))
                moved_bc = lax.ppermute(behind_bc, "row", from_next)
                moved_bc, newest, behind_b = lax.optimization_barrier((moved_bc, newest, stored_b))
                moved_b = lax.ppermute(behind_b, "row", from_next)
            route = []
            for _, hop in roles:
                route += [(hop, hop + 1), (hops - hop, hops - hop - 1)]
            got = lax.ppermute(newest, "col", route)
            for piece, hop in roles:
                arrived[piece][hop] = got
            if lane == 0:
                edges[slot] = got

    result = None
    for first, count in ((0, rows - 2), (rows - 2, 2)):
        result = multiply_rows(
            first,
            count,
            panel_owner,
            plan,
            (stored_b, moved_b),
            own_a,
            pieces,
            arrived,
            targets.shape[1],
            result,
        )
    return result[None, None]


def solution(mesh):
    placed = (
        P("row", "col", None, None, None, None, None),
        P("row", "col", None, None, None),
        P("row", "col", None, None, None, None),
        P("row", "col", None, None),
        P("row", "col", None, None),
        P(),
        P(),
    )
    return jax.shard_map(
        local,
        mesh=mesh,
        in_specs=placed,
        out_specs=P("row", "col", None, None, None, None),
        check_vma=False,
    )
```

```python
import functools

import jax
import jax.numpy as jnp
from jax import lax
from jax.experimental import pallas as pl
from jax.experimental.pallas import tpu as pltpu
from jax.sharding import PartitionSpec as P

STEPS = 2
SHARES = (15, 21, 22, 22, 22, 18)
PIECES = len(SHARES)
NOTED = 1
NOTE = 16
MIB = 1024 * 1024

SMEM = pl.BlockSpec(memory_space=pltpu.SMEM)
VMEM = pl.BlockSpec(memory_space=pltpu.VMEM)
ANYWHERE = pl.BlockSpec(memory_space=pl.ANY)


def places_of(owner_ref):
    row_id, row_count = lax.axis_index("row"), lax.axis_size("row")
    panels = [lax.rem(row_id + t, row_count) for t in range(STEPS)]
    places = [owner_ref[row_id, k] for k in panels]
    return panels, [lax.div(p, 2) for p in places], [lax.rem(p, 2) for p in places]


def lag_of(hop, hops):
    return hop + (2 * hop >= hops)


def cut(rows, size):
    total = STEPS * rows * size
    pieces, at = [], 0
    for piece in range(PIECES):
        begin, end = at, total * sum(SHARES[: piece + 1]) // sum(SHARES)
        segments = []
        while at < end:
            unit, first = divmod(at, size)
            count = min(size - first, end - at)
            segments.append((unit % STEPS, unit // STEPS, first, count, at - begin))
            at += count
        if piece == NOTED:
            segments += [(t, -1, 0, NOTE, end - begin + t * NOTE) for t in range(STEPS)]
        pieces.append(tuple(segments))
    return pieces


def extent_of(segments):
    return max(offset + count for _, _, _, count, offset in segments)


def relay_kernel(roles, waits, owner, own, *refs):
    refs = list(refs)
    notes = refs.pop(0) if any(i < 0 for segments, _, _ in roles for _, i, _, _, _ in segments) else None
    arrivals = [refs.pop(0) if arrives else None for _, _, arrives in roles]
    del refs[:waits]
    onward, sem = refs
    _, holders, slots = places_of(owner)
    col_id, last = lax.axis_index("col"), lax.axis_size("col") - 1
    jobs = []
    for place, (segments, hop, _) in enumerate(roles):
        sends = (col_id == hop) | (col_id == last - hop)
        for n, (t, i, first, count, offset) in enumerate(segments):
            mine = sends if hop == 0 else sends & (holders[t] == col_id)
            src = notes.at[slots[t]] if i < 0 else own.at[slots[t], i, pl.ds(first, count)]
            jobs.append((mine, pltpu.make_async_copy(src, onward.at[pl.ds(offset, count)], sem.at[place, n])))
    for when, copy in jobs:
        pl.when(when)(copy.start)
    for (segments, hop, _), arrived in zip(roles, arrivals):
        if arrived is None:
            continue
        sends = (col_id == hop) | (col_id == last - hop)
        for t, _, _, count, offset in segments:

            @pl.when(sends & (holders[t] != col_id))
            def _():
                onward[offset : offset + count] = arrived[offset : offset + count]

    for when, copy in jobs:
        pl.when(when)(copy.wait)


def relay(owner, own, notes, roles, arrivals, after, limit, flops, name):
    noted = any(i < 0 for segments, _ in roles for _, i, _, _, _ in segments)
    size = max(extent_of(segments) for segments, _ in roles)
    given = [a for a in arrivals if a is not None]
    operands = [owner, own] + [notes] * noted + given + after
    specs = [SMEM, ANYWHERE] + [ANYWHERE] * noted + [VMEM] * len(given)
    specs += [pl.BlockSpec(memory_space=pltpu.HBM) if name == "lane0_1" else ANYWHERE] * len(after)
    roles = tuple((segments, hop, a is not None) for (segments, hop), a in zip(roles, arrivals))
    return pl.pallas_call(
        functools.partial(relay_kernel, roles, len(after)),
        out_shape=jax.ShapeDtypeStruct((size, own.shape[3]), own.dtype),
        in_specs=specs,
        out_specs=VMEM,
        scratch_shapes=[pltpu.SemaphoreType.DMA((2, max(len(segments) for segments, _, _ in roles)))],
        compiler_params=pltpu.CompilerParams(vmem_limit_bytes=limit),
        cost_estimate=pl.CostEstimate(flops=flops, bytes_accessed=1024, transcendentals=0),
        name=name,
    )(*operands)


def plan_kernel(nz, spots, owner, atoms, bcols0, bcols1, ccols, notes, *refs):
    arrivals, (plan, note_vm, ccols_vm) = refs[:-4], refs[-3:]
    panels, holders, slots = places_of(owner)
    row_id, col_id, col_count = lax.axis_index("row"), lax.axis_index("col"), lax.axis_size("col")
    panel_rows, nzb = bcols0.shape
    rows, kept = ccols.shape
    lanes = plan.shape[1]
    width = STEPS * nz
    sizes_at, row_at = kept * width, (kept + 1) * width
    for t in range(STEPS):
        hop = jnp.where(holders[t] < col_id, col_id - 1, col_count - 2 - col_id)
        mine = holders[t] == col_id

        @pl.when(mine)
        def _():
            note_vm[t] = notes[slots[t]]

        for h, arrived in enumerate(arrivals):

            @pl.when(jnp.logical_not(mine) & (hop == h))
            def _():
                note_vm[t] = arrived[spots[t] : spots[t] + NOTE]

    ccols_vm[...] = jnp.zeros_like(ccols_vm)
    ccols_vm[:rows, :kept] = ccols[...].astype(jnp.float32)

    source = lax.broadcasted_iota(jnp.int32, (lanes, lanes), 0)
    target = lax.broadcasted_iota(jnp.int32, (lanes, lanes), 1)

    def spread(values, hits):
        return jnp.dot(values, hits.astype(jnp.float32).astype(jnp.bfloat16), preferred_element_type=jnp.float32)

    lane = lax.broadcasted_iota(jnp.int32, plan.shape, 1)
    line = lax.broadcasted_iota(jnp.int32, plan.shape, 0)
    inner = jnp.zeros(plan.shape, jnp.float32)
    second = jnp.zeros(plan.shape, jnp.bool_)
    for t in range(STEPS):
        hits = source < 0
        for e in range(kept + 1):
            at = e * width + t * nz
            hits = hits | (target == source + at)
            if t:
                second = second | ((lane >= at) & (lane < at + nz))
        inner = inner + spread(note_vm[t], hits & (source < nz))
    inner = inner.astype(jnp.int32) + jnp.where(second, panel_rows, 0)
    hits = target == source + row_at + 1
    for e in range(kept):
        hits = hits | ((source == e) & (target >= e * width) & (target < (e + 1) * width))
    column = spread(ccols_vm[...].astype(jnp.bfloat16), hits & (source < kept)).astype(jnp.int32)

    block = jnp.full(plan.shape, -1, jnp.int32)
    size = jnp.zeros(plan.shape, jnp.int32)
    for t, bcols in enumerate((bcols0, bcols1)):
        for j in range(panel_rows):
            here = inner == t * panel_rows + j
            size = jnp.where(here, atoms[panels[t] * panel_rows + j], size)
            for n in range(nzb):
                block = jnp.where(here & (column == bcols[j, n]), j * nzb + n, block)
    col_size = jnp.zeros(plan.shape, jnp.int32)
    for c in range(2 * rows):
        col_size = jnp.where(column == c, atoms[col_id * 2 * rows + c], col_size)
    row_size = jnp.zeros(plan.shape, jnp.int32)
    for i in range(rows):
        row_size = jnp.where(line == i, atoms[row_id * panel_rows + i], row_size)
    tail = jnp.where(lane == row_at, row_size, col_size)
    plan[...] = jnp.where(lane < sizes_at, block, jnp.where(lane < row_at, size, tail))


def make_plan(owner, atoms, bcols0, bcols1, ccols, notes, arrivals, nz, spots, after):
    operands = [owner, atoms, bcols0, bcols1, ccols, notes, *arrivals, after]
    return pl.pallas_call(
        functools.partial(plan_kernel, nz, spots),
        out_shape=jax.ShapeDtypeStruct(notes.shape[1:], jnp.int32),
        in_specs=[SMEM] * 4 + [VMEM] * (2 + len(arrivals)) + [ANYWHERE],
        out_specs=VMEM,
        scratch_shapes=[pltpu.VMEM(notes.shape, notes.dtype), pltpu.VMEM(notes.shape[1:], jnp.float32)],
        compiler_params=pltpu.CompilerParams(vmem_limit_bytes=8 * MIB),
        cost_estimate=pl.CostEstimate(flops=10**9, bytes_accessed=1024, transcendentals=0),
        name="make_plan",
    )(*operands)


def rows_kernel(first, count, hops, sources, owner, plan, b0, b1, own, *refs):
    places = 1 + max(source[0] for source in sources)
    arrived = [refs[at * hops : (at + 1) * hops] for at in range(places)]
    out, a_vm, left_vm, o_vm, a_sem, o_sem = refs[-6:]
    kept, blk = o_vm.shape[1], o_vm.shape[-1]
    size = a_vm.shape[2]
    nz = size // blk
    width = STEPS * nz
    col_id, last = lax.axis_index("col"), lax.axis_size("col") - 1
    _, holders, slots = places_of(owner)
    copies = []
    for at in range(count):
        for t in range(STEPS):
            copy = pltpu.make_async_copy(own.at[slots[t], first + at], a_vm.at[at, t], a_sem.at[at, t])
            copies.append((holders[t] == col_id, copy))
    for when, copy in copies:
        pl.when(when)(copy.start)
    for t in range(STEPS):
        hop = jnp.where(holders[t] < col_id, col_id - 1, last - 1 - col_id)
        for h in range(hops):

            @pl.when((holders[t] != col_id) & (hop == h))
            def _():
                for place, step, i, start, lines, offset in sources:
                    if step == t:
                        a_vm[i - first, t, start : start + lines] = arrived[place][h][offset : offset + lines]

    for when, copy in copies:
        pl.when(when)(copy.wait)

    lane = lax.broadcasted_iota(jnp.int32, (blk, blk), 1)
    sub = lax.broadcasted_iota(jnp.int32, (blk, blk), 0)
    flat = [b.reshape(b.shape[0] * b.shape[1], blk, blk) for b in (b0, b1)]

    def one_row(at, carry):
        i = first + at
        for t in range(STEPS):
            for m in range(nz):
                q = t * nz + m
                left_vm[:, q * blk : (q + 1) * blk] = jnp.where(
                    lane < plan[i, kept * width + q],
                    a_vm[at, t, m * blk : (m + 1) * blk],
                    jnp.zeros((), a_vm.dtype),
                )
        row_size = plan[i, kept * width + width]

        for p in range(kept // 2):
            sides = []
            for e in range(2):
                parts = []
                for q in range(width):
                    n = plan[i, (2 * p + e) * width + q]
                    block = flat[q // nz][jnp.maximum(n, 0)]
                    parts.append(jnp.where(n >= 0, block, jnp.zeros((), block.dtype)))
                sides.append(jnp.concatenate(parts, axis=0))
            total = jnp.dot(
                left_vm[...], jnp.concatenate(sides, axis=1), preferred_element_type=jnp.float32
            )
            for e in range(2):
                col_size = plan[i, kept * width + width + 1 + 2 * p + e]
                inside = (sub < row_size) & (lane < col_size)
                part = total[:, e * blk : (e + 1) * blk]
                o_vm[at, 2 * p + e] = jnp.where(inside, part, 0.0).astype(o_vm.dtype)
        pltpu.make_async_copy(o_vm.at[at], out.at[i], o_sem.at[at]).start()
        return carry

    lax.fori_loop(0, count, one_row, 0)
    for at in range(count):
        pltpu.make_async_copy(o_vm.at[at], out.at[first + at], o_sem.at[at]).wait()


def multiply_rows(first, count, owner, plan, b_panels, own, pieces, arrived, kept, so_far):
    rows, size, blk = own.shape[1:]
    nz, hops = size // blk, len(arrived[0])
    operands = [owner, plan, *b_panels, own]
    sources, places = [], 0
    for piece, segments in enumerate(pieces):
        found = [segment for segment in segments if first <= segment[1] < first + count]
        if found:
            sources += [(places, *segment) for segment in found]
            operands += arrived[piece]
            places += 1
    specs = [SMEM] * 2 + [VMEM] * 2 + [ANYWHERE] + [VMEM] * (places * hops)
    aliases = {}
    if so_far is not None:
        aliases = {len(operands): 0}
        operands.append(so_far)
        specs.append(ANYWHERE)
    flops = 4 * count * blk * blk * blk * STEPS * nz * kept
    limit = (12 + places * hops // 2) * MIB
    return pl.pallas_call(
        functools.partial(rows_kernel, first, count, hops, tuple(sources)),
        out_shape=jax.ShapeDtypeStruct((rows, kept, blk, blk), jnp.bfloat16),
        in_specs=specs,
        out_specs=ANYWHERE,
        scratch_shapes=[
            pltpu.VMEM((count, STEPS, size, blk), jnp.bfloat16),
            pltpu.VMEM((blk, STEPS * size), jnp.bfloat16),
            pltpu.VMEM((count, kept, blk, blk), jnp.bfloat16),
            pltpu.SemaphoreType.DMA((count, STEPS)),
            pltpu.SemaphoreType.DMA((count,)),
        ],
        input_output_aliases=aliases,
        compiler_params=pltpu.CompilerParams(vmem_limit_bytes=limit),
        cost_estimate=pl.CostEstimate(flops=flops, bytes_accessed=4 * MIB, transcendentals=0),
        name="multiply_rows",
    )(*operands)


def local(a_vals, a_cols, b_vals, b_cols, c_cols, panel_owner, atom_size):
    row_count = lax.axis_size("row")
    col_count = lax.axis_size("col")
    stored_b, stored_bc = b_vals[0, 0], b_cols[0, 0]
    targets = c_cols[0, 0]
    slot_count, rows, nz, blk = a_vals.shape[2:6]
    own_a = a_vals.reshape(slot_count, rows, nz * blk, blk)
    notes = jnp.pad(
        a_cols[0, 0].astype(own_a.dtype), ((0, 0), (0, NOTE - rows), (0, blk - nz))
    )
    hops = col_count - 1
    from_next = [((i + 1) % row_count, i) for i in range(row_count)]

    pieces = cut(rows, nz * blk)
    spots = tuple(offset for _, i, _, _, offset in pieces[NOTED] if i < 0)
    arrived = [[None] * hops for _ in pieces]
    newest = plan = moved_b = moved_bc = None
    edges = {}
    last_slot = PIECES + lag_of(hops - 1, hops) - 1
    plan_slot = max(PIECES, NOTED + lag_of(hops - 1, hops) + 1)
    for slot in range(last_slot + 1):
        for lane in range((hops + 1) // 2):
            roles = []
            for hop in sorted({lane, hops - 1 - lane}):
                piece = slot - lag_of(hop, hops)
                if 0 <= piece < PIECES:
                    roles.append((piece, hop))
            if not roles:
                continue
            after = [newest] if slot > 1 else []
            if slot == lane == 1:
                after.append(moved_bc)
            if slot == PIECES and lane == 1:
                after.append(moved_b)
            before = slot - 2
            if lane == 0 and before > 0 and before in edges:
                after.append(edges[before])
            if slot == plan_slot and lane == 0:
                plan = make_plan(
                    panel_owner, atom_size, stored_bc, moved_bc[0, 0], targets, notes, arrived[NOTED], nz, spots, newest
                )
                after.append(plan)
            arrivals = [arrived[piece][hop - 1] if hop else None for piece, hop in roles]
            sent = [(pieces[piece], hop) for piece, hop in roles]
            flops = (3 - lane if slot == 2 else 2 if lane == 0 and slot == PIECES + 1 else 1) * 10**9
            limit = 62 * MIB if newest is None else 4 * MIB
            newest = relay(panel_owner, own_a, notes, sent, arrivals, after, limit, flops, f"lane{lane}_{slot}")
            if slot == 1 and lane == 0:
                behind_bc, newest = lax.optimization_barrier((b_cols, newest))
                moved_bc = lax.ppermute(behind_bc, "row", from_next)
                moved_bc, behind_b = lax.optimization_barrier((moved_bc, stored_b))
                moved_b = lax.ppermute(behind_b, "row", from_next)
            route = []
            for _, hop in roles:
                route += [(hop, hop + 1), (hops - hop, hops - hop - 1)]
            got = lax.ppermute(newest, "col", route)
            for piece, hop in roles:
                arrived[piece][hop] = got
            if lane == 0:
                edges[slot] = got

    result = None
    for first, count in ((0, rows - 2), (rows - 2, 2)):
        result = multiply_rows(
            first,
            count,
            panel_owner,
            plan,
            (stored_b, moved_b),
            own_a,
            pieces,
            arrived,
            targets.shape[1],
            result,
        )
    return result[None, None]


def solution(mesh):
    placed = (
        P("row", "col", None, None, None, None, None),
        P("row", "col", None, None, None),
        P("row", "col", None, None, None, None),
        P("row", "col", None, None),
        P("row", "col", None, None),
        P(),
        P(),
    )
    return jax.shard_map(
        local,
        mesh=mesh,
        in_specs=placed,
        out_specs=P("row", "col", None, None, None, None),
        check_vma=False,
    )
```

```python
import functools

import jax
import jax.numpy as jnp
from jax import lax
from jax.experimental import pallas as pl
from jax.experimental.pallas import tpu as pltpu
from jax.sharding import PartitionSpec as P

STEPS = 2
SHARES = (1, 1, 1, 1, 1, 1)
PIECES = len(SHARES)
NOTED = 1
NOTE = 16
MIB = 1024 * 1024

SMEM = pl.BlockSpec(memory_space=pltpu.SMEM)
VMEM = pl.BlockSpec(memory_space=pltpu.VMEM)
ANYWHERE = pl.BlockSpec(memory_space=pl.ANY)


def places_of(owner_ref):
    row_id, row_count = lax.axis_index("row"), lax.axis_size("row")
    panels = [lax.rem(row_id + t, row_count) for t in range(STEPS)]
    places = [owner_ref[row_id, k] for k in panels]
    return panels, [lax.div(p, 2) for p in places], [lax.rem(p, 2) for p in places]


def lag_of(hop, hops):
    return hop + (2 * hop >= hops)


def cut(rows, size):
    total = STEPS * rows * size
    pieces, at = [], 0
    for piece in range(PIECES):
        begin, end = at, total * sum(SHARES[: piece + 1]) // sum(SHARES)
        segments = []
        while at < end:
            unit, first = divmod(at, size)
            count = min(size - first, end - at)
            segments.append((unit % STEPS, unit // STEPS, first, count, at - begin))
            at += count
        if piece == NOTED:
            segments += [(t, -1, 0, NOTE, end - begin + t * NOTE) for t in range(STEPS)]
        pieces.append(tuple(segments))
    return pieces


def extent_of(segments):
    return max(offset + count for _, _, _, count, offset in segments)


def relay_kernel(roles, waits, owner, own, *refs):
    refs = list(refs)
    notes = refs.pop(0) if any(i < 0 for segments, _, _ in roles for _, i, _, _, _ in segments) else None
    arrivals = [refs.pop(0) if arrives else None for _, _, arrives in roles]
    del refs[:waits]
    onward, sem = refs
    _, holders, slots = places_of(owner)
    col_id, last = lax.axis_index("col"), lax.axis_size("col") - 1
    jobs = []
    for place, (segments, hop, _) in enumerate(roles):
        sends = (col_id == hop) | (col_id == last - hop)
        for n, (t, i, first, count, offset) in enumerate(segments):
            mine = sends if hop == 0 else sends & (holders[t] == col_id)
            src = notes.at[slots[t]] if i < 0 else own.at[slots[t], i, pl.ds(first, count)]
            jobs.append((mine, pltpu.make_async_copy(src, onward.at[pl.ds(offset, count)], sem.at[place, n])))
    for when, copy in jobs:
        pl.when(when)(copy.start)
    for (segments, hop, _), arrived in zip(roles, arrivals):
        if arrived is None:
            continue
        sends = (col_id == hop) | (col_id == last - hop)
        for t, _, _, count, offset in segments:

            @pl.when(sends & (holders[t] != col_id))
            def _():
                onward[offset : offset + count] = arrived[offset : offset + count]

    for when, copy in jobs:
        pl.when(when)(copy.wait)


def relay(owner, own, notes, roles, arrivals, after, limit, flops, name):
    noted = any(i < 0 for segments, _ in roles for _, i, _, _, _ in segments)
    size = max(extent_of(segments) for segments, _ in roles)
    given = [a for a in arrivals if a is not None]
    operands = [owner, own] + [notes] * noted + given + after
    specs = [SMEM, ANYWHERE] + [ANYWHERE] * noted + [VMEM] * len(given)
    specs += [pl.BlockSpec(memory_space=pltpu.HBM) if name == "lane0_1" else ANYWHERE] * len(after)
    roles = tuple((segments, hop, a is not None) for (segments, hop), a in zip(roles, arrivals))
    return pl.pallas_call(
        functools.partial(relay_kernel, roles, len(after)),
        out_shape=jax.ShapeDtypeStruct((size, own.shape[3]), own.dtype),
        in_specs=specs,
        out_specs=VMEM,
        scratch_shapes=[pltpu.SemaphoreType.DMA((2, max(len(segments) for segments, _, _ in roles)))],
        compiler_params=pltpu.CompilerParams(vmem_limit_bytes=limit),
        cost_estimate=pl.CostEstimate(flops=flops, bytes_accessed=1024, transcendentals=0),
        name=name,
    )(*operands)


def plan_kernel(nz, spots, owner, atoms, bcols0, bcols1, ccols, notes, *refs):
    arrivals, (plan, note_vm, ccols_vm) = refs[:-4], refs[-3:]
    panels, holders, slots = places_of(owner)
    row_id, col_id, col_count = lax.axis_index("row"), lax.axis_index("col"), lax.axis_size("col")
    panel_rows, nzb = bcols0.shape
    rows, kept = ccols.shape
    lanes = plan.shape[1]
    width = STEPS * nz
    sizes_at, row_at = kept * width, (kept + 1) * width
    for t in range(STEPS):
        hop = jnp.where(holders[t] < col_id, col_id - 1, col_count - 2 - col_id)
        mine = holders[t] == col_id

        @pl.when(mine)
        def _():
            note_vm[t] = notes[slots[t]]

        for h, arrived in enumerate(arrivals):

            @pl.when(jnp.logical_not(mine) & (hop == h))
            def _():
                note_vm[t] = arrived[spots[t] : spots[t] + NOTE]

    ccols_vm[...] = jnp.zeros_like(ccols_vm)
    ccols_vm[:rows, :kept] = ccols[...].astype(jnp.float32)

    source = lax.broadcasted_iota(jnp.int32, (lanes, lanes), 0)
    target = lax.broadcasted_iota(jnp.int32, (lanes, lanes), 1)

    def spread(values, hits):
        return jnp.dot(values, hits.astype(jnp.float32).astype(jnp.bfloat16), preferred_element_type=jnp.float32)

    lane = lax.broadcasted_iota(jnp.int32, plan.shape, 1)
    line = lax.broadcasted_iota(jnp.int32, plan.shape, 0)
    inner = jnp.zeros(plan.shape, jnp.float32)
    second = jnp.zeros(plan.shape, jnp.bool_)
    for t in range(STEPS):
        hits = source < 0
        for e in range(kept + 1):
            at = e * width + t * nz
            hits = hits | (target == source + at)
            if t:
                second = second | ((lane >= at) & (lane < at + nz))
        inner = inner + spread(note_vm[t], hits & (source < nz))
    inner = inner.astype(jnp.int32) + jnp.where(second, panel_rows, 0)
    hits = target == source + row_at + 1
    for e in range(kept):
        hits = hits | ((source == e) & (target >= e * width) & (target < (e + 1) * width))
    column = spread(ccols_vm[...].astype(jnp.bfloat16), hits & (source < kept)).astype(jnp.int32)

    block = jnp.full(plan.shape, -1, jnp.int32)
    size = jnp.zeros(plan.shape, jnp.int32)
    for t, bcols in enumerate((bcols0, bcols1)):
        for j in range(panel_rows):
            here = inner == t * panel_rows + j
            size = jnp.where(here, atoms[panels[t] * panel_rows + j], size)
            for n in range(nzb):
                block = jnp.where(here & (column == bcols[j, n]), j * nzb + n, block)
    col_size = jnp.zeros(plan.shape, jnp.int32)
    for c in range(2 * rows):
        col_size = jnp.where(column == c, atoms[col_id * 2 * rows + c], col_size)
    row_size = jnp.zeros(plan.shape, jnp.int32)
    for i in range(rows):
        row_size = jnp.where(line == i, atoms[row_id * panel_rows + i], row_size)
    tail = jnp.where(lane == row_at, row_size, col_size)
    plan[...] = jnp.where(lane < sizes_at, block, jnp.where(lane < row_at, size, tail))


def make_plan(owner, atoms, bcols0, bcols1, ccols, notes, arrivals, nz, spots, after):
    operands = [owner, atoms, bcols0, bcols1, ccols, notes, *arrivals, after]
    return pl.pallas_call(
        functools.partial(plan_kernel, nz, spots),
        out_shape=jax.ShapeDtypeStruct(notes.shape[1:], jnp.int32),
        in_specs=[SMEM] * 4 + [VMEM] * (2 + len(arrivals)) + [ANYWHERE],
        out_specs=VMEM,
        scratch_shapes=[pltpu.VMEM(notes.shape, notes.dtype), pltpu.VMEM(notes.shape[1:], jnp.float32)],
        compiler_params=pltpu.CompilerParams(vmem_limit_bytes=8 * MIB),
        cost_estimate=pl.CostEstimate(flops=10**9, bytes_accessed=1024, transcendentals=0),
        name="make_plan",
    )(*operands)


def rows_kernel(first, count, hops, sources, owner, plan, b0, b1, own, *refs):
    places = 1 + max(source[0] for source in sources)
    arrived = [refs[at * hops : (at + 1) * hops] for at in range(places)]
    out, a_vm, left_vm, o_vm, a_sem, o_sem = refs[-6:]
    kept, blk = o_vm.shape[1], o_vm.shape[-1]
    size = a_vm.shape[2]
    nz = size // blk
    width = STEPS * nz
    col_id, last = lax.axis_index("col"), lax.axis_size("col") - 1
    _, holders, slots = places_of(owner)
    copies = []
    for at in range(count):
        for t in range(STEPS):
            copy = pltpu.make_async_copy(own.at[slots[t], first + at], a_vm.at[at, t], a_sem.at[at, t])
            copies.append((holders[t] == col_id, copy))
    for when, copy in copies:
        pl.when(when)(copy.start)
    for t in range(STEPS):
        hop = jnp.where(holders[t] < col_id, col_id - 1, last - 1 - col_id)
        for h in range(hops):

            @pl.when((holders[t] != col_id) & (hop == h))
            def _():
                for place, step, i, start, lines, offset in sources:
                    if step == t:
                        a_vm[i - first, t, start : start + lines] = arrived[place][h][offset : offset + lines]

    for when, copy in copies:
        pl.when(when)(copy.wait)

    lane = lax.broadcasted_iota(jnp.int32, (blk, blk), 1)
    sub = lax.broadcasted_iota(jnp.int32, (blk, blk), 0)
    flat = [b.reshape(b.shape[0] * b.shape[1], blk, blk) for b in (b0, b1)]

    def one_row(at, carry):
        i = first + at
        for t in range(STEPS):
            for m in range(nz):
                q = t * nz + m
                left_vm[:, q * blk : (q + 1) * blk] = jnp.where(
                    lane < plan[i, kept * width + q],
                    a_vm[at, t, m * blk : (m + 1) * blk],
                    jnp.zeros((), a_vm.dtype),
                )
        row_size = plan[i, kept * width + width]

        for p in range(kept // 2):
            sides = []
            for e in range(2):
                parts = []
                for q in range(width):
                    n = plan[i, (2 * p + e) * width + q]
                    block = flat[q // nz][jnp.maximum(n, 0)]
                    parts.append(jnp.where(n >= 0, block, jnp.zeros((), block.dtype)))
                sides.append(jnp.concatenate(parts, axis=0))
            total = jnp.dot(
                left_vm[...], jnp.concatenate(sides, axis=1), preferred_element_type=jnp.float32
            )
            for e in range(2):
                col_size = plan[i, kept * width + width + 1 + 2 * p + e]
                inside = (sub < row_size) & (lane < col_size)
                part = total[:, e * blk : (e + 1) * blk]
                o_vm[at, 2 * p + e] = jnp.where(inside, part, 0.0).astype(o_vm.dtype)
        pltpu.make_async_copy(o_vm.at[at], out.at[i], o_sem.at[at]).start()
        return carry

    lax.fori_loop(0, count, one_row, 0)
    for at in range(count):
        pltpu.make_async_copy(o_vm.at[at], out.at[first + at], o_sem.at[at]).wait()


def multiply_rows(first, count, owner, plan, b_panels, own, pieces, arrived, kept, so_far):
    rows, size, blk = own.shape[1:]
    nz, hops = size // blk, len(arrived[0])
    operands = [owner, plan, *b_panels, own]
    sources, places = [], 0
    for piece, segments in enumerate(pieces):
        found = [segment for segment in segments if first <= segment[1] < first + count]
        if found:
            sources += [(places, *segment) for segment in found]
            operands += arrived[piece]
            places += 1
    specs = [SMEM] * 2 + [VMEM] * 2 + [ANYWHERE] + [VMEM] * (places * hops)
    aliases = {}
    if so_far is not None:
        aliases = {len(operands): 0}
        operands.append(so_far)
        specs.append(ANYWHERE)
    flops = 4 * count * blk * blk * blk * STEPS * nz * kept
    limit = (12 + places * hops // 2) * MIB
    return pl.pallas_call(
        functools.partial(rows_kernel, first, count, hops, tuple(sources)),
        out_shape=jax.ShapeDtypeStruct((rows, kept, blk, blk), jnp.bfloat16),
        in_specs=specs,
        out_specs=ANYWHERE,
        scratch_shapes=[
            pltpu.VMEM((count, STEPS, size, blk), jnp.bfloat16),
            pltpu.VMEM((blk, STEPS * size), jnp.bfloat16),
            pltpu.VMEM((count, kept, blk, blk), jnp.bfloat16),
            pltpu.SemaphoreType.DMA((count, STEPS)),
            pltpu.SemaphoreType.DMA((count,)),
        ],
        input_output_aliases=aliases,
        compiler_params=pltpu.CompilerParams(vmem_limit_bytes=limit),
        cost_estimate=pl.CostEstimate(flops=flops, bytes_accessed=4 * MIB, transcendentals=0),
        name="multiply_rows",
    )(*operands)


def local(a_vals, a_cols, b_vals, b_cols, c_cols, panel_owner, atom_size):
    row_count = lax.axis_size("row")
    col_count = lax.axis_size("col")
    stored_b, stored_bc = b_vals[0, 0], b_cols[0, 0]
    targets = c_cols[0, 0]
    slot_count, rows, nz, blk = a_vals.shape[2:6]
    own_a = a_vals.reshape(slot_count, rows, nz * blk, blk)
    notes = jnp.pad(
        a_cols[0, 0].astype(own_a.dtype), ((0, 0), (0, NOTE - rows), (0, blk - nz))
    )
    hops = col_count - 1
    from_next = [((i + 1) % row_count, i) for i in range(row_count)]

    pieces = cut(rows, nz * blk)
    spots = tuple(offset for _, i, _, _, offset in pieces[NOTED] if i < 0)
    arrived = [[None] * hops for _ in pieces]
    newest = plan = moved_b = moved_bc = None
    edges = {}
    last_slot = PIECES + lag_of(hops - 1, hops) - 1
    plan_slot = max(PIECES, NOTED + lag_of(hops - 1, hops) + 1)
    for slot in range(last_slot + 1):
        for lane in range((hops + 1) // 2):
            roles = []
            for hop in sorted({lane, hops - 1 - lane}):
                piece = slot - lag_of(hop, hops)
                if 0 <= piece < PIECES:
                    roles.append((piece, hop))
            if not roles:
                continue
            after = [newest] if slot > 1 else []
            if slot == lane == 1:
                after.append(moved_bc)
            if slot == PIECES and lane == 1:
                after.append(moved_b)
            before = slot - 2
            if lane == 0 and before > 0 and before in edges:
                after.append(edges[before])
            if slot == plan_slot and lane == 0:
                plan = make_plan(
                    panel_owner, atom_size, stored_bc, moved_bc[0, 0], targets, notes, arrived[NOTED], nz, spots, newest
                )
                after.append(plan)
            arrivals = [arrived[piece][hop - 1] if hop else None for piece, hop in roles]
            sent = [(pieces[piece], hop) for piece, hop in roles]
            flops = (3 - lane if slot == 2 else 2 if lane == 0 and slot == PIECES + 1 else 1) * 10**9
            limit = 62 * MIB if newest is None else 4 * MIB
            newest = relay(panel_owner, own_a, notes, sent, arrivals, after, limit, flops, f"lane{lane}_{slot}")
            if slot == 1 and lane == 0:
                behind_bc, newest = lax.optimization_barrier((b_cols, newest))
                moved_bc = lax.ppermute(behind_bc, "row", from_next)
                moved_bc, behind_b = lax.optimization_barrier((moved_bc, stored_b))
                moved_b = lax.ppermute(behind_b, "row", from_next)
            route = []
            for hop in sorted({lane, hops - 1 - lane}):
                route += [(hop, hop + 1), (hops - hop, hops - hop - 1)]
            got = lax.ppermute(newest, "col", route)
            for piece, hop in roles:
                arrived[piece][hop] = got
            if lane == 0:
                edges[slot] = got

    result = None
    for first, count in ((0, rows - 2), (rows - 2, 1), (rows - 1, 1)):
        result = multiply_rows(
            first,
            count,
            panel_owner,
            plan,
            (stored_b, moved_b),
            own_a,
            pieces,
            arrived,
            targets.shape[1],
            result,
        )
    return result[None, None]


def solution(mesh):
    placed = (
        P("row", "col", None, None, None, None, None),
        P("row", "col", None, None, None),
        P("row", "col", None, None, None, None),
        P("row", "col", None, None),
        P("row", "col", None, None),
        P(),
        P(),
    )
    return jax.shard_map(
        local,
        mesh=mesh,
        in_specs=placed,
        out_specs=P("row", "col", None, None, None, None),
        check_vma=False,
    )
```

```python
import functools

import jax
import jax.numpy as jnp
from jax import lax
from jax.experimental import pallas as pl
from jax.experimental.pallas import tpu as pltpu
from jax.sharding import PartitionSpec as P

STEPS = 2
SHARES = (1, 1, 1, 1, 1, 1)
PIECES = len(SHARES)
NOTED = 1
NOTE = 16
MIB = 1024 * 1024

SMEM = pl.BlockSpec(memory_space=pltpu.SMEM)
VMEM = pl.BlockSpec(memory_space=pltpu.VMEM)
ANYWHERE = pl.BlockSpec(memory_space=pl.ANY)


def places_of(owner_ref):
    row_id, row_count = lax.axis_index("row"), lax.axis_size("row")
    panels = [lax.rem(row_id + t, row_count) for t in range(STEPS)]
    places = [owner_ref[row_id, k] for k in panels]
    return panels, [lax.div(p, 2) for p in places], [lax.rem(p, 2) for p in places]


def lag_of(hop, hops):
    return hop + (2 * hop >= hops)


def cut(rows, size):
    total = STEPS * rows * size
    pieces, at = [], 0
    for piece in range(PIECES):
        begin, end = at, total * sum(SHARES[: piece + 1]) // sum(SHARES)
        segments = []
        while at < end:
            unit, first = divmod(at, size)
            count = min(size - first, end - at)
            segments.append((unit % STEPS, unit // STEPS, first, count, at - begin))
            at += count
        if piece == NOTED:
            segments += [(t, -1, 0, NOTE, end - begin + t * NOTE) for t in range(STEPS)]
        pieces.append(tuple(segments))
    return pieces


def extent_of(segments):
    return max(offset + count for _, _, _, count, offset in segments)


def relay_kernel(roles, waits, owner, own, *refs):
    refs = list(refs)
    notes = refs.pop(0) if any(i < 0 for segments, _, _ in roles for _, i, _, _, _ in segments) else None
    arrivals = [refs.pop(0) if arrives else None for _, _, arrives in roles]
    del refs[:waits]
    onward, sem = refs
    _, holders, slots = places_of(owner)
    col_id, last = lax.axis_index("col"), lax.axis_size("col") - 1
    jobs = []
    for place, (segments, hop, _) in enumerate(roles):
        sends = (col_id == hop) | (col_id == last - hop)
        for n, (t, i, first, count, offset) in enumerate(segments):
            mine = sends if hop == 0 else sends & (holders[t] == col_id)
            src = notes.at[slots[t]] if i < 0 else own.at[slots[t], i, pl.ds(first, count)]
            jobs.append((mine, pltpu.make_async_copy(src, onward.at[pl.ds(offset, count)], sem.at[place, n])))
    for when, copy in jobs:
        pl.when(when)(copy.start)
    for (segments, hop, _), arrived in zip(roles, arrivals):
        if arrived is None:
            continue
        sends = (col_id == hop) | (col_id == last - hop)
        for t, _, _, count, offset in segments:

            @pl.when(sends & (holders[t] != col_id))
            def _():
                onward[offset : offset + count] = arrived[offset : offset + count]

    for when, copy in jobs:
        pl.when(when)(copy.wait)


def relay(owner, own, notes, roles, arrivals, after, limit, flops, name):
    noted = any(i < 0 for segments, _ in roles for _, i, _, _, _ in segments)
    size = max(extent_of(segments) for segments, _ in roles)
    given = [a for a in arrivals if a is not None]
    operands = [owner, own] + [notes] * noted + given + after
    specs = [SMEM, ANYWHERE] + [ANYWHERE] * noted + [VMEM] * len(given)
    specs += [pl.BlockSpec(memory_space=pltpu.HBM) if name == "lane0_1" else ANYWHERE] * len(after)
    roles = tuple((segments, hop, a is not None) for (segments, hop), a in zip(roles, arrivals))
    return pl.pallas_call(
        functools.partial(relay_kernel, roles, len(after)),
        out_shape=jax.ShapeDtypeStruct((size, own.shape[3]), own.dtype),
        in_specs=specs,
        out_specs=VMEM,
        scratch_shapes=[pltpu.SemaphoreType.DMA((2, max(len(segments) for segments, _, _ in roles)))],
        compiler_params=pltpu.CompilerParams(vmem_limit_bytes=limit),
        cost_estimate=pl.CostEstimate(flops=flops, bytes_accessed=1024, transcendentals=0),
        name=name,
    )(*operands)


def plan_kernel(nz, spots, owner, atoms, bcols0, bcols1, ccols, notes, *refs):
    arrivals, (plan, note_vm, ccols_vm) = refs[:-4], refs[-3:]
    panels, holders, slots = places_of(owner)
    row_id, col_id, col_count = lax.axis_index("row"), lax.axis_index("col"), lax.axis_size("col")
    panel_rows, nzb = bcols0.shape
    rows, kept = ccols.shape
    lanes = plan.shape[1]
    width = STEPS * nz
    sizes_at, row_at = kept * width, (kept + 1) * width
    for t in range(STEPS):
        hop = jnp.where(holders[t] < col_id, col_id - 1, col_count - 2 - col_id)
        mine = holders[t] == col_id

        @pl.when(mine)
        def _():
            note_vm[t] = notes[slots[t]]

        for h, arrived in enumerate(arrivals):

            @pl.when(jnp.logical_not(mine) & (hop == h))
            def _():
                note_vm[t] = arrived[spots[t] : spots[t] + NOTE]

    ccols_vm[...] = jnp.zeros_like(ccols_vm)
    ccols_vm[:rows, :kept] = ccols[...].astype(jnp.float32)

    source = lax.broadcasted_iota(jnp.int32, (lanes, lanes), 0)
    target = lax.broadcasted_iota(jnp.int32, (lanes, lanes), 1)

    def spread(values, hits):
        return jnp.dot(values, hits.astype(jnp.float32).astype(jnp.bfloat16), preferred_element_type=jnp.float32)

    lane = lax.broadcasted_iota(jnp.int32, plan.shape, 1)
    line = lax.broadcasted_iota(jnp.int32, plan.shape, 0)
    inner = jnp.zeros(plan.shape, jnp.float32)
    second = jnp.zeros(plan.shape, jnp.bool_)
    for t in range(STEPS):
        hits = source < 0
        for e in range(kept + 1):
            at = e * width + t * nz
            hits = hits | (target == source + at)
            if t:
                second = second | ((lane >= at) & (lane < at + nz))
        inner = inner + spread(note_vm[t], hits & (source < nz))
    inner = inner.astype(jnp.int32) + jnp.where(second, panel_rows, 0)
    hits = target == source + row_at + 1
    for e in range(kept):
        hits = hits | ((source == e) & (target >= e * width) & (target < (e + 1) * width))
    column = spread(ccols_vm[...].astype(jnp.bfloat16), hits & (source < kept)).astype(jnp.int32)

    block = jnp.full(plan.shape, -1, jnp.int32)
    size = jnp.zeros(plan.shape, jnp.int32)
    for t, bcols in enumerate((bcols0, bcols1)):
        for j in range(panel_rows):
            here = inner == t * panel_rows + j
            size = jnp.where(here, atoms[panels[t] * panel_rows + j], size)
            for n in range(nzb):
                block = jnp.where(here & (column == bcols[j, n]), j * nzb + n, block)
    col_size = jnp.zeros(plan.shape, jnp.int32)
    for c in range(2 * rows):
        col_size = jnp.where(column == c, atoms[col_id * 2 * rows + c], col_size)
    row_size = jnp.zeros(plan.shape, jnp.int32)
    for i in range(rows):
        row_size = jnp.where(line == i, atoms[row_id * panel_rows + i], row_size)
    tail = jnp.where(lane == row_at, row_size, col_size)
    plan[...] = jnp.where(lane < sizes_at, block, jnp.where(lane < row_at, size, tail))


def make_plan(owner, atoms, bcols0, bcols1, ccols, notes, arrivals, nz, spots, after):
    operands = [owner, atoms, bcols0, bcols1, ccols, notes, *arrivals, after]
    return pl.pallas_call(
        functools.partial(plan_kernel, nz, spots),
        out_shape=jax.ShapeDtypeStruct(notes.shape[1:], jnp.int32),
        in_specs=[SMEM] * 4 + [VMEM] * (2 + len(arrivals)) + [ANYWHERE],
        out_specs=VMEM,
        scratch_shapes=[pltpu.VMEM(notes.shape, notes.dtype), pltpu.VMEM(notes.shape[1:], jnp.float32)],
        compiler_params=pltpu.CompilerParams(vmem_limit_bytes=8 * MIB),
        cost_estimate=pl.CostEstimate(flops=10**9, bytes_accessed=1024, transcendentals=0),
        name="make_plan",
    )(*operands)


def rows_kernel(first, count, hops, sources, owner, plan, b0, b1, own, *refs):
    places = 1 + max(source[0] for source in sources)
    arrived = [refs[at * hops : (at + 1) * hops] for at in range(places)]
    out, a_vm, left_vm, o_vm, a_sem, o_sem = refs[-6:]
    kept, blk = o_vm.shape[1], o_vm.shape[-1]
    size = a_vm.shape[2]
    nz = size // blk
    width = STEPS * nz
    col_id, last = lax.axis_index("col"), lax.axis_size("col") - 1
    _, holders, slots = places_of(owner)
    copies = []
    for at in range(count):
        for t in range(STEPS):
            copy = pltpu.make_async_copy(own.at[slots[t], first + at], a_vm.at[at, t], a_sem.at[at, t])
            copies.append((holders[t] == col_id, copy))
    for when, copy in copies:
        pl.when(when)(copy.start)
    for t in range(STEPS):
        hop = jnp.where(holders[t] < col_id, col_id - 1, last - 1 - col_id)
        for h in range(hops):

            @pl.when((holders[t] != col_id) & (hop == h))
            def _():
                for place, step, i, start, lines, offset in sources:
                    if step == t:
                        a_vm[i - first, t, start : start + lines] = arrived[place][h][offset : offset + lines]

    for when, copy in copies:
        pl.when(when)(copy.wait)

    lane = lax.broadcasted_iota(jnp.int32, (blk, blk), 1)
    sub = lax.broadcasted_iota(jnp.int32, (blk, blk), 0)
    flat = [b.reshape(b.shape[0] * b.shape[1], blk, blk) for b in (b0, b1)]

    def one_row(at, carry):
        i = first + at
        for t in range(STEPS):
            for m in range(nz):
                q = t * nz + m
                left_vm[:, q * blk : (q + 1) * blk] = jnp.where(
                    lane < plan[i, kept * width + q],
                    a_vm[at, t, m * blk : (m + 1) * blk],
                    jnp.zeros((), a_vm.dtype),
                )
        row_size = plan[i, kept * width + width]

        for p in range(kept // 2):
            sides = []
            for e in range(2):
                parts = []
                for q in range(width):
                    n = plan[i, (2 * p + e) * width + q]
                    block = flat[q // nz][jnp.maximum(n, 0)]
                    parts.append(jnp.where(n >= 0, block, jnp.zeros((), block.dtype)))
                sides.append(jnp.concatenate(parts, axis=0))
            total = jnp.dot(
                left_vm[...], jnp.concatenate(sides, axis=1), preferred_element_type=jnp.float32
            )
            for e in range(2):
                col_size = plan[i, kept * width + width + 1 + 2 * p + e]
                inside = (sub < row_size) & (lane < col_size)
                part = total[:, e * blk : (e + 1) * blk]
                o_vm[at, 2 * p + e] = jnp.where(inside, part, 0.0).astype(o_vm.dtype)
        pltpu.make_async_copy(o_vm.at[at], out.at[i], o_sem.at[at]).start()
        return carry

    lax.fori_loop(0, count, one_row, 0)
    for at in range(count):
        pltpu.make_async_copy(o_vm.at[at], out.at[first + at], o_sem.at[at]).wait()


def multiply_rows(first, count, owner, plan, b_panels, own, pieces, arrived, kept, so_far):
    rows, size, blk = own.shape[1:]
    nz, hops = size // blk, len(arrived[0])
    operands = [owner, plan, *b_panels, own]
    sources, places = [], 0
    for piece, segments in enumerate(pieces):
        found = [segment for segment in segments if first <= segment[1] < first + count]
        if found:
            sources += [(places, *segment) for segment in found]
            operands += arrived[piece]
            places += 1
    specs = [SMEM] * 2 + [VMEM] * 2 + [ANYWHERE] + [VMEM] * (places * hops)
    aliases = {}
    if so_far is not None:
        aliases = {len(operands): 0}
        operands.append(so_far)
        specs.append(ANYWHERE)
    flops = 4 * count * blk * blk * blk * STEPS * nz * kept
    limit = (12 + places * hops // 2) * MIB
    return pl.pallas_call(
        functools.partial(rows_kernel, first, count, hops, tuple(sources)),
        out_shape=jax.ShapeDtypeStruct((rows, kept, blk, blk), jnp.bfloat16),
        in_specs=specs,
        out_specs=ANYWHERE,
        scratch_shapes=[
            pltpu.VMEM((count, STEPS, size, blk), jnp.bfloat16),
            pltpu.VMEM((blk, STEPS * size), jnp.bfloat16),
            pltpu.VMEM((count, kept, blk, blk), jnp.bfloat16),
            pltpu.SemaphoreType.DMA((count, STEPS)),
            pltpu.SemaphoreType.DMA((count,)),
        ],
        input_output_aliases=aliases,
        compiler_params=pltpu.CompilerParams(vmem_limit_bytes=limit),
        cost_estimate=pl.CostEstimate(flops=flops, bytes_accessed=4 * MIB, transcendentals=0),
        name="multiply_rows",
    )(*operands)


def local(a_vals, a_cols, b_vals, b_cols, c_cols, panel_owner, atom_size):
    row_count = lax.axis_size("row")
    col_count = lax.axis_size("col")
    stored_b, stored_bc = b_vals[0, 0], b_cols[0, 0]
    targets = c_cols[0, 0]
    slot_count, rows, nz, blk = a_vals.shape[2:6]
    own_a = a_vals.reshape(slot_count, rows, nz * blk, blk)
    notes = jnp.pad(
        a_cols[0, 0].astype(own_a.dtype), ((0, 0), (0, NOTE - rows), (0, blk - nz))
    )
    hops = col_count - 1
    from_next = [((i + 1) % row_count, i) for i in range(row_count)]

    pieces = cut(rows, nz * blk)
    spots = tuple(offset for _, i, _, _, offset in pieces[NOTED] if i < 0)
    arrived = [[None] * hops for _ in pieces]
    newest = plan = moved_b = moved_bc = None
    edges = {}
    last_slot = PIECES + lag_of(hops - 1, hops) - 1
    plan_slot = max(PIECES, NOTED + lag_of(hops - 1, hops) + 1)
    for slot in range(last_slot + 1):
        for lane in range((hops + 1) // 2):
            roles = []
            for hop in sorted({lane, hops - 1 - lane}):
                piece = slot - lag_of(hop, hops)
                if 0 <= piece < PIECES:
                    roles.append((piece, hop))
            if not roles:
                continue
            after = [newest] if slot > 1 else []
            if slot == lane == 1:
                after.append(moved_bc)
            if slot == PIECES and lane == 1:
                after.append(moved_b)
            before = slot - 2
            if lane == 0 and before > 0 and before in edges:
                after.append(edges[before])
            if slot == plan_slot and lane == 0:
                plan = make_plan(
                    panel_owner, atom_size, stored_bc, moved_bc[0, 0], targets, notes, arrived[NOTED], nz, spots, newest
                )
                after.append(plan)
            arrivals = [arrived[piece][hop - 1] if hop else None for piece, hop in roles]
            sent = [(pieces[piece], hop) for piece, hop in roles]
            flops = (2 if lane == 0 and slot == PIECES + 1 else 1) * 10**9
            limit = 62 * MIB if newest is None else 4 * MIB
            newest = relay(panel_owner, own_a, notes, sent, arrivals, after, limit, flops, f"lane{lane}_{slot}")
            if slot == 1 and lane == 0:
                behind_bc, newest = lax.optimization_barrier((b_cols, newest))
                moved_bc = lax.ppermute(behind_bc, "row", from_next)
                moved_bc, behind_b = lax.optimization_barrier((moved_bc, stored_b))
                moved_b = lax.ppermute(behind_b, "row", from_next)
            route = []
            for hop in sorted({lane, hops - 1 - lane}):
                route += [(hop, hop + 1), (hops - hop, hops - hop - 1)]
            route += [(i, i) for i in range(col_count) if i not in dict(route)]
            got = lax.ppermute(newest, "col", route)
            for piece, hop in roles:
                arrived[piece][hop] = got
            if lane == 0:
                edges[slot] = got

    result = None
    for first, count in ((0, rows - 2), (rows - 2, 1), (rows - 1, 1)):
        result = multiply_rows(
            first,
            count,
            panel_owner,
            plan,
            (stored_b, moved_b),
            own_a,
            pieces,
            arrived,
            targets.shape[1],
            result,
        )
    return result[None, None]


def solution(mesh):
    placed = (
        P("row", "col", None, None, None, None, None),
        P("row", "col", None, None, None),
        P("row", "col", None, None, None, None),
        P("row", "col", None, None),
        P("row", "col", None, None),
        P(),
        P(),
    )
    return jax.shard_map(
        local,
        mesh=mesh,
        in_specs=placed,
        out_specs=P("row", "col", None, None, None, None),
        check_vma=False,
    )
```

```python
import functools

import jax
import jax.numpy as jnp
from jax import lax
from jax.experimental import pallas as pl
from jax.experimental.pallas import tpu as pltpu
from jax.sharding import PartitionSpec as P

STEPS = 2
SHARES = (1, 1, 1, 1, 1, 1, 1, 1)
PIECES = len(SHARES)
NOTED = 1
NOTE = 16
MIB = 1024 * 1024

SMEM = pl.BlockSpec(memory_space=pltpu.SMEM)
VMEM = pl.BlockSpec(memory_space=pltpu.VMEM)
ANYWHERE = pl.BlockSpec(memory_space=pl.ANY)


def places_of(owner_ref):
    row_id, row_count = lax.axis_index("row"), lax.axis_size("row")
    panels = [lax.rem(row_id + t, row_count) for t in range(STEPS)]
    places = [owner_ref[row_id, k] for k in panels]
    return panels, [lax.div(p, 2) for p in places], [lax.rem(p, 2) for p in places]


def lag_of(hop, hops):
    return hop + (2 * hop >= hops)


def cut(rows, size):
    total = STEPS * rows * size
    pieces, at = [], 0
    for piece in range(PIECES):
        begin, end = at, total * sum(SHARES[: piece + 1]) // sum(SHARES)
        segments = []
        while at < end:
            unit, first = divmod(at, size)
            count = min(size - first, end - at)
            segments.append((unit % STEPS, unit // STEPS, first, count, at - begin))
            at += count
        if piece == NOTED:
            segments += [(t, -1, 0, NOTE, end - begin + t * NOTE) for t in range(STEPS)]
        pieces.append(tuple(segments))
    return pieces


def extent_of(segments):
    return max(offset + count for _, _, _, count, offset in segments)


def relay_kernel(roles, waits, owner, own, *refs):
    refs = list(refs)
    notes = refs.pop(0) if any(i < 0 for segments, _, _ in roles for _, i, _, _, _ in segments) else None
    arrivals = [refs.pop(0) if arrives else None for _, _, arrives in roles]
    del refs[:waits]
    onward, sem = refs
    _, holders, slots = places_of(owner)
    col_id, last = lax.axis_index("col"), lax.axis_size("col") - 1
    jobs = []
    for place, (segments, hop, _) in enumerate(roles):
        sends = (col_id == hop) | (col_id == last - hop)
        for n, (t, i, first, count, offset) in enumerate(segments):
            mine = sends if hop == 0 else sends & (holders[t] == col_id)
            src = notes.at[slots[t]] if i < 0 else own.at[slots[t], i, pl.ds(first, count)]
            jobs.append((mine, pltpu.make_async_copy(src, onward.at[pl.ds(offset, count)], sem.at[place, n])))
    for when, copy in jobs:
        pl.when(when)(copy.start)
    for (segments, hop, _), arrived in zip(roles, arrivals):
        if arrived is None:
            continue
        sends = (col_id == hop) | (col_id == last - hop)
        for t, _, _, count, offset in segments:

            @pl.when(sends & (holders[t] != col_id))
            def _():
                onward[offset : offset + count] = arrived[offset : offset + count]

    for when, copy in jobs:
        pl.when(when)(copy.wait)


def relay(owner, own, notes, roles, arrivals, after, limit, flops, name):
    noted = any(i < 0 for segments, _ in roles for _, i, _, _, _ in segments)
    size = max(extent_of(segments) for segments, _ in roles)
    given = [a for a in arrivals if a is not None]
    operands = [owner, own] + [notes] * noted + given + after
    specs = [SMEM, ANYWHERE] + [ANYWHERE] * noted + [VMEM] * len(given)
    specs += [pl.BlockSpec(memory_space=pltpu.HBM) if name == "lane0_1" else ANYWHERE] * len(after)
    roles = tuple((segments, hop, a is not None) for (segments, hop), a in zip(roles, arrivals))
    return pl.pallas_call(
        functools.partial(relay_kernel, roles, len(after)),
        out_shape=jax.ShapeDtypeStruct((size, own.shape[3]), own.dtype),
        in_specs=specs,
        out_specs=VMEM,
        scratch_shapes=[pltpu.SemaphoreType.DMA((2, max(len(segments) for segments, _, _ in roles)))],
        compiler_params=pltpu.CompilerParams(vmem_limit_bytes=limit),
        cost_estimate=pl.CostEstimate(flops=flops, bytes_accessed=1024, transcendentals=0),
        name=name,
    )(*operands)


def plan_kernel(nz, spots, owner, atoms, bcols0, bcols1, ccols, notes, *refs):
    arrivals, (plan, note_vm, ccols_vm) = refs[:-4], refs[-3:]
    panels, holders, slots = places_of(owner)
    row_id, col_id, col_count = lax.axis_index("row"), lax.axis_index("col"), lax.axis_size("col")
    panel_rows, nzb = bcols0.shape
    rows, kept = ccols.shape
    lanes = plan.shape[1]
    width = STEPS * nz
    sizes_at, row_at = kept * width, (kept + 1) * width
    for t in range(STEPS):
        hop = jnp.where(holders[t] < col_id, col_id - 1, col_count - 2 - col_id)
        mine = holders[t] == col_id

        @pl.when(mine)
        def _():
            note_vm[t] = notes[slots[t]]

        for h, arrived in enumerate(arrivals):

            @pl.when(jnp.logical_not(mine) & (hop == h))
            def _():
                note_vm[t] = arrived[spots[t] : spots[t] + NOTE]

    ccols_vm[...] = jnp.zeros_like(ccols_vm)
    ccols_vm[:rows, :kept] = ccols[...].astype(jnp.float32)

    source = lax.broadcasted_iota(jnp.int32, (lanes, lanes), 0)
    target = lax.broadcasted_iota(jnp.int32, (lanes, lanes), 1)

    def spread(values, hits):
        return jnp.dot(values, hits.astype(jnp.float32).astype(jnp.bfloat16), preferred_element_type=jnp.float32)

    lane = lax.broadcasted_iota(jnp.int32, plan.shape, 1)
    line = lax.broadcasted_iota(jnp.int32, plan.shape, 0)
    inner = jnp.zeros(plan.shape, jnp.float32)
    second = jnp.zeros(plan.shape, jnp.bool_)
    for t in range(STEPS):
        hits = source < 0
        for e in range(kept + 1):
            at = e * width + t * nz
            hits = hits | (target == source + at)
            if t:
                second = second | ((lane >= at) & (lane < at + nz))
        inner = inner + spread(note_vm[t], hits & (source < nz))
    inner = inner.astype(jnp.int32) + jnp.where(second, panel_rows, 0)
    hits = target == source + row_at + 1
    for e in range(kept):
        hits = hits | ((source == e) & (target >= e * width) & (target < (e + 1) * width))
    column = spread(ccols_vm[...].astype(jnp.bfloat16), hits & (source < kept)).astype(jnp.int32)

    block = jnp.full(plan.shape, -1, jnp.int32)
    size = jnp.zeros(plan.shape, jnp.int32)
    for t, bcols in enumerate((bcols0, bcols1)):
        for j in range(panel_rows):
            here = inner == t * panel_rows + j
            size = jnp.where(here, atoms[panels[t] * panel_rows + j], size)
            for n in range(nzb):
                block = jnp.where(here & (column == bcols[j, n]), j * nzb + n, block)
    col_size = jnp.zeros(plan.shape, jnp.int32)
    for c in range(2 * rows):
        col_size = jnp.where(column == c, atoms[col_id * 2 * rows + c], col_size)
    row_size = jnp.zeros(plan.shape, jnp.int32)
    for i in range(rows):
        row_size = jnp.where(line == i, atoms[row_id * panel_rows + i], row_size)
    tail = jnp.where(lane == row_at, row_size, col_size)
    plan[...] = jnp.where(lane < sizes_at, block, jnp.where(lane < row_at, size, tail))


def make_plan(owner, atoms, bcols0, bcols1, ccols, notes, arrivals, nz, spots, after):
    operands = [owner, atoms, bcols0, bcols1, ccols, notes, *arrivals, after]
    return pl.pallas_call(
        functools.partial(plan_kernel, nz, spots),
        out_shape=jax.ShapeDtypeStruct(notes.shape[1:], jnp.int32),
        in_specs=[SMEM] * 4 + [VMEM] * (2 + len(arrivals)) + [ANYWHERE],
        out_specs=VMEM,
        scratch_shapes=[pltpu.VMEM(notes.shape, notes.dtype), pltpu.VMEM(notes.shape[1:], jnp.float32)],
        compiler_params=pltpu.CompilerParams(vmem_limit_bytes=8 * MIB),
        cost_estimate=pl.CostEstimate(flops=10**9, bytes_accessed=1024, transcendentals=0),
        name="make_plan",
    )(*operands)


def rows_kernel(first, count, hops, sources, owner, plan, b0, b1, own, *refs):
    places = 1 + max(source[0] for source in sources)
    arrived = [refs[at * hops : (at + 1) * hops] for at in range(places)]
    out, a_vm, left_vm, o_vm, a_sem, o_sem = refs[-6:]
    kept, blk = o_vm.shape[1], o_vm.shape[-1]
    size = a_vm.shape[2]
    nz = size // blk
    width = STEPS * nz
    col_id, last = lax.axis_index("col"), lax.axis_size("col") - 1
    _, holders, slots = places_of(owner)
    copies = []
    for at in range(count):
        for t in range(STEPS):
            copy = pltpu.make_async_copy(own.at[slots[t], first + at], a_vm.at[at, t], a_sem.at[at, t])
            copies.append((holders[t] == col_id, copy))
    for when, copy in copies:
        pl.when(when)(copy.start)
    for t in range(STEPS):
        hop = jnp.where(holders[t] < col_id, col_id - 1, last - 1 - col_id)
        for h in range(hops):

            @pl.when((holders[t] != col_id) & (hop == h))
            def _():
                for place, step, i, start, lines, offset in sources:
                    if step == t:
                        a_vm[i - first, t, start : start + lines] = arrived[place][h][offset : offset + lines]

    for when, copy in copies:
        pl.when(when)(copy.wait)

    lane = lax.broadcasted_iota(jnp.int32, (blk, blk), 1)
    sub = lax.broadcasted_iota(jnp.int32, (blk, blk), 0)
    flat = [b.reshape(b.shape[0] * b.shape[1], blk, blk) for b in (b0, b1)]

    def one_row(at, carry):
        i = first + at
        for t in range(STEPS):
            for m in range(nz):
                q = t * nz + m
                left_vm[:, q * blk : (q + 1) * blk] = jnp.where(
                    lane < plan[i, kept * width + q],
                    a_vm[at, t, m * blk : (m + 1) * blk],
                    jnp.zeros((), a_vm.dtype),
                )
        row_size = plan[i, kept * width + width]

        for p in range(kept // 2):
            sides = []
            for e in range(2):
                parts = []
                for q in range(width):
                    n = plan[i, (2 * p + e) * width + q]
                    block = flat[q // nz][jnp.maximum(n, 0)]
                    parts.append(jnp.where(n >= 0, block, jnp.zeros((), block.dtype)))
                sides.append(jnp.concatenate(parts, axis=0))
            total = jnp.dot(
                left_vm[...], jnp.concatenate(sides, axis=1), preferred_element_type=jnp.float32
            )
            for e in range(2):
                col_size = plan[i, kept * width + width + 1 + 2 * p + e]
                inside = (sub < row_size) & (lane < col_size)
                part = total[:, e * blk : (e + 1) * blk]
                o_vm[at, 2 * p + e] = jnp.where(inside, part, 0.0).astype(o_vm.dtype)
        pltpu.make_async_copy(o_vm.at[at], out.at[i], o_sem.at[at]).start()
        return carry

    lax.fori_loop(0, count, one_row, 0)
    for at in range(count):
        pltpu.make_async_copy(o_vm.at[at], out.at[first + at], o_sem.at[at]).wait()


def multiply_rows(first, count, owner, plan, b_panels, own, pieces, arrived, kept, so_far):
    rows, size, blk = own.shape[1:]
    nz, hops = size // blk, len(arrived[0])
    operands = [owner, plan, *b_panels, own]
    sources, places = [], 0
    for piece, segments in enumerate(pieces):
        found = [segment for segment in segments if first <= segment[1] < first + count]
        if found:
            sources += [(places, *segment) for segment in found]
            operands += arrived[piece]
            places += 1
    specs = [SMEM] * 2 + [VMEM] * 2 + [ANYWHERE] + [VMEM] * (places * hops)
    aliases = {}
    if so_far is not None:
        aliases = {len(operands): 0}
        operands.append(so_far)
        specs.append(ANYWHERE)
    flops = 4 * count * blk * blk * blk * STEPS * nz * kept
    limit = (12 + places * hops // 2) * MIB
    return pl.pallas_call(
        functools.partial(rows_kernel, first, count, hops, tuple(sources)),
        out_shape=jax.ShapeDtypeStruct((rows, kept, blk, blk), jnp.bfloat16),
        in_specs=specs,
        out_specs=ANYWHERE,
        scratch_shapes=[
            pltpu.VMEM((count, STEPS, size, blk), jnp.bfloat16),
            pltpu.VMEM((blk, STEPS * size), jnp.bfloat16),
            pltpu.VMEM((count, kept, blk, blk), jnp.bfloat16),
            pltpu.SemaphoreType.DMA((count, STEPS)),
            pltpu.SemaphoreType.DMA((count,)),
        ],
        input_output_aliases=aliases,
        compiler_params=pltpu.CompilerParams(vmem_limit_bytes=limit),
        cost_estimate=pl.CostEstimate(flops=flops, bytes_accessed=4 * MIB, transcendentals=0),
        name="multiply_rows",
    )(*operands)


def local(a_vals, a_cols, b_vals, b_cols, c_cols, panel_owner, atom_size):
    row_count = lax.axis_size("row")
    col_count = lax.axis_size("col")
    stored_b, stored_bc = b_vals[0, 0], b_cols[0, 0]
    targets = c_cols[0, 0]
    slot_count, rows, nz, blk = a_vals.shape[2:6]
    own_a = a_vals.reshape(slot_count, rows, nz * blk, blk)
    notes = jnp.pad(
        a_cols[0, 0].astype(own_a.dtype), ((0, 0), (0, NOTE - rows), (0, blk - nz))
    )
    hops = col_count - 1
    from_next = [((i + 1) % row_count, i) for i in range(row_count)]

    pieces = cut(rows, nz * blk)
    spots = tuple(offset for _, i, _, _, offset in pieces[NOTED] if i < 0)
    arrived = [[None] * hops for _ in pieces]
    newest = plan = moved_b = moved_bc = None
    edges = {}
    last_slot = PIECES + lag_of(hops - 1, hops) - 1
    plan_slot = max(PIECES, NOTED + lag_of(hops - 1, hops) + 1)
    for slot in range(last_slot + 1):
        for lane in range((hops + 1) // 2):
            roles = []
            for hop in sorted({lane, hops - 1 - lane}):
                piece = slot - lag_of(hop, hops)
                if 0 <= piece < PIECES:
                    roles.append((piece, hop))
            if not roles:
                continue
            after = [newest] if slot > 1 else []
            if slot == lane == 1:
                after.append(moved_bc)
            if slot == PIECES and lane == 1:
                after.append(moved_b)
            before = slot - 2
            if lane == 0 and before > 0 and before in edges:
                after.append(edges[before])
            if slot == plan_slot and lane == 0:
                plan = make_plan(
                    panel_owner, atom_size, stored_bc, moved_bc[0, 0], targets, notes, arrived[NOTED], nz, spots, newest
                )
                after.append(plan)
            arrivals = [arrived[piece][hop - 1] if hop else None for piece, hop in roles]
            sent = [(pieces[piece], hop) for piece, hop in roles]
            flops = (3 - lane if slot == 2 else 2 if lane == 0 and slot == PIECES + 1 else 1) * 10**9
            limit = 62 * MIB if newest is None else 4 * MIB
            newest = relay(panel_owner, own_a, notes, sent, arrivals, after, limit, flops, f"lane{lane}_{slot}")
            if slot == 1 and lane == 0:
                behind_bc, newest = lax.optimization_barrier((b_cols, newest))
                moved_bc = lax.ppermute(behind_bc, "row", from_next)
                moved_bc, behind_b = lax.optimization_barrier((moved_bc, stored_b))
                moved_b = lax.ppermute(behind_b, "row", from_next)
            route = []
            for hop in sorted({lane, hops - 1 - lane}):
                route += [(hop, hop + 1), (hops - hop, hops - hop - 1)]
            got = lax.ppermute(newest, "col", route)
            for piece, hop in roles:
                arrived[piece][hop] = got
            if lane == 0:
                edges[slot] = got

    result = None
    for first, count in ((0, rows - 2), (rows - 2, 1), (rows - 1, 1)):
        result = multiply_rows(
            first,
            count,
            panel_owner,
            plan,
            (stored_b, moved_b),
            own_a,
            pieces,
            arrived,
            targets.shape[1],
            result,
        )
    return result[None, None]


def solution(mesh):
    placed = (
        P("row", "col", None, None, None, None, None),
        P("row", "col", None, None, None),
        P("row", "col", None, None, None, None),
        P("row", "col", None, None),
        P("row", "col", None, None),
        P(),
        P(),
    )
    return jax.shard_map(
        local,
        mesh=mesh,
        in_specs=placed,
        out_specs=P("row", "col", None, None, None, None),
        check_vma=False,
    )
```

```python
import functools

import jax
import jax.numpy as jnp
from jax import lax
from jax.experimental import pallas as pl
from jax.experimental.pallas import tpu as pltpu
from jax.sharding import PartitionSpec as P

STEPS = 2
SHARES = (16, 21, 21, 22, 20, 20)
PIECES = len(SHARES)
NOTED = 1
NOTE = 16
MIB = 1024 * 1024

SMEM = pl.BlockSpec(memory_space=pltpu.SMEM)
VMEM = pl.BlockSpec(memory_space=pltpu.VMEM)
ANYWHERE = pl.BlockSpec(memory_space=pl.ANY)


def places_of(owner_ref):
    row_id, row_count = lax.axis_index("row"), lax.axis_size("row")
    panels = [lax.rem(row_id + t, row_count) for t in range(STEPS)]
    places = [owner_ref[row_id, k] for k in panels]
    return panels, [lax.div(p, 2) for p in places], [lax.rem(p, 2) for p in places]


def lag_of(hop, hops):
    return hop + (2 * hop >= hops)


def cut(rows, size):
    total = STEPS * rows * size
    pieces, at = [], 0
    for piece in range(PIECES):
        begin, end = at, total * sum(SHARES[: piece + 1]) // sum(SHARES)
        segments = []
        while at < end:
            unit, first = divmod(at, size)
            count = min(size - first, end - at)
            segments.append((unit % STEPS, unit // STEPS, first, count, at - begin))
            at += count
        if piece == NOTED:
            segments += [(t, -1, 0, NOTE, end - begin + t * NOTE) for t in range(STEPS)]
        pieces.append(tuple(segments))
    return pieces


def extent_of(segments):
    return max(offset + count for _, _, _, count, offset in segments)


def relay_kernel(roles, waits, owner, own, *refs):
    refs = list(refs)
    notes = refs.pop(0) if any(i < 0 for segments, _, _ in roles for _, i, _, _, _ in segments) else None
    arrivals = [refs.pop(0) if arrives else None for _, _, arrives in roles]
    del refs[:waits]
    onward, sem = refs
    _, holders, slots = places_of(owner)
    col_id, last = lax.axis_index("col"), lax.axis_size("col") - 1
    jobs = []
    for place, (segments, hop, _) in enumerate(roles):
        sends = (col_id == hop) | (col_id == last - hop)
        for n, (t, i, first, count, offset) in enumerate(segments):
            mine = sends if hop == 0 else sends & (holders[t] == col_id)
            src = notes.at[slots[t]] if i < 0 else own.at[slots[t], i, pl.ds(first, count)]
            jobs.append((mine, pltpu.make_async_copy(src, onward.at[pl.ds(offset, count)], sem.at[place, n])))
    for when, copy in jobs:
        pl.when(when)(copy.start)
    for (segments, hop, _), arrived in zip(roles, arrivals):
        if arrived is None:
            continue
        sends = (col_id == hop) | (col_id == last - hop)
        for t, _, _, count, offset in segments:

            @pl.when(sends & (holders[t] != col_id))
            def _():
                onward[offset : offset + count] = arrived[offset : offset + count]

    for when, copy in jobs:
        pl.when(when)(copy.wait)


def relay(owner, own, notes, roles, arrivals, after, limit, flops, name):
    noted = any(i < 0 for segments, _ in roles for _, i, _, _, _ in segments)
    size = max(extent_of(segments) for segments, _ in roles)
    given = [a for a in arrivals if a is not None]
    operands = [owner, own] + [notes] * noted + given + after
    specs = [SMEM, ANYWHERE] + [ANYWHERE] * noted + [VMEM] * len(given)
    specs += [pl.BlockSpec(memory_space=pltpu.HBM) if name == "lane0_1" else ANYWHERE] * len(after)
    roles = tuple((segments, hop, a is not None) for (segments, hop), a in zip(roles, arrivals))
    return pl.pallas_call(
        functools.partial(relay_kernel, roles, len(after)),
        out_shape=jax.ShapeDtypeStruct((size, own.shape[3]), own.dtype),
        in_specs=specs,
        out_specs=VMEM,
        scratch_shapes=[pltpu.SemaphoreType.DMA((2, max(len(segments) for segments, _, _ in roles)))],
        compiler_params=pltpu.CompilerParams(vmem_limit_bytes=limit),
        cost_estimate=pl.CostEstimate(flops=flops, bytes_accessed=1024, transcendentals=0),
        name=name,
    )(*operands)


def plan_kernel(nz, spots, owner, atoms, bcols0, bcols1, ccols, notes, *refs):
    arrivals, (plan, note_vm, ccols_vm) = refs[:-4], refs[-3:]
    panels, holders, slots = places_of(owner)
    row_id, col_id, col_count = lax.axis_index("row"), lax.axis_index("col"), lax.axis_size("col")
    panel_rows, nzb = bcols0.shape
    rows, kept = ccols.shape
    lanes = plan.shape[1]
    width = STEPS * nz
    sizes_at, row_at = kept * width, (kept + 1) * width
    for t in range(STEPS):
        hop = jnp.where(holders[t] < col_id, col_id - 1, col_count - 2 - col_id)
        mine = holders[t] == col_id

        @pl.when(mine)
        def _():
            note_vm[t] = notes[slots[t]]

        for h, arrived in enumerate(arrivals):

            @pl.when(jnp.logical_not(mine) & (hop == h))
            def _():
                note_vm[t] = arrived[spots[t] : spots[t] + NOTE]

    ccols_vm[...] = jnp.zeros_like(ccols_vm)
    ccols_vm[:rows, :kept] = ccols[...].astype(jnp.float32)

    source = lax.broadcasted_iota(jnp.int32, (lanes, lanes), 0)
    target = lax.broadcasted_iota(jnp.int32, (lanes, lanes), 1)

    def spread(values, hits):
        return jnp.dot(values, hits.astype(jnp.float32).astype(jnp.bfloat16), preferred_element_type=jnp.float32)

    lane = lax.broadcasted_iota(jnp.int32, plan.shape, 1)
    line = lax.broadcasted_iota(jnp.int32, plan.shape, 0)
    inner = jnp.zeros(plan.shape, jnp.float32)
    second = jnp.zeros(plan.shape, jnp.bool_)
    for t in range(STEPS):
        hits = source < 0
        for e in range(kept + 1):
            at = e * width + t * nz
            hits = hits | (target == source + at)
            if t:
                second = second | ((lane >= at) & (lane < at + nz))
        inner = inner + spread(note_vm[t], hits & (source < nz))
    inner = inner.astype(jnp.int32) + jnp.where(second, panel_rows, 0)
    hits = target == source + row_at + 1
    for e in range(kept):
        hits = hits | ((source == e) & (target >= e * width) & (target < (e + 1) * width))
    column = spread(ccols_vm[...].astype(jnp.bfloat16), hits & (source < kept)).astype(jnp.int32)

    block = jnp.full(plan.shape, -1, jnp.int32)
    size = jnp.zeros(plan.shape, jnp.int32)
    for t, bcols in enumerate((bcols0, bcols1)):
        for j in range(panel_rows):
            here = inner == t * panel_rows + j
            size = jnp.where(here, atoms[panels[t] * panel_rows + j], size)
            for n in range(nzb):
                block = jnp.where(here & (column == bcols[j, n]), j * nzb + n, block)
    col_size = jnp.zeros(plan.shape, jnp.int32)
    for c in range(2 * rows):
        col_size = jnp.where(column == c, atoms[col_id * 2 * rows + c], col_size)
    row_size = jnp.zeros(plan.shape, jnp.int32)
    for i in range(rows):
        row_size = jnp.where(line == i, atoms[row_id * panel_rows + i], row_size)
    tail = jnp.where(lane == row_at, row_size, col_size)
    plan[...] = jnp.where(lane < sizes_at, block, jnp.where(lane < row_at, size, tail))


def make_plan(owner, atoms, bcols0, bcols1, ccols, notes, arrivals, nz, spots, after):
    operands = [owner, atoms, bcols0, bcols1, ccols, notes, *arrivals, after]
    return pl.pallas_call(
        functools.partial(plan_kernel, nz, spots),
        out_shape=jax.ShapeDtypeStruct(notes.shape[1:], jnp.int32),
        in_specs=[SMEM] * 4 + [VMEM] * (2 + len(arrivals)) + [ANYWHERE],
        out_specs=VMEM,
        scratch_shapes=[pltpu.VMEM(notes.shape, notes.dtype), pltpu.VMEM(notes.shape[1:], jnp.float32)],
        compiler_params=pltpu.CompilerParams(vmem_limit_bytes=8 * MIB),
        cost_estimate=pl.CostEstimate(flops=10**9, bytes_accessed=1024, transcendentals=0),
        name="make_plan",
    )(*operands)


def rows_kernel(first, count, hops, sources, owner, plan, b0, b1, own, *refs):
    places = 1 + max(source[0] for source in sources)
    arrived = [refs[at * hops : (at + 1) * hops] for at in range(places)]
    out, a_vm, left_vm, o_vm, a_sem, o_sem = refs[-6:]
    kept, blk = o_vm.shape[1], o_vm.shape[-1]
    size = a_vm.shape[2]
    nz = size // blk
    width = STEPS * nz
    col_id, last = lax.axis_index("col"), lax.axis_size("col") - 1
    _, holders, slots = places_of(owner)
    copies = []
    for at in range(count):
        for t in range(STEPS):
            copy = pltpu.make_async_copy(own.at[slots[t], first + at], a_vm.at[at, t], a_sem.at[at, t])
            copies.append((holders[t] == col_id, copy))
    for when, copy in copies:
        pl.when(when)(copy.start)
    for t in range(STEPS):
        hop = jnp.where(holders[t] < col_id, col_id - 1, last - 1 - col_id)
        for h in range(hops):

            @pl.when((holders[t] != col_id) & (hop == h))
            def _():
                for place, step, i, start, lines, offset in sources:
                    if step == t:
                        a_vm[i - first, t, start : start + lines] = arrived[place][h][offset : offset + lines]

    for when, copy in copies:
        pl.when(when)(copy.wait)

    lane = lax.broadcasted_iota(jnp.int32, (blk, blk), 1)
    sub = lax.broadcasted_iota(jnp.int32, (blk, blk), 0)
    flat = [b.reshape(b.shape[0] * b.shape[1], blk, blk) for b in (b0, b1)]

    def one_row(at, carry):
        i = first + at
        for t in range(STEPS):
            for m in range(nz):
                q = t * nz + m
                left_vm[:, q * blk : (q + 1) * blk] = jnp.where(
                    lane < plan[i, kept * width + q],
                    a_vm[at, t, m * blk : (m + 1) * blk],
                    jnp.zeros((), a_vm.dtype),
                )
        row_size = plan[i, kept * width + width]

        for p in range(kept // 2):
            sides = []
            for e in range(2):
                parts = []
                for q in range(width):
                    n = plan[i, (2 * p + e) * width + q]
                    block = flat[q // nz][jnp.maximum(n, 0)]
                    parts.append(jnp.where(n >= 0, block, jnp.zeros((), block.dtype)))
                sides.append(jnp.concatenate(parts, axis=0))
            total = jnp.dot(
                left_vm[...], jnp.concatenate(sides, axis=1), preferred_element_type=jnp.float32
            )
            for e in range(2):
                col_size = plan[i, kept * width + width + 1 + 2 * p + e]
                inside = (sub < row_size) & (lane < col_size)
                part = total[:, e * blk : (e + 1) * blk]
                o_vm[at, 2 * p + e] = jnp.where(inside, part, 0.0).astype(o_vm.dtype)
        pltpu.make_async_copy(o_vm.at[at], out.at[i], o_sem.at[at]).start()
        return carry

    lax.fori_loop(0, count, one_row, 0)
    for at in range(count):
        pltpu.make_async_copy(o_vm.at[at], out.at[first + at], o_sem.at[at]).wait()


def multiply_rows(first, count, owner, plan, b_panels, own, pieces, arrived, kept, so_far):
    rows, size, blk = own.shape[1:]
    nz, hops = size // blk, len(arrived[0])
    operands = [owner, plan, *b_panels, own]
    sources, places = [], 0
    for piece, segments in enumerate(pieces):
        found = [segment for segment in segments if first <= segment[1] < first + count]
        if found:
            sources += [(places, *segment) for segment in found]
            operands += arrived[piece]
            places += 1
    specs = [SMEM] * 2 + [VMEM] * 2 + [ANYWHERE] + [VMEM] * (places * hops)
    aliases = {}
    if so_far is not None:
        aliases = {len(operands): 0}
        operands.append(so_far)
        specs.append(ANYWHERE)
    flops = 4 * count * blk * blk * blk * STEPS * nz * kept
    limit = (12 + places * hops // 2) * MIB
    return pl.pallas_call(
        functools.partial(rows_kernel, first, count, hops, tuple(sources)),
        out_shape=jax.ShapeDtypeStruct((rows, kept, blk, blk), jnp.bfloat16),
        in_specs=specs,
        out_specs=ANYWHERE,
        scratch_shapes=[
            pltpu.VMEM((count, STEPS, size, blk), jnp.bfloat16),
            pltpu.VMEM((blk, STEPS * size), jnp.bfloat16),
            pltpu.VMEM((count, kept, blk, blk), jnp.bfloat16),
            pltpu.SemaphoreType.DMA((count, STEPS)),
            pltpu.SemaphoreType.DMA((count,)),
        ],
        input_output_aliases=aliases,
        compiler_params=pltpu.CompilerParams(vmem_limit_bytes=limit),
        cost_estimate=pl.CostEstimate(flops=flops, bytes_accessed=4 * MIB, transcendentals=0),
        name="multiply_rows",
    )(*operands)


def local(a_vals, a_cols, b_vals, b_cols, c_cols, panel_owner, atom_size):
    row_count = lax.axis_size("row")
    col_count = lax.axis_size("col")
    stored_b, stored_bc = b_vals[0, 0], b_cols[0, 0]
    targets = c_cols[0, 0]
    slot_count, rows, nz, blk = a_vals.shape[2:6]
    own_a = a_vals.reshape(slot_count, rows, nz * blk, blk)
    notes = jnp.pad(
        a_cols[0, 0].astype(own_a.dtype), ((0, 0), (0, NOTE - rows), (0, blk - nz))
    )
    hops = col_count - 1
    from_next = [((i + 1) % row_count, i) for i in range(row_count)]

    pieces = cut(rows, nz * blk)
    spots = tuple(offset for _, i, _, _, offset in pieces[NOTED] if i < 0)
    arrived = [[None] * hops for _ in pieces]
    newest = plan = moved_b = moved_bc = None
    edges = {}
    last_slot = PIECES + lag_of(hops - 1, hops) - 1
    plan_slot = max(PIECES, NOTED + lag_of(hops - 1, hops) + 1)
    for slot in range(last_slot + 1):
        for lane in range((hops + 1) // 2):
            roles = []
            for hop in sorted({lane, hops - 1 - lane}):
                piece = slot - lag_of(hop, hops)
                if 0 <= piece < PIECES:
                    roles.append((piece, hop))
            if not roles:
                continue
            after = [newest] if slot > 1 else []
            if slot == lane == 1:
                after.append(moved_bc)
            if slot == PIECES and lane == 1:
                after.append(moved_b)
            before = slot - 2
            if lane == 0 and before > 0 and before in edges:
                after.append(edges[before])
            if slot == plan_slot and lane == 0:
                plan = make_plan(
                    panel_owner, atom_size, stored_bc, moved_bc[0, 0], targets, notes, arrived[NOTED], nz, spots, newest
                )
                after.append(plan)
            arrivals = [arrived[piece][hop - 1] if hop else None for piece, hop in roles]
            sent = [(pieces[piece], hop) for piece, hop in roles]
            flops = (3 - lane if slot == 2 else 2 if lane == 0 and slot == PIECES + 1 else 1) * 10**9
            limit = 62 * MIB if newest is None else 4 * MIB
            newest = relay(panel_owner, own_a, notes, sent, arrivals, after, limit, flops, f"lane{lane}_{slot}")
            if slot == 1 and lane == 0:
                behind_bc, newest = lax.optimization_barrier((b_cols, newest))
                moved_bc = lax.ppermute(behind_bc, "row", from_next)
                moved_bc, behind_b = lax.optimization_barrier((moved_bc, stored_b))
                moved_b = lax.ppermute(behind_b, "row", from_next)
            route = []
            for hop in sorted({lane, hops - 1 - lane}):
                route += [(hop, hop + 1), (hops - hop, hops - hop - 1)]
            got = lax.ppermute(newest, "col", route)
            for piece, hop in roles:
                arrived[piece][hop] = got
            if lane == 0:
                edges[slot] = got

    result = None
    for first, count in ((0, rows - 2), (rows - 2, 1), (rows - 1, 1)):
        result = multiply_rows(
            first,
            count,
            panel_owner,
            plan,
            (stored_b, moved_b),
            own_a,
            pieces,
            arrived,
            targets.shape[1],
            result,
        )
    return result[None, None]


def solution(mesh):
    placed = (
        P("row", "col", None, None, None, None, None),
        P("row", "col", None, None, None),
        P("row", "col", None, None, None, None),
        P("row", "col", None, None),
        P("row", "col", None, None),
        P(),
        P(),
    )
    return jax.shard_map(
        local,
        mesh=mesh,
        in_specs=placed,
        out_specs=P("row", "col", None, None, None, None),
        check_vma=False,
    )
```

```python
import functools

import jax
import jax.numpy as jnp
from jax import lax
from jax.experimental import pallas as pl
from jax.experimental.pallas import tpu as pltpu
from jax.sharding import PartitionSpec as P

STEPS = 2
SHARES = (1, 1, 1, 1, 1, 1)
PIECES = len(SHARES)
NOTED = 1
NOTE = 16
MIB = 1024 * 1024

SMEM = pl.BlockSpec(memory_space=pltpu.SMEM)
VMEM = pl.BlockSpec(memory_space=pltpu.VMEM)
ANYWHERE = pl.BlockSpec(memory_space=pl.ANY)


def places_of(owner_ref):
    row_id, row_count = lax.axis_index("row"), lax.axis_size("row")
    panels = [lax.rem(row_id + t, row_count) for t in range(STEPS)]
    places = [owner_ref[row_id, k] for k in panels]
    return panels, [lax.div(p, 2) for p in places], [lax.rem(p, 2) for p in places]


def lag_of(hop, hops):
    return hop + (2 * hop >= hops)


def cut(rows, size):
    total = STEPS * rows * size
    pieces, at = [], 0
    for piece in range(PIECES):
        begin, end = at, total * sum(SHARES[: piece + 1]) // sum(SHARES)
        segments = []
        while at < end:
            unit, first = divmod(at, size)
            count = min(size - first, end - at)
            segments.append((unit % STEPS, unit // STEPS, first, count, at - begin))
            at += count
        if piece == NOTED:
            segments += [(t, -1, 0, NOTE, end - begin + t * NOTE) for t in range(STEPS)]
        pieces.append(tuple(segments))
    return pieces


def extent_of(segments):
    return max(offset + count for _, _, _, count, offset in segments)


def relay_kernel(roles, waits, owner, own, *refs):
    refs = list(refs)
    notes = refs.pop(0) if any(i < 0 for segments, _, _ in roles for _, i, _, _, _ in segments) else None
    arrivals = [refs.pop(0) if arrives else None for _, _, arrives in roles]
    del refs[:waits]
    onward, sem = refs
    _, holders, slots = places_of(owner)
    col_id, last = lax.axis_index("col"), lax.axis_size("col") - 1
    jobs = []
    for place, (segments, hop, _) in enumerate(roles):
        sends = (col_id == hop) | (col_id == last - hop)
        for n, (t, i, first, count, offset) in enumerate(segments):
            mine = sends if hop == 0 else sends & (holders[t] == col_id)
            src = notes.at[slots[t]] if i < 0 else own.at[slots[t], i, pl.ds(first, count)]
            jobs.append((mine, pltpu.make_async_copy(src, onward.at[pl.ds(offset, count)], sem.at[place, n])))
    for when, copy in jobs:
        pl.when(when)(copy.start)
    for (segments, hop, _), arrived in zip(roles, arrivals):
        if arrived is None:
            continue
        sends = (col_id == hop) | (col_id == last - hop)
        for t, _, _, count, offset in segments:

            @pl.when(sends & (holders[t] != col_id))
            def _():
                onward[offset : offset + count] = arrived[offset : offset + count]

    for when, copy in jobs:
        pl.when(when)(copy.wait)


def relay(owner, own, notes, roles, arrivals, after, limit, flops, name):
    noted = any(i < 0 for segments, _ in roles for _, i, _, _, _ in segments)
    size = max(extent_of(segments) for segments, _ in roles)
    given = [a for a in arrivals if a is not None]
    operands = [owner, own] + [notes] * noted + given + after
    specs = [SMEM, ANYWHERE] + [ANYWHERE] * noted + [VMEM] * len(given)
    specs += [pl.BlockSpec(memory_space=pltpu.HBM) if name == "lane0_1" else ANYWHERE] * len(after)
    roles = tuple((segments, hop, a is not None) for (segments, hop), a in zip(roles, arrivals))
    return pl.pallas_call(
        functools.partial(relay_kernel, roles, len(after)),
        out_shape=jax.ShapeDtypeStruct((size, own.shape[3]), own.dtype),
        in_specs=specs,
        out_specs=VMEM,
        scratch_shapes=[pltpu.SemaphoreType.DMA((2, max(len(segments) for segments, _, _ in roles)))],
        compiler_params=pltpu.CompilerParams(vmem_limit_bytes=limit),
        cost_estimate=pl.CostEstimate(flops=flops, bytes_accessed=1024, transcendentals=0),
        name=name,
    )(*operands)


def plan_kernel(nz, spots, owner, atoms, bcols0, bcols1, ccols, notes, *refs):
    arrivals, (plan, note_vm, ccols_vm) = refs[:-4], refs[-3:]
    panels, holders, slots = places_of(owner)
    row_id, col_id, col_count = lax.axis_index("row"), lax.axis_index("col"), lax.axis_size("col")
    panel_rows, nzb = bcols0.shape
    rows, kept = ccols.shape
    lanes = plan.shape[1]
    width = STEPS * nz
    sizes_at, row_at = kept * width, (kept + 1) * width
    for t in range(STEPS):
        hop = jnp.where(holders[t] < col_id, col_id - 1, col_count - 2 - col_id)
        mine = holders[t] == col_id

        @pl.when(mine)
        def _():
            note_vm[t] = notes[slots[t]]

        for h, arrived in enumerate(arrivals):

            @pl.when(jnp.logical_not(mine) & (hop == h))
            def _():
                note_vm[t] = arrived[spots[t] : spots[t] + NOTE]

    ccols_vm[...] = jnp.zeros_like(ccols_vm)
    ccols_vm[:rows, :kept] = ccols[...].astype(jnp.float32)

    source = lax.broadcasted_iota(jnp.int32, (lanes, lanes), 0)
    target = lax.broadcasted_iota(jnp.int32, (lanes, lanes), 1)

    def spread(values, hits):
        return jnp.dot(values, hits.astype(jnp.float32).astype(jnp.bfloat16), preferred_element_type=jnp.float32)

    lane = lax.broadcasted_iota(jnp.int32, plan.shape, 1)
    line = lax.broadcasted_iota(jnp.int32, plan.shape, 0)
    inner = jnp.zeros(plan.shape, jnp.float32)
    second = jnp.zeros(plan.shape, jnp.bool_)
    for t in range(STEPS):
        hits = source < 0
        for e in range(kept + 1):
            at = e * width + t * nz
            hits = hits | (target == source + at)
            if t:
                second = second | ((lane >= at) & (lane < at + nz))
        inner = inner + spread(note_vm[t], hits & (source < nz))
    inner = inner.astype(jnp.int32) + jnp.where(second, panel_rows, 0)
    hits = target == source + row_at + 1
    for e in range(kept):
        hits = hits | ((source == e) & (target >= e * width) & (target < (e + 1) * width))
    column = spread(ccols_vm[...].astype(jnp.bfloat16), hits & (source < kept)).astype(jnp.int32)

    block = jnp.full(plan.shape, -1, jnp.int32)
    size = jnp.zeros(plan.shape, jnp.int32)
    for t, bcols in enumerate((bcols0, bcols1)):
        for j in range(panel_rows):
            here = inner == t * panel_rows + j
            size = jnp.where(here, atoms[panels[t] * panel_rows + j], size)
            for n in range(nzb):
                block = jnp.where(here & (column == bcols[j, n]), j * nzb + n, block)
    col_size = jnp.zeros(plan.shape, jnp.int32)
    for c in range(2 * rows):
        col_size = jnp.where(column == c, atoms[col_id * 2 * rows + c], col_size)
    row_size = jnp.zeros(plan.shape, jnp.int32)
    for i in range(rows):
        row_size = jnp.where(line == i, atoms[row_id * panel_rows + i], row_size)
    tail = jnp.where(lane == row_at, row_size, col_size)
    plan[...] = jnp.where(lane < sizes_at, block, jnp.where(lane < row_at, size, tail))


def make_plan(owner, atoms, bcols0, bcols1, ccols, notes, arrivals, nz, spots, after):
    operands = [owner, atoms, bcols0, bcols1, ccols, notes, *arrivals, after]
    return pl.pallas_call(
        functools.partial(plan_kernel, nz, spots),
        out_shape=jax.ShapeDtypeStruct(notes.shape[1:], jnp.int32),
        in_specs=[SMEM] * 4 + [VMEM] * (2 + len(arrivals)) + [ANYWHERE],
        out_specs=VMEM,
        scratch_shapes=[pltpu.VMEM(notes.shape, notes.dtype), pltpu.VMEM(notes.shape[1:], jnp.float32)],
        compiler_params=pltpu.CompilerParams(vmem_limit_bytes=8 * MIB),
        cost_estimate=pl.CostEstimate(flops=10**9, bytes_accessed=1024, transcendentals=0),
        name="make_plan",
    )(*operands)


def rows_kernel(first, count, hops, sources, owner, plan, b0, b1, own, *refs):
    places = 1 + max(source[0] for source in sources)
    arrived = [refs[at * hops : (at + 1) * hops] for at in range(places)]
    out, a_vm, left_vm, o_vm, a_sem, o_sem = refs[-6:]
    kept, blk = o_vm.shape[1], o_vm.shape[-1]
    size = a_vm.shape[2]
    nz = size // blk
    width = STEPS * nz
    col_id, last = lax.axis_index("col"), lax.axis_size("col") - 1
    _, holders, slots = places_of(owner)
    copies = []
    for at in range(count):
        for t in range(STEPS):
            copy = pltpu.make_async_copy(own.at[slots[t], first + at], a_vm.at[at, t], a_sem.at[at, t])
            copies.append((holders[t] == col_id, copy))
    for when, copy in copies:
        pl.when(when)(copy.start)
    for t in range(STEPS):
        hop = jnp.where(holders[t] < col_id, col_id - 1, last - 1 - col_id)
        for h in range(hops):

            @pl.when((holders[t] != col_id) & (hop == h))
            def _():
                for place, step, i, start, lines, offset in sources:
                    if step == t:
                        a_vm[i - first, t, start : start + lines] = arrived[place][h][offset : offset + lines]

    for when, copy in copies:
        pl.when(when)(copy.wait)

    lane = lax.broadcasted_iota(jnp.int32, (blk, blk), 1)
    sub = lax.broadcasted_iota(jnp.int32, (blk, blk), 0)
    flat = [b.reshape(b.shape[0] * b.shape[1], blk, blk) for b in (b0, b1)]

    def one_row(at, carry):
        i = first + at
        for t in range(STEPS):
            for m in range(nz):
                q = t * nz + m
                left_vm[:, q * blk : (q + 1) * blk] = jnp.where(
                    lane < plan[i, kept * width + q],
                    a_vm[at, t, m * blk : (m + 1) * blk],
                    jnp.zeros((), a_vm.dtype),
                )
        row_size = plan[i, kept * width + width]

        for p in range(kept // 2):
            sides = []
            for e in range(2):
                parts = []
                for q in range(width):
                    n = plan[i, (2 * p + e) * width + q]
                    block = flat[q // nz][jnp.maximum(n, 0)]
                    parts.append(jnp.where(n >= 0, block, jnp.zeros((), block.dtype)))
                sides.append(jnp.concatenate(parts, axis=0))
            total = jnp.dot(
                left_vm[...], jnp.concatenate(sides, axis=1), preferred_element_type=jnp.float32
            )
            for e in range(2):
                col_size = plan[i, kept * width + width + 1 + 2 * p + e]
                inside = (sub < row_size) & (lane < col_size)
                part = total[:, e * blk : (e + 1) * blk]
                o_vm[at, 2 * p + e] = jnp.where(inside, part, 0.0).astype(o_vm.dtype)
        pltpu.make_async_copy(o_vm.at[at], out.at[i], o_sem.at[at]).start()
        return carry

    lax.fori_loop(0, count, one_row, 0)
    for at in range(count):
        pltpu.make_async_copy(o_vm.at[at], out.at[first + at], o_sem.at[at]).wait()


def multiply_rows(first, count, owner, plan, b_panels, own, pieces, arrived, kept, so_far):
    rows, size, blk = own.shape[1:]
    nz, hops = size // blk, len(arrived[0])
    operands = [owner, plan, *b_panels, own]
    sources, places = [], 0
    for piece, segments in enumerate(pieces):
        found = [segment for segment in segments if first <= segment[1] < first + count]
        if found:
            sources += [(places, *segment) for segment in found]
            operands += arrived[piece]
            places += 1
    specs = [SMEM] * 2 + [VMEM] * 2 + [ANYWHERE] + [VMEM] * (places * hops)
    aliases = {}
    if so_far is not None:
        aliases = {len(operands): 0}
        operands.append(so_far)
        specs.append(ANYWHERE)
    flops = 4 * count * blk * blk * blk * STEPS * nz * kept
    limit = (12 + places * hops // 2) * MIB
    return pl.pallas_call(
        functools.partial(rows_kernel, first, count, hops, tuple(sources)),
        out_shape=jax.ShapeDtypeStruct((rows, kept, blk, blk), jnp.bfloat16),
        in_specs=specs,
        out_specs=ANYWHERE,
        scratch_shapes=[
            pltpu.VMEM((count, STEPS, size, blk), jnp.bfloat16),
            pltpu.VMEM((blk, STEPS * size), jnp.bfloat16),
            pltpu.VMEM((count, kept, blk, blk), jnp.bfloat16),
            pltpu.SemaphoreType.DMA((count, STEPS)),
            pltpu.SemaphoreType.DMA((count,)),
        ],
        input_output_aliases=aliases,
        compiler_params=pltpu.CompilerParams(vmem_limit_bytes=limit),
        cost_estimate=pl.CostEstimate(flops=flops, bytes_accessed=4 * MIB, transcendentals=0),
        name="multiply_rows",
    )(*operands)


def local(a_vals, a_cols, b_vals, b_cols, c_cols, panel_owner, atom_size):
    row_count = lax.axis_size("row")
    col_count = lax.axis_size("col")
    stored_b, stored_bc = b_vals[0, 0], b_cols[0, 0]
    targets = c_cols[0, 0]
    slot_count, rows, nz, blk = a_vals.shape[2:6]
    own_a = a_vals.reshape(slot_count, rows, nz * blk, blk)
    notes = jnp.pad(
        a_cols[0, 0].astype(own_a.dtype), ((0, 0), (0, NOTE - rows), (0, blk - nz))
    )
    hops = col_count - 1
    from_next = [((i + 1) % row_count, i) for i in range(row_count)]

    pieces = cut(rows, nz * blk)
    spots = tuple(offset for _, i, _, _, offset in pieces[NOTED] if i < 0)
    arrived = [[None] * hops for _ in pieces]
    newest = plan = moved_b = moved_bc = None
    edges = {}
    last_slot = PIECES + lag_of(hops - 1, hops) - 1
    plan_slot = max(PIECES, NOTED + lag_of(hops - 1, hops) + 1)
    for slot in range(last_slot + 1):
        for lane in range((hops + 1) // 2):
            roles = []
            for hop in sorted({lane, hops - 1 - lane}):
                piece = slot - lag_of(hop, hops)
                if 0 <= piece < PIECES:
                    roles.append((piece, hop))
            if not roles:
                continue
            after = [newest] if slot > 1 else []
            if slot == lane == 1:
                after.append(moved_bc)
            if slot == PIECES and lane == 1:
                after.append(moved_b)
            before = slot - 2
            if lane == 0 and before > 0 and before in edges:
                after.append(edges[before])
            if slot == plan_slot and lane == 1:
                plan = make_plan(
                    panel_owner, atom_size, stored_bc, moved_bc[0, 0], targets, notes, arrived[NOTED], nz, spots, newest
                )
                after.append(plan)
            arrivals = [arrived[piece][hop - 1] if hop else None for piece, hop in roles]
            sent = [(pieces[piece], hop) for piece, hop in roles]
            flops = (3 - lane if slot == 2 else 2 if lane == 0 and slot == PIECES + 1 else 1) * 10**9
            limit = 62 * MIB if newest is None else 4 * MIB
            newest = relay(panel_owner, own_a, notes, sent, arrivals, after, limit, flops, f"lane{lane}_{slot}")
            if slot == 1 and lane == 0:
                behind_bc, newest = lax.optimization_barrier((b_cols, newest))
                moved_bc = lax.ppermute(behind_bc, "row", from_next)
                moved_bc, behind_b = lax.optimization_barrier((moved_bc, stored_b))
                moved_b = lax.ppermute(behind_b, "row", from_next)
            route = []
            for hop in sorted({lane, hops - 1 - lane}):
                route += [(hop, hop + 1), (hops - hop, hops - hop - 1)]
            got = lax.ppermute(newest, "col", route)
            for piece, hop in roles:
                arrived[piece][hop] = got
            if lane == 0:
                edges[slot] = got

    result = None
    for first, count in ((0, rows - 2), (rows - 2, 1), (rows - 1, 1)):
        result = multiply_rows(
            first,
            count,
            panel_owner,
            plan,
            (stored_b, moved_b),
            own_a,
            pieces,
            arrived,
            targets.shape[1],
            result,
        )
    return result[None, None]


def solution(mesh):
    placed = (
        P("row", "col", None, None, None, None, None),
        P("row", "col", None, None, None),
        P("row", "col", None, None, None, None),
        P("row", "col", None, None),
        P("row", "col", None, None),
        P(),
        P(),
    )
    return jax.shard_map(
        local,
        mesh=mesh,
        in_specs=placed,
        out_specs=P("row", "col", None, None, None, None),
        check_vma=False,
    )
```
